32 devices in a mesh: page: 8 (over z, x), blk: 4 (over y, core).
Axes of the slice: x: 2, y: 2, z: 4, core: 2. Of those that a mesh axis runs over, the one named last changes fastest.
Arguments:
- tokens: bfloat16 [24, 512, 768], P('page', 'blk'), may hold values from -6 to 6
- lengths: int32 [24], P('page'), may hold values from 40 to 512, as said below
- boxes: int32 [24, 512, 4], P('page', 'blk'), may hold values from 0 to 1000
- qkv_weight: bfloat16 [768, 2304], replicated, may hold values from -0.21875 to 0.21875
- qkv_bias: float32 [2304], replicated, may hold values from -3 to 3
- box_weight: bfloat16 [64, 128], replicated, may hold values from -0.5 to 0.5
- out_weight: bfloat16 [768, 768], replicated, may hold values from -1.5 to 1.5
- out_bias: float32 [768], replicated, may hold values from -2 to 2
- norm1_gain: float32 [768], replicated, may hold values from 0.1 to 1.9
- norm1_bias: float32 [768], replicated, may hold values from -2 to 2
- up_weight: bfloat16 [768, 3072], replicated, may hold values from -0.21875 to 0.21875
- up_bias: float32 [3072], replicated, may hold values from -3 to 3
- down_weight: bfloat16 [3072, 768], replicated, may hold values from -0.109375 to 0.109375
- down_bias: float32 [768], replicated, may hold values from -2 to 2
- norm2_gain: float32 [768], replicated, may hold values from 0.1 to 1.9
- norm2_bias: float32 [768], replicated, may hold values from -2 to 2
- cotangent: bfloat16 [24, 512, 768], P('page', 'blk'), may hold values from -6 to 6
Outputs:
- layer_output: bfloat16 [24, 512, 768], P('page', 'blk')
- input_grad: bfloat16 [24, 512, 768], P('page', 'blk')
- qkv_weight_grad: float32 [768, 2304], P('page')
- qkv_bias_grad: float32 [2304], P('page')
- box_weight_grad: float32 [8192], P('page')
- out_weight_grad: float32 [768, 768], P('page')
- out_bias_grad: float32 [768], P('page')
- norm1_gain_grad: float32 [768], P('page')
- norm1_bias_grad: float32 [768], P('page')
- up_weight_grad: float32 [768, 3072], P('page')
- up_bias_grad: float32 [3072], P('page')
- down_weight_grad: float32 [3072, 768], P('page')
- down_bias_grad: float32 [768], P('page')
- norm2_gain_grad: float32 [768], P('page')
- norm2_bias_grad: float32 [768], P('page')
The draws below stay inside these ranges and needn't reach their ends.
Inputs may be any that keep to these rules, and one draw needn't show every extreme that they name: `lengths`: real tokens of each page; in each aligned run of 3 pages one page is longer than 384, and some page is 512 long.
All inputs are finite; a program needn't handle non-finite values.
Results may differ from the reference program's by a relative error of at most 0.018.
Values may be sent and summed in bfloat16 or wider, within the bound.
A program may use at most 192 MiB of HBM per device.

```python
import math
import jax
import jax.numpy as jnp
from jax import lax

D = 768
FF = 3072
HEADS = 12
HD = 64
POS = 128
PAGE_LEN = 512
PAGES_DEV = 3
BLOCK = 128
PAGES = 24


def draw_lengths(key, part):
    key = jax.random.fold_in(key, 3)
    draw_key, pick_key, long_key, top_key = jax.random.split(key, 4)
    drawn = jax.random.randint(draw_key, (PAGES,), PAGE_LEN * 5 // 64, PAGE_LEN + 1)
    chosen = jax.random.randint(pick_key, (PAGES // PAGES_DEV,), 0, PAGES_DEV)
    places = jnp.arange(PAGES) % PAGES_DEV
    long_page = places == jnp.repeat(chosen, PAGES_DEV)
    long_len = jax.random.randint(long_key, (PAGES,), PAGE_LEN - BLOCK + 1, PAGE_LEN + 1)
    top_page = jax.random.randint(top_key, (), 0, PAGES // PAGES_DEV)
    top_index = top_page * PAGES_DEV + chosen[top_page]
    result = jnp.where(long_page, long_len, drawn)
    result = jnp.where(jnp.arange(PAGES) == top_index, PAGE_LEN, result)
    return result.astype(jnp.int32)


def touch_ends(values, rng, least, largest):
    shape = values.shape
    spot = [jax.random.randint(jax.random.fold_in(rng, axis), (), 0, shape[axis]) for axis in range(len(shape))]
    values = values.at[tuple(spot)].set(least)
    longest = shape.index(max(shape))
    spot[longest] = (spot[longest] + 1) % shape[longest]
    return values.at[tuple(spot)].set(largest)


def with_spikes(entries, stream_key, source, target, shards_of, factor):
    def block_of(dim):
        return (jnp.arange(entries.shape[dim]) // (entries.shape[dim] // shards_of)).reshape((-1,) + (1,) * (entries.ndim - 1 - dim))

    one_side = jax.random.permutation(stream_key, shards_of)[block_of(target)]
    second = (block_of(target) + shards_of // 2) % shards_of
    return jnp.where((block_of(source) == one_side) | (block_of(source) == second), factor * entries, entries)


def steps_of(stream_key, extent, pieces, low, largest):
    level, own = 1.0, jax.random.fold_in(stream_key, 6)
    for axis_at, parts in pieces:
        heights = jnp.exp(jax.random.uniform(jax.random.fold_in(own, axis_at), (parts,), jnp.float32, low / len(pieces), largest / len(pieces)))
        level = level * jnp.repeat(heights, extent[axis_at] // parts).reshape([-1 if axis == axis_at else 1 for axis in range(len(extent))])
    return level


def noise(key, extent, deviation, limit, cuts=(), kind=jnp.bfloat16):
    values = jax.random.normal(key, extent, jnp.float32) * deviation
    if len(cuts) > 0:
        values = steps_of(key, extent, cuts, -0.22, 0.18) * values
    return jnp.clip(values, min=-limit, max=limit).astype(kind)


def noise_with(stream_key, extent, scale, bound, cuts, heavy, held_as=jnp.bfloat16):
    values = scale * jax.random.normal(stream_key, extent, jnp.float32)
    if cuts:
        values = values * steps_of(stream_key, extent, cuts, -0.22, 0.18)
    return jnp.clip(with_spikes(values, jax.random.fold_in(stream_key, 3), *heavy), -bound, bound).astype(held_as)


def setup_inputs(seed: int = 0) -> dict:
    streams_of = jax.random.split(jax.random.key(seed), 18)
    return {
        "tokens": noise_with(streams_of[0], (PAGES, PAGE_LEN, D), 1.0, 6.0, ((0, 8), (1, 4)), (0, 2, 8, 2.0)),
        "lengths": draw_lengths(jax.random.fold_in(streams_of[17], 71), 0),
        "boxes": touch_ends(jax.random.randint(streams_of[2], (PAGES, PAGE_LEN, 4), 0, 1001), jax.random.fold_in(streams_of[2], 1), 0, 1000).astype(jnp.int32),
        "qkv_weight": noise(streams_of[3], (D, 3 * D), D ** -0.5, 0.21875),
        "qkv_bias": noise(streams_of[4], (3 * D,), 0.5, 3.0, (), jnp.float32),
        "box_weight": noise(streams_of[5], (HD, POS), POS ** -0.5, 0.5),
        "out_weight": noise(streams_of[6], (D, D), (max(1, D // 48)) ** -0.5, 1.5),
        "out_bias": noise(streams_of[7], (D,), 0.3, 2.0, (), jnp.float32),
        "norm1_gain": jnp.clip(1.0 + 0.18 * jax.random.normal(streams_of[8], (D,), jnp.float32), 0.1, 1.9),
        "norm1_bias": noise(streams_of[9], (D,), 0.3, 2.0, (), jnp.float32),
        "up_weight": noise(streams_of[10], (D, FF), D ** -0.5, 0.21875),
        "up_bias": noise(streams_of[11], (FF,), 0.5, 3.0, (), jnp.float32),
        "down_weight": noise(streams_of[12], (FF, D), FF ** -0.5, 0.109375),
        "down_bias": noise(streams_of[13], (D,), 0.3, 2.0, (), jnp.float32),
        "norm2_gain": jnp.clip(1.0 + 0.18 * jax.random.normal(streams_of[14], (D,), jnp.float32), 0.1, 1.9),
        "norm2_bias": noise(streams_of[15], (D,), 0.3, 2.0, (), jnp.float32),
        "cotangent": noise_with(streams_of[16], (PAGES, PAGE_LEN, D), 1.0, 6.0, ((0, 8), (1, 4)), (0, 2, 8, 2.0)),
    }


@jax.custom_vjp
def low(v):
    return lax.optimization_barrier(v.astype(jnp.bfloat16)).astype(jnp.float32)

@jax.custom_vjp
def low_back(v):
    return v

def low_keep(v):
    return (low(v), None)

def low_pass(kept, grad):
    return (grad,)

def back_keep(v):
    return (v, None)

def back_low(kept, grad):
    return (low(grad),)
low.defvjp(low_keep, low_pass)
low_back.defvjp(back_keep, back_low)
highest = lax.Precision.HIGHEST
norm_eps = 1e-12

def angles(boxes, count):
    freqs = 10000.0 ** (-jnp.arange(count, dtype=jnp.float32) / count)
    theta = boxes.astype(jnp.float32)[..., :, None] * freqs
    theta = theta.reshape(boxes.shape[:-1] + (4 * count,))
    return (jnp.sin(theta), jnp.cos(theta))

def layer_norm(resid, gain, shift):
    center = resid - lax.optimization_barrier(jnp.mean(resid, axis=-1, keepdims=True))
    spread = lax.optimization_barrier(jnp.mean(center * center, axis=-1, keepdims=True))
    return center * lax.rsqrt(spread + norm_eps) * gain + shift

def block_layer(inputs, weights, lengths, boxes):
    qkv_weight, qkv_bias, box_weight, out_weight, out_bias, norm1_gain, norm1_bias, up_weight, up_bias, down_weight, down_bias, norm2_gain, norm2_bias = weights
    group, seq_len, width = inputs.shape
    half = POS // 2
    projected = jnp.einsum('gtd,de->gte', inputs, qkv_weight, precision=highest) + qkv_bias
    projected = low(low_back(projected))
    query_rows = projected[..., :width].reshape(group, seq_len, HEADS, HD)
    key_rows = projected[..., width:2 * width].reshape(group, seq_len, HEADS, HD)
    value_rows = projected[..., 2 * width:].reshape(group, seq_len, HEADS, HD)
    sines, cosines = angles(boxes, POS // 8)
    sine_h = sines[:, :, None, :]
    cosine_h = cosines[:, :, None, :]
    query_proj = jnp.einsum('gthd,de->gthe', query_rows, box_weight, precision=highest)
    q_sin, q_cos = (query_proj[..., :half], query_proj[..., half:])
    query_pos = low(jnp.concatenate([q_sin * cosine_h + q_cos * sine_h, q_cos * cosine_h - q_sin * sine_h], -1))
    key_proj = jnp.einsum('gthd,de->gthe', key_rows, box_weight, precision=highest)
    k_sin, k_cos = (key_proj[..., :half], key_proj[..., half:])
    key_pos = low(jnp.concatenate([k_cos * sine_h - k_sin * cosine_h, k_sin * sine_h + k_cos * cosine_h], -1))
    basis = low(jnp.concatenate([sines, cosines], -1))
    raw = jnp.einsum('gihd,gjhd->ghij', query_rows, key_rows, precision=highest)
    raw = raw + jnp.einsum('gihe,gje->ghij', query_pos, basis, precision=highest)
    raw = raw + jnp.einsum('gie,gjhe->ghij', basis, key_pos, precision=highest)
    scores = low_back(raw * HD ** (-0.5))
    valid = jnp.arange(seq_len, dtype=jnp.int32)[None, :] < lengths[:, None]
    scores = jnp.where(valid[:, None, None, :], scores, -1e+30)
    probs = jax.nn.softmax(scores, axis=-1)
    context = jnp.einsum('ghij,gjhd->gihd', low(probs), value_rows, precision=highest)
    context = low(low_back(context.reshape(group, seq_len, width)))
    attention = low_back(jnp.einsum('gtd,de->gte', context, out_weight, precision=highest) + out_bias)
    hidden1 = layer_norm(inputs + attention, norm1_gain, norm1_bias)
    upper = low_back(jnp.einsum('gtd,df->gtf', low(hidden1), up_weight, precision=highest) + up_bias)
    activated = low(jax.nn.gelu(upper, approximate=False))
    ffn_out = low_back(jnp.einsum('gtf,fd->gtd', activated, down_weight, precision=highest) + down_bias)
    return layer_norm(hidden1 + ffn_out, norm2_gain, norm2_bias)

def reference(tokens, lengths, boxes, qkv_weight, qkv_bias, box_weight, out_weight, out_bias, norm1_gain, norm1_bias, up_weight, up_bias, down_weight, down_bias, norm2_gain, norm2_bias, cotangent):
    weights = tuple((w.astype(jnp.float32) for w in (qkv_weight, qkv_bias, box_weight, out_weight, out_bias, norm1_gain, norm1_bias, up_weight, up_bias, down_weight, down_bias, norm2_gain, norm2_bias)))
    group = math.gcd(PAGES, max(1, 4096 // PAGE_LEN))
    steps_count = PAGES // group

    def grouped(array):
        return array.reshape((steps_count, group) + array.shape[1:])

    def group_step(totals, item):
        inputs, grad_out, page_lengths, page_boxes = item

        def forward(inputs_f, *weight_list):
            return block_layer(inputs_f, weight_list, page_lengths, page_boxes)
        output, pullback = jax.vjp(forward, inputs.astype(jnp.float32), *weights)
        grads = pullback(grad_out.astype(jnp.float32))
        totals = tuple((acc + grad for acc, grad in zip(totals, grads[1:])))
        return (totals, (output.astype(jnp.bfloat16), grads[0].astype(jnp.bfloat16)))
    start = tuple((jnp.zeros(w.shape, jnp.float32) for w in weights))
    totals, (outputs, input_grads) = lax.scan(group_step, start, (grouped(tokens), grouped(cotangent), grouped(lengths), grouped(boxes)))
    layer_output = outputs.reshape(PAGES, PAGE_LEN, D)
    input_grad = input_grads.reshape(PAGES, PAGE_LEN, D)
    return (layer_output, input_grad, totals[0], totals[1], totals[2].reshape(-1), totals[3], totals[4], totals[5], totals[6], totals[7], totals[8], totals[9], totals[10], totals[11], totals[12])
```

```python
import functools

import jax
import jax.numpy as jnp
from jax import lax
from jax.experimental import pallas as pl
from jax.experimental.pallas import tpu as pltpu
from jax.sharding import PartitionSpec as P

HEADS = 12


norm_eps = 1e-12
highest = lax.Precision.HIGHEST


def shortened(shard):

    def short(part):
        return part.astype(jnp.bfloat16) if part.dtype == jnp.float32 else part

    return jax.tree.map(short, shard)


def angles(boxes, count):
    freqs = 10000.0 ** (-(lax.iota(jnp.float32, count) / count))
    theta = boxes.astype(jnp.float32)[..., :, None] * freqs
    theta = theta.reshape(boxes.shape[:-1] + (4 * count,))
    return (jnp.sin(theta), jnp.cos(theta))


def layer_norm(resid, gain, shift):
    center = resid - jnp.mean(resid, axis=-1, keepdims=True)
    spread = jnp.mean(center * center, axis=-1, keepdims=True)
    return center * lax.rsqrt(spread + norm_eps) * gain + shift


def gelu_exact(values):
    return jax.nn.gelu(values, approximate=False)


def key_parts(key_rows, boxes, box_weight, heads):
    pages, count, width = key_rows.shape
    head_dim = width // heads
    half = box_weight.shape[1] // 2
    keyed = key_rows.reshape(pages, count, heads, head_dim)
    sines, cosines = angles(boxes, box_weight.shape[1] // 8)
    sine_h = sines[:, :, None, :]
    cosine_h = cosines[:, :, None, :]
    key_proj = jnp.einsum("pthd,de->pthe", keyed, box_weight, preferred_element_type=jnp.float32)
    k_sin, k_cos = (key_proj[..., :half], key_proj[..., half:])
    key_pos = jnp.concatenate(
        [k_cos * sine_h - k_sin * cosine_h, k_sin * sine_h + k_cos * cosine_h], -1
    )
    basis = jnp.concatenate([sines, cosines], -1).astype(jnp.bfloat16)
    return (jnp.concatenate([keyed, key_pos.astype(jnp.bfloat16)], -1), basis)


def join_features(head_part, basis, head_dim):
    pages, count, heads, _ = head_part.shape
    basis_heads = jnp.broadcast_to(basis[:, :, None, :], (pages, count, heads, basis.shape[-1]))
    return jnp.concatenate([head_part[..., :head_dim], basis_heads, head_part[..., head_dim:]], -1)


def local(
    tokens,
    lengths,
    boxes,
    qkv_weight,
    qkv_bias,
    box_weight,
    out_weight,
    out_bias,
    norm1_gain,
    norm1_bias,
    up_weight,
    up_bias,
    down_weight,
    down_bias,
    norm2_gain,
    norm2_bias,
    cotangent,
):
    pages, block, width = tokens.shape
    heads = HEADS
    head_dim = width // heads
    pos_width = box_weight.shape[1]
    half = pos_width // 2
    scale = head_dim ** (-0.5)
    row_count = pages * block
    flat_in = tokens.reshape(row_count, width)
    projected = (
        jnp.dot(flat_in, qkv_weight, preferred_element_type=jnp.float32) + qkv_bias
    ).astype(jnp.bfloat16)
    query_rows = projected[:, :width].reshape(pages, block, heads, head_dim)
    key_rows = projected[:, width : 2 * width].reshape(pages, block, width)
    value_rows = projected[:, 2 * width :].reshape(pages, block, width)
    sines, cosines = angles(boxes, pos_width // 8)
    sine_h = sines[:, :, None, :]
    cosine_h = cosines[:, :, None, :]
    query_proj = jnp.einsum(
        "pthd,de->pthe", query_rows, box_weight, preferred_element_type=jnp.float32
    )
    q_sin, q_cos = (query_proj[..., :half], query_proj[..., half:])
    query_pos = jnp.concatenate(
        [q_sin * cosine_h + q_cos * sine_h, q_cos * cosine_h - q_sin * sine_h], -1
    )
    basis = jnp.concatenate([sines, cosines], -1).astype(jnp.bfloat16)
    basis_heads = jnp.broadcast_to(basis[:, :, None, :], (pages, block, heads, pos_width))
    query_feat = jnp.concatenate([query_rows, query_pos.astype(jnp.bfloat16), basis_heads], -1)
    all_keys, all_values, all_boxes = (
        lax.all_gather(key_rows, "blk", axis=1, tiled=True),
        lax.all_gather(value_rows, "blk", axis=1, tiled=True),
        lax.all_gather(boxes, "blk", axis=1, tiled=True),
    )
    head_part, key_basis = key_parts(all_keys, all_boxes, box_weight, heads)
    key_feat = join_features(head_part, key_basis, head_dim)
    seq_len = all_values.shape[1]
    values_h = all_values.reshape(pages, seq_len, heads, head_dim)
    valid = (lax.iota(jnp.int32, seq_len)[None, :] < lengths[:, None])[:, None, None, :]

    def score_pages():
        raw = (
            jnp.einsum("pihe,pjhe->phij", query_feat, key_feat, preferred_element_type=jnp.float32)
            * scale
        )
        return jnp.where(valid, raw, -1e30)

    scores = score_pages()
    top_score = jnp.max(scores, axis=-1, keepdims=True)
    expanded = jnp.exp(scores - top_score)
    summed = jnp.sum(expanded, axis=-1, keepdims=True)
    log_total = top_score + jnp.log(summed)
    probs_low = (expanded / summed).astype(jnp.bfloat16)
    context = jnp.einsum("phij,pjhd->pihd", probs_low, values_h, preferred_element_type=jnp.float32)
    context = context.reshape(row_count, width).astype(jnp.bfloat16)
    attention = jnp.dot(context, out_weight, preferred_element_type=jnp.float32) + out_bias
    resid1 = flat_in.astype(jnp.float32) + attention
    hidden1, norm1_pull = jax.vjp(layer_norm, resid1, norm1_gain, norm1_bias)
    hidden1_low = hidden1.astype(jnp.bfloat16)
    upper = jnp.dot(hidden1_low, up_weight, preferred_element_type=jnp.float32) + up_bias
    activated, gelu_pull = jax.vjp(gelu_exact, upper)
    act_low = activated.astype(jnp.bfloat16)
    ffn_out = jnp.dot(act_low, down_weight, preferred_element_type=jnp.float32) + down_bias
    output_full, norm2_pull = jax.vjp(layer_norm, hidden1 + ffn_out, norm2_gain, norm2_bias)
    layer_output = output_full.astype(jnp.bfloat16).reshape(pages, block, width)
    dresid2, norm2_gain_grad, norm2_bias_grad = norm2_pull(
        cotangent.reshape(row_count, width).astype(jnp.float32)
    )
    dffn = dresid2.astype(jnp.bfloat16)
    down_weight_grad = jnp.dot(act_low.T, dffn, preferred_element_type=jnp.float32)
    down_bias_grad = jnp.sum(dffn.astype(jnp.float32), axis=0)
    dact = jnp.dot(dffn, down_weight.T, preferred_element_type=jnp.float32)
    (dupper,) = gelu_pull(dact)
    dupper_low = dupper.astype(jnp.bfloat16)
    up_weight_grad = jnp.dot(hidden1_low.T, dupper_low, preferred_element_type=jnp.float32)
    up_bias_grad = jnp.sum(dupper_low.astype(jnp.float32), axis=0)
    dhidden1 = jnp.dot(dupper_low, up_weight.T, preferred_element_type=jnp.float32) + dresid2
    dresid1, norm1_gain_grad, norm1_bias_grad = norm1_pull(dhidden1)
    dattn = dresid1.astype(jnp.bfloat16)
    out_weight_grad = jnp.dot(context.T, dattn, preferred_element_type=jnp.float32)
    out_bias_grad = jnp.sum(dattn.astype(jnp.float32), axis=0)
    dcontext = jnp.dot(dattn, out_weight.T, preferred_element_type=jnp.float32).astype(jnp.bfloat16)
    dcontext = dcontext.reshape(pages, block, heads, head_dim)
    probs = jnp.exp(score_pages() - log_total)
    probs_low = probs.astype(jnp.bfloat16)
    dprobs = jnp.einsum("pihd,pjhd->phij", dcontext, values_h, preferred_element_type=jnp.float32)
    dvalues = jnp.einsum("phij,pihd->pjhd", probs_low, dcontext, preferred_element_type=jnp.float32)
    delta = jnp.sum(probs * dprobs, axis=-1, keepdims=True)
    dscores = (probs * (dprobs - delta)).astype(jnp.bfloat16)
    dquery_feat = (
        jnp.einsum("phij,pjhe->pihe", dscores, key_feat, preferred_element_type=jnp.float32) * scale
    )
    dkey_feat = (
        jnp.einsum("phij,pihe->pjhe", dscores, query_feat, preferred_element_type=jnp.float32)
        * scale
    )
    dq_pos = dquery_feat[..., head_dim : head_dim + pos_width]
    dq_first, dq_second = (dq_pos[..., :half], dq_pos[..., half:])
    dquery_proj = jnp.concatenate(
        [dq_first * cosine_h - dq_second * sine_h, dq_first * sine_h + dq_second * cosine_h], -1
    )
    key_sines, key_cosines = angles(all_boxes, pos_width // 8)
    key_sine_h = key_sines[:, :, None, :]
    key_cosine_h = key_cosines[:, :, None, :]
    dk_pos = dkey_feat[..., head_dim + pos_width :]
    dk_first, dk_second = (dk_pos[..., :half], dk_pos[..., half:])
    dkey_proj = jnp.concatenate(
        [
            dk_second * key_sine_h - dk_first * key_cosine_h,
            dk_first * key_sine_h + dk_second * key_cosine_h,
        ],
        -1,
    )
    box_float = box_weight.astype(jnp.float32)
    keyed = key_feat[..., :head_dim].astype(jnp.float32)
    box_grad = jnp.einsum(
        "pthd,pthe->de", query_rows.astype(jnp.float32), dquery_proj, precision=highest
    )
    box_grad = box_grad + jnp.einsum("pthd,pthe->de", keyed, dkey_proj, precision=highest)
    dquery = dquery_feat[..., :head_dim] + jnp.einsum(
        "pthe,de->pthd", dquery_proj, box_float, precision=highest
    )
    dkey = dkey_feat[..., :head_dim] + jnp.einsum(
        "pthe,de->pthd", dkey_proj, box_float, precision=highest
    )
    key_terms = jnp.concatenate(
        [dkey.reshape(pages, seq_len, width), dvalues.reshape(pages, seq_len, width)], -1
    )
    key_sums = lax.psum_scatter(
        key_terms.astype(jnp.bfloat16), "blk", scatter_dimension=1, tiled=True
    ).astype(jnp.float32)
    dprojected = jnp.concatenate(
        [dquery.reshape(row_count, width), key_sums.reshape(row_count, 2 * width)], -1
    )
    dprojected = dprojected.astype(jnp.bfloat16)
    qkv_weight_grad = jnp.dot(flat_in.T, dprojected, preferred_element_type=jnp.float32)
    qkv_bias_grad = jnp.sum(dprojected.astype(jnp.float32), axis=0)
    input_grad = jnp.dot(dprojected, qkv_weight.T, preferred_element_type=jnp.float32) + dresid1
    input_grad = input_grad.astype(jnp.bfloat16).reshape(pages, block, width)
    box_flat = box_grad.reshape(-1)
    shards = lax.axis_size("page")
    grads = (
        qkv_weight_grad,
        qkv_bias_grad,
        box_flat,
        out_weight_grad,
        out_bias_grad,
        norm1_gain_grad,
        norm1_bias_grad,
        up_weight_grad,
        up_bias_grad,
        down_weight_grad,
        down_bias_grad,
        norm2_gain_grad,
        norm2_bias_grad,
    )
    if shards == 8 and lax.axis_size("blk") == 4:
        sums = reduce_by_kernel(grads)
    else:
        sums = reduce_by_collectives(grads)
    return (layer_output, input_grad, *sums)


def reduce_by_collectives(grads):
    page_sums = tuple(
        lax.psum_scatter(grad, "page", scatter_dimension=0, tiled=True) for grad in grads
    )
    return jax.tree.map(
        lambda part: part.astype(jnp.float32), lax.psum(shortened(page_sums), "blk")
    )


MESH = pl.DeviceIdType.MESH
LANES = 128
SMALL_ROWS = 16
ORDERS = ((0, 1, 2), (1, 2, 0), (2, 0, 1))


def flip(page, way):
    x, z = page % 2, page // 2
    if way == 0:
        return z * 2 + (1 - x)
    if way == 1:
        return (z + 1 - 2 * (z % 2)) * 2 + x
    return (3 - z) * 2 + x


def core_of(blk):
    return blk + 1 - 2 * (blk % 2)


def side_of(blk):
    return (blk + 2) % 4


def shard_at(page, order, code):
    for place, way in enumerate(ORDERS[order]):
        if code >> (2 - place) & 1:
            page = flip(page, way)
    return page


def greet(page, blk):
    barrier = pltpu.get_barrier_semaphore()
    others = [(flip(page, way), blk) for way in range(3)]
    others += [(page, core_of(blk)), (page, side_of(blk))]
    for other in others:
        pl.semaphore_signal(barrier, inc=1, device_id=other, device_id_type=MESH)
    pl.semaphore_wait(barrier, len(others))


def reduce_kernel(
    packed, up_ref, down_ref, out_ref, qkv_ref, small_ref,
    held, from_core, got1, got2, got3, got_side, total, got_core,
    local_sem, core_send, core_recv, send1, recv1, send2, recv2, send3, recv3,
    side_send, side_recv, last_send, last_recv,
):
    page, blk = lax.axis_index("page"), lax.axis_index("blk")
    core = blk % 2
    greet(page, blk)
    mate = (page, core_of(blk))
    side = (page, side_of(blk))

    def send(src, dst, sems, recv, to):
        copy = pltpu.make_async_remote_copy(
            src_ref=src, dst_ref=dst, send_sem=sems, recv_sem=recv, device_id=to,
            device_id_type=MESH,
        )
        copy.start()
        return copy

    codes = (6, 7, 4, 5, 2, 3, 0, 1)
    first, locals_ = {}, {}
    for code in codes:
        for order in range(3):
            shard = shard_at(page, order, code)
            first[order, code] = send(
                packed.at[1 - core, order, shard], from_core.at[order, code],
                core_send.at[order, code], core_recv.at[order, code], mate,
            )
            copy = pltpu.make_async_copy(
                packed.at[core, order, shard], held.at[order, code], local_sem.at[order, code]
            )
            copy.start()
            locals_[order, code] = copy
    sent = {}

    def partner(order, place):
        return (flip(page, ORDERS[order][place]), blk)

    for code in codes:
        for order in range(3):
            locals_[order, code].wait()
            first[order, code].wait_recv()
            held[order, code] = held[order, code] + from_core[order, code]
            if code >= 4:
                slot = code - 4
                sent[1, order, slot] = send(
                    held.at[order, code], got1.at[order, slot], send1.at[order, slot],
                    recv1.at[order, slot], partner(order, 0),
                )
    for slot in (2, 3, 0, 1):
        for order in range(3):
            sent[1, order, slot].wait_recv()
            held[order, slot] = held[order, slot] + got1[order, slot]
            if slot >= 2:
                sent[2, order, slot - 2] = send(
                    held.at[order, slot], got2.at[order, slot - 2], send2.at[order, slot - 2],
                    recv2.at[order, slot - 2], partner(order, 1),
                )
    for slot in (1, 0):
        for order in range(3):
            sent[2, order, slot].wait_recv()
            held[order, slot] = held[order, slot] + got2[order, slot]
            if slot == 1:
                sent[3, order] = send(
                    held.at[order, 1], got3.at[order], send3.at[order], recv3.at[order],
                    partner(order, 2),
                )
    for order in range(3):
        sent[3, order].wait_recv()
        held[order, 0] = held[order, 0] + got3[order]
        sent[4, order] = send(
            held.at[order, 0], got_side.at[order], side_send.at[order], side_recv.at[order], side
        )

    def write(part, order, which):
        rows = part[order].astype(jnp.float32)
        at = 0
        for piece in range(4):
            lanes = pl.ds(pl.multiple_of(which * 1536 + order * 512 + piece * LANES, LANES), LANES)
            up_ref[:, lanes] = rows[at : at + 96]
            at += 96
        lanes = pl.ds(pl.multiple_of(which * 384 + order * LANES, LANES), LANES)
        down_ref[:, lanes] = rows[at : at + 384]
        at += 384
        out_ref[:, lanes] = rows[at : at + 96]
        at += 96
        for piece in range(3):
            lanes = pl.ds(pl.multiple_of(piece * 768 + which * 384 + order * LANES, LANES), LANES)
            qkv_ref[:, lanes] = rows[at : at + 96]
            at += 96
        small_ref[pl.ds(which, 1), order] = rows[None, at : at + SMALL_ROWS]

    for order in range(3):
        sent[4, order].wait_recv()
        total[order] = held[order, 0] + got_side[order]
        sent[5, order] = send(
            total.at[order], got_core.at[order], last_send.at[order], last_recv.at[order], mate
        )
        write(total, order, core)
    for order in range(3):
        sent[5, order].wait_recv()
        write(got_core, order, 1 - core)
    for copy in first.values():
        copy.wait_send()
    for copy in sent.values():
        copy.wait_send()


def reduce_by_kernel(grads):
    (qkv_w, qkv_b, box, out_w, out_b, gain1, shift1, up_w, up_b, down_w, down_b, gain2, shift2) = grads
    vectors = (qkv_b, box, out_b, gain1, shift1, up_b, down_b, gain2, shift2)
    shards = lax.axis_size("page")
    low = jnp.bfloat16
    up = up_w.astype(low).reshape(8, 96, 2, 3, 4, LANES).transpose(2, 3, 0, 4, 1, 5)
    down = down_w.astype(low).reshape(8, 384, 2, 3, LANES).transpose(2, 3, 0, 1, 4)
    out = out_w.astype(low).reshape(8, 96, 2, 3, LANES).transpose(2, 3, 0, 1, 4)
    qkv = qkv_w.astype(low).reshape(8, 96, 3, 2, 3, LANES).transpose(3, 4, 0, 2, 1, 5)
    small = jnp.concatenate([v.reshape(shards, -1) for v in vectors], axis=1).astype(low)
    width = small.shape[1]
    small = jnp.pad(small, ((0, 0), (0, 6 * SMALL_ROWS * LANES - width)))
    small = small.reshape(8, 2, 3, SMALL_ROWS, LANES).transpose(1, 2, 0, 3, 4)
    packed = jnp.concatenate(
        [
            up.reshape(2, 3, 8, 384, LANES),
            down,
            out,
            qkv.reshape(2, 3, 8, 288, LANES),
            small,
        ],
        axis=3,
    )
    rows = packed.shape[3]
    f32 = jnp.float32
    dma = pltpu.SemaphoreType.DMA
    vmem = pltpu.VMEM
    whole = pl.BlockSpec(memory_space=pltpu.VMEM)
    up_s, down_s, out_s, qkv_s, small_s = pl.pallas_call(
        reduce_kernel,
        out_shape=(
            jax.ShapeDtypeStruct((96, 3072), f32),
            jax.ShapeDtypeStruct((384, 768), f32),
            jax.ShapeDtypeStruct((96, 768), f32),
            jax.ShapeDtypeStruct((96, 2304), f32),
            jax.ShapeDtypeStruct((2, 3, SMALL_ROWS, LANES), f32),
        ),
        in_specs=[pl.BlockSpec(memory_space=pl.ANY)],
        out_specs=(whole,) * 5,
        scratch_shapes=[
            vmem((3, 8, rows, LANES), low),
            vmem((3, 8, rows, LANES), low),
            vmem((3, 4, rows, LANES), low),
            vmem((3, 2, rows, LANES), low),
            vmem((3, rows, LANES), low),
            vmem((3, rows, LANES), low),
            vmem((3, rows, LANES), low),
            vmem((3, rows, LANES), low),
            dma((3, 8)), dma((3, 8)), dma((3, 8)),
            dma((3, 4)), dma((3, 4)),
            dma((3, 2)), dma((3, 2)),
            dma((3,)), dma((3,)),
            dma((3,)), dma((3,)),
            dma((3,)), dma((3,)),
        ],
        compiler_params=pltpu.CompilerParams(
            collective_id=1, has_side_effects=True, vmem_limit_bytes=56 * 2**20
        ),
        name="reduce_grads",
    )(packed)
    flat = small_s.reshape(-1)
    sums, at = [], 0
    for vector in vectors:
        count = vector.shape[0] // shards
        sums.append(flat[at : at + count])
        at += count
    qkv_b, box, out_b, gain1, shift1, up_b, down_b, gain2, shift2 = sums
    return (qkv_s, qkv_b, box, out_s, out_b, gain1, shift1, up_s, up_b, down_s, down_b, gain2, shift2)


def solution(mesh):
    return jax.shard_map(
        local,
        mesh=mesh,
        in_specs=(
            P("page", "blk", None),
            P("page"),
            P("page", "blk", None),
            P(),
            P(),
            P(),
            P(),
            P(),
            P(),
            P(),
            P(),
            P(),
            P(),
            P(),
            P(),
            P(),
            P("page", "blk", None),
        ),
        out_specs=(
            P("page", "blk", None),
            P("page", "blk", None),
            P("page", None),
            P("page"),
            P("page"),
            P("page", None),
            P("page"),
            P("page"),
            P("page"),
            P("page", None),
            P("page"),
            P("page", None),
            P("page"),
            P("page"),
            P("page"),
        ),
        check_vma=False,
    )
```

```python
import functools

import jax
import jax.numpy as jnp
import numpy as np
from jax import lax
from jax.experimental import pallas as pl
from jax.experimental.pallas import tpu as pltpu
from jax.sharding import PartitionSpec as P

norm_eps = 1e-12

MESH = pl.DeviceIdType.MESH
LANES = 128
SMALL_ROWS = 16
low = jnp.bfloat16
f32 = jnp.float32
ORDERS = ((0, 1, 2), (1, 2, 0), (2, 0, 1))


def flip(page, way):
    x, z = page % 2, page // 2
    if way == 0:
        return z * 2 + (1 - x)
    if way == 1:
        return (z + 1 - 2 * (z % 2)) * 2 + x
    return (3 - z) * 2 + x


def core_of(blk):
    return blk + 1 - 2 * (blk % 2)


def side_of(blk):
    return (blk + 2) % 4


def shard_at(page, order, code):
    for place, way in enumerate(ORDERS[order]):
        if code >> (2 - place) & 1:
            page = flip(page, way)
    return page


def greet(others):
    barrier = pltpu.get_barrier_semaphore()
    for other in others:
        pl.semaphore_signal(barrier, inc=1, device_id=other, device_id_type=MESH)
    pl.semaphore_wait(barrier, len(others))


def remote(src, dst, send_sem, recv_sem, to):
    return pltpu.make_async_remote_copy(
        src_ref=src, dst_ref=dst, send_sem=send_sem, recv_sem=recv_sem, device_id=to,
        device_id_type=MESH,
    )


def dot(a, b):
    return jnp.dot(a, b, preferred_element_type=f32)


def dot_nt(a, b):
    return lax.dot_general(a, b, (((1,), (1,)), ((), ())), preferred_element_type=f32)


def dot_tn(a, b):
    return lax.dot_general(a, b, (((0,), (0,)), ((), ())), preferred_element_type=f32)


def sin_cos(theta):
    turns = jnp.floor(theta * 0.6366197723675814 + 0.5)
    rest = theta - turns * 1.5703125
    rest = rest - turns * 4.837512969970703125e-4
    rest = rest - turns * 7.54978995489188216e-8
    square = rest * rest
    sine = ((-1.9515295891e-4 * square + 8.3321608736e-3) * square - 1.6666654611e-1) * square
    sine = sine * rest + rest
    cosine = (2.443315711809948e-5 * square - 1.388731625493765e-3) * square + 4.166664568298827e-2
    cosine = cosine * square * square - 0.5 * square + 1.0
    quarter = turns.astype(jnp.int32)
    odd = (quarter & 1) == 1
    sine_at = jnp.where(odd, cosine, sine)
    cosine_at = jnp.where(odd, sine, cosine)
    sine_at = jnp.where((quarter & 2) == 2, -sine_at, sine_at)
    cosine_at = jnp.where(((quarter + 1) & 2) == 2, -cosine_at, cosine_at)
    return sine_at, cosine_at


def lane_halves(shape):
    return lax.broadcasted_iota(jnp.int32, shape, 1) < LANES // 2


def turned(both):
    swapped = pltpu.roll(both, LANES // 2, 1)
    left = lane_halves(both.shape)
    return jnp.where(left, -swapped, both), jnp.where(left, both, swapped)


def rotate_key(proj, cosine2, sine2):
    return proj * cosine2 + pltpu.roll(proj, LANES // 2, 1) * sine2


def attend_kernel(
    tokens, boxes, lengths, freq, qkv_w, qkv_b, box2,
    x_out, q_out, k_out, v_out, sc_out, p_out, ctx_out,
    x, box, w_q, w_kv, q, k, v, sc, probs, ctx,
    own_sem, w_sem, out_sem, p_sem, ctx_sem,
    mate_send, mate_recv, side_send, side_recv, pass_send, pass_recv, ctx_send, ctx_recv,
):
    page, blk = lax.axis_index("page"), lax.axis_index("blk")
    core, side_at = blk % 2, blk // 2
    mate, side = (page, core_of(blk)), (page, side_of(blk))
    pages = tokens.shape[0]
    half = w_q.shape[1]
    pairs = half // LANES
    chip = 2 * tokens.shape[1]
    keys = 2 * chip
    scale = 0.125

    def of_half(part):
        return pl.ds(pl.multiple_of(part * 2 * half + core * half, LANES), half)

    loads = [
        pltpu.make_async_copy(qkv_w.at[:, of_half(0)], w_q, w_sem.at[0]),
        pltpu.make_async_copy(qkv_w.at[:, of_half(1)], w_kv.at[:, :half], w_sem.at[1]),
        pltpu.make_async_copy(qkv_w.at[:, of_half(2)], w_kv.at[:, half:], w_sem.at[2]),
    ]
    own = []
    for pg in range(pages):
        own.append(pltpu.make_async_copy(tokens.at[pg], x.at[pg, core], own_sem.at[pg, 0]))
        own.append(pltpu.make_async_copy(boxes.at[pg], box.at[pg, core], own_sem.at[pg, 1]))
    for copy in own:
        copy.start()
    for copy in loads:
        copy.start()
    greet((mate, side))
    to_mate, to_side = [], []
    for pg in range(pages):
        for which, (src, dst) in enumerate(((tokens, x), (boxes, box))):
            to_side.append(
                remote(src.at[pg], dst.at[pg, 2 + core], side_send.at[pg, which], side_recv.at[pg, which], side)
            )
            to_side[-1].start()
            to_mate.append(
                remote(src.at[pg], dst.at[pg, core], mate_send.at[pg, which], mate_recv.at[pg, which], mate)
            )
            to_mate[-1].start()
    for copy in loads:
        copy.wait()

    @pl.loop(0, pages)
    def _(pg):
        passed = []
        for which, (src, dst) in enumerate(((tokens, x), (boxes, box))):
            remote(
                src.at[pg], dst.at[pg, 2 + core], side_send.at[pg, which], side_recv.at[pg, which], side
            ).wait_recv()
            copy = remote(
                dst.at[pg, 2 + core], dst.at[pg, 2 + core], pass_send.at[pg, which],
                pass_recv.at[pg, which], mate,
            )
            copy.start()
            passed.append(copy)
            pltpu.make_async_copy(src.at[pg], dst.at[pg, core], own_sem.at[pg, which]).wait()
            remote(
                src.at[pg], dst.at[pg, core], mate_send.at[pg, which], mate_recv.at[pg, which], mate
            ).wait_recv()
        for copy in passed:
            copy.wait_recv()
        pltpu.make_async_copy(x.at[pg], x_out.at[pg], out_sem.at[pg, 0]).start()
        for at in range(4):
            rows = box[pg, at]
            spread = [
                jnp.broadcast_to(rows[c : c + 1], (freq.shape[0] // 4, LANES)) for c in range(4)
            ]
            sine, cosine = sin_cos(jnp.concatenate(spread, 0) * freq[...])
            sc[pg, at * LANES : (at + 1) * LANES] = jnp.concatenate([sine, cosine], 0).T
        pltpu.make_async_copy(sc.at[pg], sc_out.at[pg], out_sem.at[pg, 1]).start()
        x_all = x[pg].reshape(keys, x.shape[-1])
        q_all = (dot(x_all[:chip], w_q[...]) + qkv_b[:, of_half(0)]).astype(low)
        bias = jnp.concatenate([qkv_b[:, of_half(1)], qkv_b[:, of_half(2)]], 1)
        kv_all = (dot(x_all, w_kv[...]) + bias).astype(low)
        for hp in range(pairs):
            q[pg, hp] = q_all[:, hp * LANES : (hp + 1) * LANES]
            k[pg, hp] = kv_all[:, hp * LANES : (hp + 1) * LANES]
            v[pg, hp] = kv_all[:, half + hp * LANES : half + (hp + 1) * LANES]
        for which, (src, dst) in enumerate(((q, q_out), (k, k_out), (v, v_out))):
            pltpu.make_async_copy(src.at[pg], dst.at[pg], out_sem.at[pg, 2 + which]).start()
        place = lax.broadcasted_iota(jnp.int32, (keys, chip), 0) + side_at * chip
        place = jnp.where(place >= keys, place - keys, place)
        valid = place < lengths[pg]

        @pl.loop(0, pairs)
        def _(hp):
            both = sc[pg]
            cosine2, sine2 = turned(both)
            basis = both.astype(low)
            basis_q = (both[:chip] * scale).astype(low)
            left = lane_halves((chip, LANES))
            cosine_q = jnp.where(left, -cosine2[:chip], cosine2[:chip]) * scale
            sine_q = jnp.where(left, sine2[:chip], -sine2[:chip]) * scale
            q_pair, k_pair = q[pg, hp], k[pg, hp]
            q_proj = dot(q_pair, box2[...])
            k_proj = dot(k_pair, box2[...])
            v_t = v[pg, hp].T
            outs = []
            for e in range(2):
                at = slice(e * LANES, (e + 1) * LANES)
                q_pos = rotate_key(q_proj[:, at], cosine_q, sine_q).astype(low)
                k_pos = rotate_key(k_proj[:, at], cosine2, sine2).astype(low)
                mine = left if e == 0 else jnp.logical_not(left)
                q_own = jnp.where(mine, q_pair.astype(f32) * scale, 0.0).astype(low)
                scores = dot_nt(
                    jnp.concatenate([basis, k_pos], 1), jnp.concatenate([q_pos, basis_q], 1)
                )
                scores = scores + dot_nt(k_pair, q_own)
                scores = jnp.where(valid, scores, -1e30)
                top = jnp.max(scores, axis=0, keepdims=True)
                grown = jnp.exp(scores - top)
                total = jnp.sum(grown, axis=0, keepdims=True)
                p = (grown * (1.0 / total)).astype(low)
                probs[pg, hp, e] = p
                outs.append(dot(v_t[e * LANES // 2 : (e + 1) * LANES // 2], p))
            pltpu.make_async_copy(probs.at[pg, hp], p_out.at[pg, hp], p_sem.at[pg, hp]).start()
            context = jnp.concatenate(outs, 0).T.astype(low)
            lanes = pl.ds(pl.multiple_of(hp * LANES, LANES), LANES)
            ctx[pg, 0, :, lanes] = context[: chip // 2]
            ctx[pg, 1, :, lanes] = context[chip // 2 :]

        mine = pl.ds(pl.multiple_of(core * half, LANES), half)
        pltpu.make_async_copy(ctx.at[pg, core], ctx_out.at[pg, :, mine], ctx_sem.at[pg]).start()
        remote(
            ctx.at[pg, 1 - core], ctx_out.at[pg, :, mine], ctx_send.at[pg], ctx_recv.at[pg], mate
        ).start()
        for copy in passed:
            copy.wait_send()

    mine = pl.ds(pl.multiple_of(core * half, LANES), half)
    for pg in range(pages):
        for which, (src, dst) in enumerate(((x, x_out), (sc, sc_out), (q, q_out), (k, k_out), (v, v_out))):
            pltpu.make_async_copy(src.at[pg], dst.at[pg], out_sem.at[pg, which]).wait()
        for hp in range(pairs):
            pltpu.make_async_copy(probs.at[pg, hp], p_out.at[pg, hp], p_sem.at[pg, hp]).wait()
        pltpu.make_async_copy(ctx.at[pg, core], ctx_out.at[pg, :, mine], ctx_sem.at[pg]).wait()
        remote(
            ctx.at[pg, 1 - core], ctx_out.at[pg, :, mine], ctx_send.at[pg], ctx_recv.at[pg], mate
        ).wait()
    for copy in to_side + to_mate:
        copy.wait_send()


def any_spec():
    return pl.BlockSpec(memory_space=pl.ANY)


def vmem_spec():
    return pl.BlockSpec(memory_space=pltpu.VMEM)


def attend(tokens, boxes, lengths, qkv_w, qkv_b, box_weight):
    pages, block, width = tokens.shape
    head_dim, pos = box_weight.shape
    half = width // 2
    pairs = half // LANES
    chip, keys = 2 * block, 4 * block
    count = pos // 8
    freqs = 10000.0 ** (-np.arange(count) / count)
    freq = jnp.asarray(np.tile(np.tile(freqs, 4)[:, None], (1, LANES)), f32)
    boxes_t = jnp.pad(boxes.astype(f32).transpose(0, 2, 1), ((0, 0), (0, 4), (0, 0)))
    zero = jnp.zeros_like(box_weight)
    box2 = jnp.concatenate(
        [jnp.concatenate([box_weight, zero], 1), jnp.concatenate([zero, box_weight], 1)], 0
    )
    struct = jax.ShapeDtypeStruct
    vmem, dma = pltpu.VMEM, pltpu.SemaphoreType.DMA
    return pl.pallas_call(
        attend_kernel,
        out_shape=(
            struct((pages, 4, block, width), low),
            struct((pages, pairs, chip, LANES), low),
            struct((pages, pairs, keys, LANES), low),
            struct((pages, pairs, keys, LANES), low),
            struct((pages, keys, LANES), f32),
            struct((pages, pairs, 2, keys, chip), low),
            struct((pages, block, width), low),
        ),
        in_specs=[any_spec(), any_spec(), pl.BlockSpec(memory_space=pltpu.SMEM), vmem_spec(), any_spec(), vmem_spec(), vmem_spec()],
        out_specs=(any_spec(),) * 7,
        scratch_shapes=[
            vmem((pages, 4, block, width), low),
            vmem((pages, 4, 8, LANES), f32),
            vmem((width, half), low),
            vmem((width, 2 * half), low),
            vmem((pages, pairs, chip, LANES), low),
            vmem((pages, pairs, keys, LANES), low),
            vmem((pages, pairs, keys, LANES), low),
            vmem((pages, keys, LANES), f32),
            vmem((pages, pairs, 2, keys, chip), low),
            vmem((pages, 2, block, half), low),
            dma((pages, 2)), dma((3,)), dma((pages, 5)), dma((pages, pairs)), dma((pages,)),
            dma((pages, 2)), dma((pages, 2)), dma((pages, 2)), dma((pages, 2)),
            dma((pages, 2)), dma((pages, 2)), dma((pages,)), dma((pages,)),
        ],
        compiler_params=pltpu.CompilerParams(
            collective_id=1, has_side_effects=True, vmem_limit_bytes=56 * 2**20
        ),
        name="attend",
    )(tokens, boxes_t, lengths, freq, qkv_w, qkv_b.reshape(1, -1), box2)


def norm_of(resid):
    center = resid - jnp.mean(resid, axis=-1, keepdims=True)
    spread = jnp.mean(center * center, axis=-1, keepdims=True)
    inverse = lax.rsqrt(spread + norm_eps)
    return center * inverse, inverse


def norm_back(grad, normed, inverse):
    mean = jnp.mean(grad, axis=-1, keepdims=True)
    along = jnp.mean(grad * normed, axis=-1, keepdims=True)
    return inverse * (grad - mean - normed * along)


def column_sum(values):
    return jnp.sum(values, axis=0, keepdims=True)


def feed_kernel(
    ctx, tokens, cotangent, out_w, up_w, down_w, out_b, gain1, shift1, up_b, down_b, gain2, shift2,
    output, dresid1, dctx, packed, g_up_b, g_rows,
    w_out, w_up, w_down, act, slope, norm1, inverse1, hidden, hidden_t, grow, staged, w_sem, up_sem, down_sem, pack_sem,
):
    chunks, chunk = w_up.shape[0], w_up.shape[2]
    width = ctx.shape[1]
    up_pieces = chunk // LANES
    shard = width // 8
    out_load = pltpu.make_async_copy(out_w, w_out, w_sem)
    out_load.start()

    def up_load(j):
        return pltpu.make_async_copy(
            up_w.at[:, pl.ds(pl.multiple_of(j * chunk, LANES), chunk)], w_up.at[j], up_sem.at[j]
        )

    def down_load(j):
        return pltpu.make_async_copy(
            down_w.at[pl.ds(pl.multiple_of(j * chunk, LANES), chunk)], w_down.at[j], down_sem.at[j]
        )

    for j in range(chunks):
        up_load(j).start()
        down_load(j).start()
    out_load.wait()
    resid = tokens[...].astype(f32) + dot(ctx[...], w_out[...]) + out_b[...]
    normed, inverse = norm_of(resid)
    norm1[...] = normed
    inverse1[...] = jnp.broadcast_to(inverse, inverse1.shape)
    first = normed * gain1[...] + shift1[...]
    hidden[...] = first.astype(low)
    hidden_t[...] = first.astype(low).T
    grow[...] = first + down_b[...]

    @pl.loop(0, chunks)
    def _(j):
        up_load(j).wait()
        upper = dot(hidden[...], w_up[j]) + up_b[pl.ds(j, 1)]
        cdf = 0.5 + 0.5 * lax.erf(upper * 0.7071067811865476)
        act_low = (upper * cdf).astype(low)
        act[j] = act_low
        slope[j] = cdf + upper * (jnp.exp(upper * upper * -0.5) * 0.3989422804014327)
        down_load(j).wait()
        grow[...] += dot(act_low, w_down[j])

    normed2, inverse2 = norm_of(grow[...])
    output[...] = (normed2 * gain2[...] + shift2[...]).astype(low)
    cot = cotangent[...].astype(f32)
    g_rows[0:1] = column_sum(cot * normed2)
    g_rows[1:2] = column_sum(cot)
    dresid2 = norm_back(cot * gain2[...], normed2, inverse2)
    dffn = dresid2.astype(low)
    g_rows[2:3] = column_sum(dffn.astype(f32))
    grow[...] = dresid2
    staged[...] = dffn

    @pl.loop(0, chunks)
    def _(j):
        dffn = staged[...]
        dupper = (dot_nt(dffn, w_down[j]) * slope[j]).astype(low)
        g_up_b[pl.ds(j, 1)] = column_sum(dupper.astype(f32))
        grow[...] += dot_nt(dupper, w_up[j])
        grad_up = dot(hidden_t[...], dupper).astype(low)
        for piece in range(up_pieces):
            part = grad_up[:, piece * LANES : (piece + 1) * LANES].reshape(8, shard, LANES)
            packed[j, :, piece * shard : (piece + 1) * shard] = part
        grad_down = dot_tn(act[j], dffn).astype(low)
        for piece in range(up_pieces):
            row = j * up_pieces + piece
            per = up_pieces * chunks // 8
            at = pl.ds(pl.multiple_of(up_pieces * shard + (row % per) * LANES, LANES), LANES)
            for column in range(6):
                packed[column, row // per, at] = grad_down[
                    piece * LANES : (piece + 1) * LANES, column * LANES : (column + 1) * LANES
                ]

    dhidden = grow[...]
    normed = norm1[...]
    g_rows[3:4] = column_sum(dhidden * normed)
    g_rows[4:5] = column_sum(dhidden)
    back = norm_back(dhidden * gain1[...], normed, inverse1[:, :1])
    dresid1[...] = back
    dattn = back.astype(low)
    g_rows[5:6] = column_sum(dattn.astype(f32))
    g_rows[6:8] = jnp.zeros((2, width), f32)
    dctx[...] = dot_nt(dattn, w_out[...]).astype(low)
    grad_out = dot_tn(ctx[...], dattn).astype(low)
    first_row = packed.shape[2] - shard
    for column in range(6):
        part = grad_out[:, column * LANES : (column + 1) * LANES].reshape(8, shard, LANES)
        packed[column, :, first_row:] = part


def feed(ctx, tokens, cotangent, out_w, up_w, down_w, out_b, gain1, shift1, up_b, down_b, gain2, shift2):
    rows, width = ctx.shape
    hidden_width = up_w.shape[1]
    chunks = 6
    chunk = hidden_width // chunks
    shard = width // 8
    packed_rows = (chunk // LANES) * shard + hidden_width // 8 + shard
    struct = jax.ShapeDtypeStruct
    vmem, dma = pltpu.VMEM, pltpu.SemaphoreType.DMA

    def row(vector):
        return vector.reshape(1, -1)

    return pl.pallas_call(
        feed_kernel,
        out_shape=(
            struct((rows, width), low),
            struct((rows, width), f32),
            struct((rows, width), low),
            struct((6, 8, packed_rows, LANES), low),
            struct((chunks, chunk), f32),
            struct((8, width), f32),
        ),
        in_specs=[vmem_spec()] * 3 + [any_spec()] * 3 + [vmem_spec()] * 7,
        out_specs=(vmem_spec(),) * 6,
        scratch_shapes=[
            vmem((width, width), low),
            vmem((chunks, width, chunk), low),
            vmem((chunks, chunk, width), low),
            vmem((chunks, rows, chunk), low),
            vmem((chunks, rows, chunk), f32),
            vmem((rows, width), f32),
            vmem((rows, LANES), f32),
            vmem((rows, width), low),
            vmem((width, rows), low),
            vmem((rows, width), f32),
            vmem((rows, width), low),
            dma, dma((chunks,)), dma((chunks,)), dma,
        ],
        compiler_params=pltpu.CompilerParams(vmem_limit_bytes=60 * 2**20),
        name="feed",
    )(
        ctx, tokens, cotangent, out_w, up_w, down_w, row(out_b), row(gain1), row(shift1),
        up_b.reshape(chunks, chunk), row(down_b), row(gain2), row(shift2),
    )


def attend_back_kernel(
    dctx_own, x_in, q_in, k_in, v_in, sc_in, p_in, qkv_w, box_w, dresid1,
    input_grad, packed, g_bias, g_box,
    x, q, k, v, sc, probs, dctx, dq, dkv, x_t, w_c, dx, dx_mate, dx_side, box_t,
    in_sem, p_sem, w_sem, own_sem, mate_send, mate_recv, core_send, core_recv, side_send, side_recv,
):
    page, blk = lax.axis_index("page"), lax.axis_index("blk")
    core = blk % 2
    mate, side = (page, core_of(blk)), (page, side_of(blk))
    pages, pairs, chip, _ = q.shape
    keys = k.shape[2]
    block = chip // 2
    half = pairs * LANES
    width = x.shape[-1]
    head = LANES // 2
    scale = 0.125

    def of_half(part, which):
        return pl.ds(pl.multiple_of(part * 2 * half + which * half, LANES), half)

    def loads(pg):
        names = ((x_in, x), (q_in, q), (k_in, k), (v_in, v), (sc_in, sc))
        return [
            pltpu.make_async_copy(src.at[pg], dst.at[pg], in_sem.at[pg, at])
            for at, (src, dst) in enumerate(names)
        ]

    def p_load(hp, pg):
        return pltpu.make_async_copy(p_in.at[pg, hp], probs.at[pg, hp], p_sem.at[pg, hp])

    w_loads = [
        pltpu.make_async_copy(qkv_w.at[:, of_half(part, core)], w_c.at[part], w_sem.at[part])
        for part in range(3)
    ]

    def own_copy(pg):
        return pltpu.make_async_copy(
            dctx_own.at[pg, :, of_half(0, core)], dctx.at[pg, core], own_sem.at[pg]
        )

    def mate_copy(pg):
        return remote(
            dctx_own.at[pg, :, of_half(0, 1 - core)], dctx.at[pg, core], mate_send.at[pg],
            mate_recv.at[pg], mate,
        )

    greet((mate, side))
    for pg in range(pages):
        mate_copy(pg).start()
        own_copy(pg).start()
        for copy in loads(pg):
            copy.start()
        p_load(0, pg).start()
    for copy in w_loads:
        copy.start()
    for hp in range(1, pairs):
        for pg in range(pages):
            p_load(hp, pg).start()
    for e in range(2):
        box_t[e] = jnp.zeros_like(box_t[e])
        box_t[e, :, e * head : (e + 1) * head] = box_w[...].astype(f32).T.astype(low)
    g_box[...] = jnp.zeros_like(g_box)
    for pg in range(pages):
        for copy in loads(pg):
            copy.wait()
        x_t[:, pg * keys : (pg + 1) * keys] = x[pg].reshape(keys, width).T
        own_copy(pg).wait()
        mate_copy(pg).wait_recv()

    @pl.loop(0, pairs)
    def _(hp):
        lanes = pl.ds(pl.multiple_of(hp * LANES, LANES), LANES)

        @pl.loop(0, pages)
        def _(pg):
            p_load(hp, pg).wait()
            both = sc[pg]
            cosine2, sine2 = turned(both)
            flat = both.T
            sine_t, cosine_t = flat[:head, :chip], flat[head:, :chip]
            basis = both.astype(low)
            basis_t = flat.astype(low)
            q_pair, k_pair, v_pair = q[pg, hp], k[pg, hp], v[pg, hp]
            q_t, k_t = q_pair.T, k_pair.T
            dc = dctx[pg, :, :, lanes].reshape(chip, LANES)
            left = lane_halves((chip, LANES))
            zero = jnp.zeros_like(dc)
            dk, dv, dqs = 0.0, 0.0, []
            for e in range(2):
                mine = left if e == 0 else jnp.logical_not(left)
                own_rows = slice(e * head, (e + 1) * head)
                p = probs[pg, hp, e]
                dc_own = jnp.where(mine, dc, zero)
                q_own = jnp.where(mine, q_pair, zero)
                dp = dot_nt(v_pair, dc_own)
                p_wide = p.astype(f32)
                delta = jnp.sum(p_wide * dp, axis=0, keepdims=True)
                ds = (p_wide * (dp - delta)).astype(low)
                dv = dv + dot(p, dc_own)
                dk_feat = dot(ds, jnp.concatenate([q_own, basis[:chip]], 1)) * scale
                dq_feat = dot(jnp.concatenate([k_t[own_rows], basis_t], 0), ds) * scale
                dk_proj = rotate_key(dk_feat[:, LANES:], cosine2, sine2).astype(low)
                a, b = dq_feat[head : 2 * head], dq_feat[2 * head :]
                dq_proj = jnp.concatenate(
                    [a * cosine_t - b * sine_t, a * sine_t + b * cosine_t], 0
                ).astype(low)
                dk = dk + dk_feat[:, :LANES] + dot(dk_proj, box_t[e])
                dqs.append(dq_feat[:head] + dot(box_w[...], dq_proj))
                g_box[...] += dot(k_t[own_rows], dk_proj) + dot_nt(q_t[own_rows], dq_proj)
            at = pl.ds(pl.multiple_of(pg * keys, LANES), keys)
            at_q = pl.ds(pl.multiple_of(pg * chip, LANES), chip)
            dq[hp, at_q] = jnp.concatenate(dqs, 0).T.astype(low)
            dkv[hp, at, :LANES] = dk.astype(low)
            dkv[hp, at, LANES:] = dv.astype(low)

        dkv_all = dkv[hp]
        dq_all = dq[hp]
        g_kv = column_sum(dkv_all.astype(f32))
        g_bias[0:1, lanes] = column_sum(dq_all.astype(f32))
        g_bias[1:2, lanes] = g_kv[:, :LANES]
        g_bias[2:3, lanes] = g_kv[:, LANES:]
        grad = dot(x_t[...], dkv_all).astype(low)
        x_q = jnp.concatenate([x_t[:, pg * keys : pg * keys + chip] for pg in range(pages)], 1)
        grad_q = dot(x_q, dq_all).astype(low)
        shard = width // 8
        packed[hp, :, :shard] = grad_q.reshape(8, shard, LANES)
        packed[hp, :, shard : 2 * shard] = grad[:, :LANES].reshape(8, shard, LANES)
        packed[hp, :, 2 * shard :] = grad[:, LANES:].reshape(8, shard, LANES)

    for copy in w_loads:
        copy.wait()

    def core_copy(pg, at):
        return remote(
            dx.at[pg, at, 1 - core], dx_mate.at[pg, at], core_send.at[pg, at], core_recv.at[pg, at],
            mate,
        )

    def side_copy(pg):
        return remote(dx.at[pg, 1, core], dx_side.at[pg], side_send.at[pg], side_recv.at[pg], side)

    @pl.loop(0, pages)
    def _(pg):
        for at in (1, 0):
            rows = pl.ds(pl.multiple_of(pg * keys + at * chip, LANES), chip)
            dks = jnp.concatenate([dkv[hp, rows, :LANES] for hp in range(pairs)], 1)
            dvs = jnp.concatenate([dkv[hp, rows, LANES:] for hp in range(pairs)], 1)
            total = dot_nt(dks, w_c[1]) + dot_nt(dvs, w_c[2])
            if at == 0:
                rows_q = pl.ds(pl.multiple_of(pg * chip, LANES), chip)
                dqs = jnp.concatenate([dq[hp, rows_q] for hp in range(pairs)], 1)
                total = total + dot_nt(dqs, w_c[0])
            dx[pg, at] = total.astype(low).reshape(2, block, width)
            core_copy(pg, at).start()

    @pl.loop(0, pages)
    def _(pg):
        core_copy(pg, 1).wait_recv()
        dx[pg, 1, core] = dx[pg, 1, core] + dx_mate[pg, 1]
        side_copy(pg).start()

    @pl.loop(0, pages)
    def _(pg):
        core_copy(pg, 0).wait_recv()
        side_copy(pg).wait_recv()
        total = dx[pg, 0, core].astype(f32) + dx_mate[pg, 0].astype(f32) + dx_side[pg].astype(f32)
        input_grad[pg] = (total + dresid1[pg]).astype(low)
        for at in range(2):
            core_copy(pg, at).wait_send()
        side_copy(pg).wait_send()
        mate_copy(pg).wait_send()


def attend_back(dctx, x, q, k, v, sc, probs, qkv_w, box_w, dresid1):
    pages, pairs, chip, _ = q.shape
    keys = k.shape[2]
    width = x.shape[-1]
    block = chip // 2
    half = pairs * LANES
    struct = jax.ShapeDtypeStruct
    vmem, dma = pltpu.VMEM, pltpu.SemaphoreType.DMA
    return pl.pallas_call(
        attend_back_kernel,
        out_shape=(
            struct((pages, block, width), low),
            struct((pairs, 8, 3 * width // 8, LANES), low),
            struct((8, half), f32),
            struct(box_w.shape, f32),
        ),
        in_specs=[any_spec()] * 8 + [vmem_spec()] * 2,
        out_specs=(vmem_spec(),) * 4,
        scratch_shapes=[
            vmem((pages, 4, block, width), low),
            vmem((pages, pairs, chip, LANES), low),
            vmem((pages, pairs, keys, LANES), low),
            vmem((pages, pairs, keys, LANES), low),
            vmem((pages, keys, LANES), f32),
            vmem((pages, pairs, 2, keys, chip), low),
            vmem((pages, 2, block, half), low),
            vmem((pairs, pages * chip, LANES), low),
            vmem((pairs, pages * keys, 2 * LANES), low),
            vmem((width, pages * keys), low),
            vmem((3, width, half), low),
            vmem((pages, 2, 2, block, width), low),
            vmem((pages, 2, block, width), low),
            vmem((pages, block, width), low),
            vmem((2, LANES, LANES), low),
            dma((pages, 5)), dma((pages, pairs)), dma((3,)), dma((pages,)), dma((pages,)), dma((pages,)),
            dma((pages, 2)), dma((pages, 2)), dma((pages,)), dma((pages,)),
        ],
        compiler_params=pltpu.CompilerParams(
            collective_id=2, has_side_effects=True, vmem_limit_bytes=60 * 2**20
        ),
        name="attend_back",
    )(dctx, x, q, k, v, sc, probs, qkv_w, box_w, dresid1)


def reduce_kernel(
    packed, small, packed_qkv, up_ref, down_ref, out_ref, qkv_ref, small_ref,
    held, from_core, got1, got2, got3, got_side, total, got_core,
    local_sem, small_sem, qkv_sem, core_send, core_recv, send1, recv1, send2, recv2, send3, recv3,
    side_send, side_recv, last_send, last_recv,
):
    page, blk = lax.axis_index("page"), lax.axis_index("blk")
    core = blk % 2
    mate = (page, core_of(blk))
    side = (page, side_of(blk))
    greet([(flip(page, way), blk) for way in range(3)] + [mate, side])
    wide = packed.shape[2]
    both = wide + SMALL_ROWS
    half = 3 * core

    def send(src, dst, sems, recv, to):
        copy = pltpu.make_async_remote_copy(
            src_ref=src, dst_ref=dst, send_sem=sems, recv_sem=recv, device_id=to,
            device_id_type=MESH,
        )
        copy.start()
        return copy

    codes = (6, 7, 4, 5, 2, 3, 0, 1)
    first, locals_ = {}, {}
    for code in codes:
        for order in range(3):
            shard = shard_at(page, order, code)
            other = 3 - half + order
            first[order, code] = (
                send(
                    packed.at[other, shard], from_core.at[order, code, :wide],
                    core_send.at[order, code, 0], core_recv.at[order, code, 0], mate,
                ),
                send(
                    small.at[other, shard], from_core.at[order, code, wide:],
                    core_send.at[order, code, 1], core_recv.at[order, code, 1], mate,
                ),
            )
            locals_[order, code] = (
                pltpu.make_async_copy(
                    packed.at[half + order, shard], held.at[order, code, :wide],
                    local_sem.at[order, code],
                ),
                pltpu.make_async_copy(
                    small.at[half + order, shard], held.at[order, code, wide:both],
                    small_sem.at[order, code],
                ),
                pltpu.make_async_copy(
                    packed_qkv.at[order, shard], held.at[order, code, both:],
                    qkv_sem.at[order, code],
                ),
            )
            for copy in locals_[order, code]:
                copy.start()
    sent = {}

    def partner(order, place):
        return (flip(page, ORDERS[order][place]), blk)

    for code in codes:
        for order in range(3):
            for copy in locals_[order, code]:
                copy.wait()
            for copy in first[order, code]:
                copy.wait_recv()
            held[order, code, :both] = held[order, code, :both] + from_core[order, code]
            if code >= 4:
                slot = code - 4
                sent[1, order, slot] = send(
                    held.at[order, code], got1.at[order, slot], send1.at[order, slot],
                    recv1.at[order, slot], partner(order, 0),
                )
    for slot in (2, 3, 0, 1):
        for order in range(3):
            sent[1, order, slot].wait_recv()
            held[order, slot] = held[order, slot] + got1[order, slot]
            if slot >= 2:
                sent[2, order, slot - 2] = send(
                    held.at[order, slot], got2.at[order, slot - 2], send2.at[order, slot - 2],
                    recv2.at[order, slot - 2], partner(order, 1),
                )
    for slot in (1, 0):
        for order in range(3):
            sent[2, order, slot].wait_recv()
            held[order, slot] = held[order, slot] + got2[order, slot]
            if slot == 1:
                sent[3, order] = send(
                    held.at[order, 1], got3.at[order], send3.at[order], recv3.at[order],
                    partner(order, 2),
                )
    for order in range(3):
        sent[3, order].wait_recv()
        held[order, 0] = held[order, 0] + got3[order]
        sent[4, order] = send(
            held.at[order, 0], got_side.at[order], side_send.at[order], side_recv.at[order], side
        )

    def write(part, order, which):
        rows = part[order].astype(jnp.float32)
        at = 0
        for piece in range(4):
            lanes = pl.ds(pl.multiple_of(which * 1536 + order * 512 + piece * LANES, LANES), LANES)
            up_ref[:, lanes] = rows[at : at + 96]
            at += 96
        lanes = pl.ds(pl.multiple_of(which * 384 + order * LANES, LANES), LANES)
        down_ref[:, lanes] = rows[at : at + 384]
        at += 384
        out_ref[:, lanes] = rows[at : at + 96]
        at += 96
        small_ref[pl.ds(which, 1), order] = rows[None, at : at + SMALL_ROWS]
        at += SMALL_ROWS
        for piece in range(3):
            lanes = pl.ds(pl.multiple_of(piece * 768 + which * 384 + order * LANES, LANES), LANES)
            qkv_ref[:, lanes] = rows[at : at + 96]
            at += 96

    for order in range(3):
        sent[4, order].wait_recv()
        total[order] = held[order, 0] + got_side[order]
        sent[5, order] = send(
            total.at[order], got_core.at[order], last_send.at[order], last_recv.at[order], mate
        )
        write(total, order, core)
    for order in range(3):
        sent[5, order].wait_recv()
        write(got_core, order, 1 - core)
    for copies in first.values():
        for copy in copies:
            copy.wait_send()
    for copy in sent.values():
        copy.wait_send()


def reduce_by_kernel(packed, packed_qkv, vectors):
    shards = lax.axis_size("page")
    small = jnp.concatenate([v.reshape(shards, -1) for v in vectors], axis=1).astype(low)
    width = small.shape[1]
    small = jnp.pad(small, ((0, 0), (0, 6 * SMALL_ROWS * LANES - width)))
    small = small.reshape(8, 6, SMALL_ROWS, LANES).transpose(1, 0, 2, 3)
    wide = packed.shape[2] + SMALL_ROWS
    rows = wide + packed_qkv.shape[2]
    struct = jax.ShapeDtypeStruct
    vmem, dma = pltpu.VMEM, pltpu.SemaphoreType.DMA
    up_s, down_s, out_s, qkv_s, small_s = pl.pallas_call(
        reduce_kernel,
        out_shape=(
            struct((96, 3072), f32),
            struct((384, 768), f32),
            struct((96, 768), f32),
            struct((96, 2304), f32),
            struct((2, 3, SMALL_ROWS, LANES), f32),
        ),
        in_specs=[any_spec()] * 3,
        out_specs=(vmem_spec(),) * 5,
        scratch_shapes=[
            vmem((3, 8, rows, LANES), low),
            vmem((3, 8, wide, LANES), low),
            vmem((3, 4, rows, LANES), low),
            vmem((3, 2, rows, LANES), low),
            vmem((3, rows, LANES), low),
            vmem((3, rows, LANES), low),
            vmem((3, rows, LANES), low),
            vmem((3, rows, LANES), low),
            dma((3, 8)), dma((3, 8)), dma((3, 8)), dma((3, 8, 2)), dma((3, 8, 2)),
            dma((3, 4)), dma((3, 4)),
            dma((3, 2)), dma((3, 2)),
            dma((3,)), dma((3,)),
            dma((3,)), dma((3,)),
            dma((3,)), dma((3,)),
        ],
        compiler_params=pltpu.CompilerParams(
            collective_id=3, has_side_effects=True, vmem_limit_bytes=56 * 2**20
        ),
        name="reduce_grads",
    )(packed, small, packed_qkv)
    flat = small_s.reshape(-1)
    sums, at = [], 0
    for vector in vectors:
        count = vector.shape[0] // shards
        sums.append(flat[at : at + count])
        at += count
    return (qkv_s, out_s, up_s, down_s), sums


def reduce_by_collectives(packed, packed_qkv, vectors):
    core = lax.axis_index("blk") % 2
    up = packed[:, :, :384].reshape(6, 8, 4, 96, LANES).transpose(1, 3, 0, 2, 4).reshape(768, 3072)
    down = packed[:, :, 384:768].transpose(1, 2, 0, 3).reshape(3072, 768)
    out = packed[:, :, 768:].transpose(1, 2, 0, 3).reshape(768, 768)
    own = packed_qkv.reshape(3, 8, 3, 96, LANES).transpose(1, 3, 2, 0, 4).reshape(768, 3, 384)
    qkv = jnp.zeros((768, 3, 2, 384), low)
    qkv = lax.dynamic_update_slice(qkv, own[:, :, None], (0, 0, core, 0)).reshape(768, 2304)
    grads = jax.tree.map(lambda g: g.astype(f32), (qkv, out, up, down, *vectors))
    page_sums = tuple(
        lax.psum_scatter(grad, "page", scatter_dimension=0, tiled=True) for grad in grads
    )
    sums = jax.tree.map(
        lambda part: part.astype(f32), lax.psum(jax.tree.map(lambda g: g.astype(low), page_sums), "blk")
    )
    return sums[:4], sums[4:]


def local(
    tokens, lengths, boxes, qkv_weight, qkv_bias, box_weight, out_weight, out_bias, norm1_gain,
    norm1_bias, up_weight, up_bias, down_weight, down_bias, norm2_gain, norm2_bias, cotangent,
):
    pages, block, width = tokens.shape
    rows = pages * block
    x, q, k, v, sc, probs, ctx = attend(tokens, boxes, lengths, qkv_weight, qkv_bias, box_weight)
    output, dresid1, dctx, packed, g_up_b, g_rows = feed(
        ctx.reshape(rows, width), tokens.reshape(rows, width), cotangent.reshape(rows, width),
        out_weight, up_weight, down_weight, out_bias, norm1_gain, norm1_bias, up_bias, down_bias,
        norm2_gain, norm2_bias,
    )
    input_grad, packed_qkv, g_bias, g_box = attend_back(
        dctx.reshape(pages, block, width), x, q, k, v, sc, probs, qkv_weight, box_weight,
        dresid1.reshape(pages, block, width),
    )
    core = lax.axis_index("blk") % 2
    own_bias = g_bias[:3].reshape(3, 1, width // 2)
    bias = lax.dynamic_update_slice(jnp.zeros((3, 2, width // 2), f32), own_bias, (0, core, 0))
    vectors = (
        bias.reshape(-1), g_box.reshape(-1), g_rows[5], g_rows[3], g_rows[4], g_up_b.reshape(-1),
        g_rows[2], g_rows[0], g_rows[1],
    )
    if lax.axis_size("page") == 8:
        weights, sums = reduce_by_kernel(packed, packed_qkv, vectors)
    else:
        weights, sums = reduce_by_collectives(packed, packed_qkv, vectors)
    qkv_w, out_w, up_w, down_w = weights
    qkv_b, box, out_b, gain1, shift1, up_b, down_b, gain2, shift2 = sums
    return (
        output.reshape(pages, block, width), input_grad, qkv_w, qkv_b, box, out_w, out_b, gain1,
        shift1, up_w, up_b, down_w, down_b, gain2, shift2,
    )


def solution(mesh):
    return jax.shard_map(
        local,
        mesh=mesh,
        in_specs=(
            P("page", "blk", None),
            P("page"),
            P("page", "blk", None),
            P(),
            P(),
            P(),
            P(),
            P(),
            P(),
            P(),
            P(),
            P(),
            P(),
            P(),
            P(),
            P(),
            P("page", "blk", None),
        ),
        out_specs=(
            P("page", "blk", None),
            P("page", "blk", None),
            P("page", None),
            P("page"),
            P("page"),
            P("page", None),
            P("page"),
            P("page"),
            P("page"),
            P("page", None),
            P("page"),
            P("page", None),
            P("page"),
            P("page"),
            P("page"),
        ),
        check_vma=False,
    )
```

```python
import functools

import jax
import jax.numpy as jnp
import numpy as np
from jax import lax
from jax.experimental import pallas as pl
from jax.experimental.pallas import tpu as pltpu
from jax.sharding import PartitionSpec as P

norm_eps = 1e-12
MESH = pl.DeviceIdType.MESH
LANES = 128
low = jnp.bfloat16
f32 = jnp.float32


def core_of(blk):
    return blk + 1 - 2 * (blk % 2)


def side_of(blk):
    return (blk + 2) % 4


def greet(others):
    barrier = pltpu.get_barrier_semaphore()
    for other in others:
        pl.semaphore_signal(barrier, inc=1, device_id=other, device_id_type=MESH)
    pl.semaphore_wait(barrier, len(others))


def remote(src, dst, send_sem, recv_sem, to):
    return pltpu.make_async_remote_copy(
        src_ref=src, dst_ref=dst, send_sem=send_sem, recv_sem=recv_sem, device_id=to,
        device_id_type=MESH,
    )


def dot(a, b):
    return jnp.dot(a, b, preferred_element_type=f32)


def dot_nt(a, b):
    return lax.dot_general(a, b, (((1,), (1,)), ((), ())), preferred_element_type=f32)


def dot_tn(a, b):
    return lax.dot_general(a, b, (((0,), (0,)), ((), ())), preferred_element_type=f32)


def sin_cos(theta):
    turns = jnp.floor(theta * 0.6366197723675814 + 0.5)
    rest = theta - turns * 1.5703125
    rest = rest - turns * 4.837512969970703125e-4
    rest = rest - turns * 7.54978995489188216e-8
    square = rest * rest
    sine = ((-1.9515295891e-4 * square + 8.3321608736e-3) * square - 1.6666654611e-1) * square
    sine = sine * rest + rest
    cosine = (2.443315711809948e-5 * square - 1.388731625493765e-3) * square + 4.166664568298827e-2
    cosine = cosine * square * square - 0.5 * square + 1.0
    quarter = turns.astype(jnp.int32)
    odd = (quarter & 1) == 1
    sine_at = jnp.where(odd, cosine, sine)
    cosine_at = jnp.where(odd, sine, cosine)
    sine_at = jnp.where((quarter & 2) == 2, -sine_at, sine_at)
    cosine_at = jnp.where(((quarter + 1) & 2) == 2, -cosine_at, cosine_at)
    return sine_at, cosine_at


def lane_halves(shape):
    return lax.broadcasted_iota(jnp.int32, shape, 1) < LANES // 2


def turned(both):
    swapped = pltpu.roll(both, LANES // 2, 1)
    left = lane_halves(both.shape)
    return jnp.where(left, -swapped, both), jnp.where(left, both, swapped)


def rotate_key(proj, cosine2, sine2):
    return proj * cosine2 + pltpu.roll(proj, LANES // 2, 1) * sine2


def attend_kernel(
    tokens, boxes, lengths, freq, qkv_w, qkv_b, box2,
    x_out, q_out, k_out, v_out, sc_out, p_out, ctx_out,
    x, box, w_q, w_kv, q, k, v, sc, probs, ctx,
    own_sem, w_sem, out_sem, p_sem, ctx_sem,
    mate_send, mate_recv, side_send, side_recv, pass_send, pass_recv, ctx_send, ctx_recv,
):
    page, blk = lax.axis_index("page"), lax.axis_index("blk")
    core, side_at = blk % 2, blk // 2
    mate, side = (page, core_of(blk)), (page, side_of(blk))
    pages = tokens.shape[0]
    half = w_q.shape[1]
    pairs = half // LANES
    chip = 2 * tokens.shape[1]
    keys = 2 * chip
    scale = 0.125

    def of_half(part):
        return pl.ds(pl.multiple_of(part * 2 * half + core * half, LANES), half)

    loads = [
        pltpu.make_async_copy(qkv_w.at[:, of_half(0)], w_q, w_sem.at[0]),
        pltpu.make_async_copy(qkv_w.at[:, of_half(1)], w_kv.at[:, :half], w_sem.at[1]),
        pltpu.make_async_copy(qkv_w.at[:, of_half(2)], w_kv.at[:, half:], w_sem.at[2]),
    ]
    own = []
    for pg in range(pages):
        own.append(pltpu.make_async_copy(tokens.at[pg], x.at[pg, core], own_sem.at[pg, 0]))
        own.append(pltpu.make_async_copy(boxes.at[pg], box.at[pg, core], own_sem.at[pg, 1]))
    for copy in own:
        copy.start()
    for copy in loads:
        copy.start()
    greet((mate, side))
    to_mate, to_side = [], []
    for pg in range(pages):
        for which, (src, dst) in enumerate(((tokens, x), (boxes, box))):
            to_side.append(
                remote(src.at[pg], dst.at[pg, 2 + core], side_send.at[pg, which], side_recv.at[pg, which], side)
            )
            to_side[-1].start()
            to_mate.append(
                remote(src.at[pg], dst.at[pg, core], mate_send.at[pg, which], mate_recv.at[pg, which], mate)
            )
            to_mate[-1].start()
    for copy in loads:
        copy.wait()

    @pl.loop(0, pages)
    def _(pg):
        passed = []
        for which, (src, dst) in enumerate(((tokens, x), (boxes, box))):
            remote(
                src.at[pg], dst.at[pg, 2 + core], side_send.at[pg, which], side_recv.at[pg, which], side
            ).wait_recv()
            copy = remote(
                dst.at[pg, 2 + core], dst.at[pg, 2 + core], pass_send.at[pg, which],
                pass_recv.at[pg, which], mate,
            )
            copy.start()
            passed.append(copy)
            pltpu.make_async_copy(src.at[pg], dst.at[pg, core], own_sem.at[pg, which]).wait()
            remote(
                src.at[pg], dst.at[pg, core], mate_send.at[pg, which], mate_recv.at[pg, which], mate
            ).wait_recv()
        for copy in passed:
            copy.wait_recv()
        pltpu.make_async_copy(x.at[pg], x_out.at[pg], out_sem.at[pg, 0]).start()
        for at in range(4):
            rows = box[pg, at]
            spread = [
                jnp.broadcast_to(rows[c : c + 1], (freq.shape[0] // 4, LANES)) for c in range(4)
            ]
            sine, cosine = sin_cos(jnp.concatenate(spread, 0) * freq[...])
            sc[pg, at * LANES : (at + 1) * LANES] = jnp.concatenate([sine, cosine], 0).T
        pltpu.make_async_copy(sc.at[pg], sc_out.at[pg], out_sem.at[pg, 1]).start()
        x_all = x[pg].reshape(keys, x.shape[-1])
        q_all = (dot(x_all[:chip], w_q[...]) + qkv_b[:, of_half(0)]).astype(low)
        bias = jnp.concatenate([qkv_b[:, of_half(1)], qkv_b[:, of_half(2)]], 1)
        kv_all = (dot(x_all, w_kv[...]) + bias).astype(low)
        for hp in range(pairs):
            q[pg, hp] = q_all[:, hp * LANES : (hp + 1) * LANES]
            k[pg, hp] = kv_all[:, hp * LANES : (hp + 1) * LANES]
            v[pg, hp] = kv_all[:, half + hp * LANES : half + (hp + 1) * LANES]
        for which, (src, dst) in enumerate(((q, q_out), (k, k_out), (v, v_out))):
            pltpu.make_async_copy(src.at[pg], dst.at[pg], out_sem.at[pg, 2 + which]).start()
        place = lax.broadcasted_iota(jnp.int32, (keys, chip), 0) + side_at * chip
        place = jnp.where(place >= keys, place - keys, place)
        valid = place < lengths[pg]

        @pl.loop(0, pairs)
        def _(hp):
            both = sc[pg]
            cosine2, sine2 = turned(both)
            basis = both.astype(low)
            basis_q = (both[:chip] * scale).astype(low)
            left = lane_halves((chip, LANES))
            cosine_q = jnp.where(left, -cosine2[:chip], cosine2[:chip]) * scale
            sine_q = jnp.where(left, sine2[:chip], -sine2[:chip]) * scale
            q_pair, k_pair = q[pg, hp], k[pg, hp]
            q_proj = dot(q_pair, box2[...])
            k_proj = dot(k_pair, box2[...])
            v_t = v[pg, hp].T
            outs = []
            for e in range(2):
                at = slice(e * LANES, (e + 1) * LANES)
                q_pos = rotate_key(q_proj[:, at], cosine_q, sine_q).astype(low)
                k_pos = rotate_key(k_proj[:, at], cosine2, sine2).astype(low)
                mine = left if e == 0 else jnp.logical_not(left)
                q_own = jnp.where(mine, q_pair.astype(f32) * scale, 0.0).astype(low)
                scores = dot_nt(
                    jnp.concatenate([basis, k_pos], 1), jnp.concatenate([q_pos, basis_q], 1)
                )
                scores = scores + dot_nt(k_pair, q_own)
                scores = jnp.where(valid, scores, -1e30)
                top = jnp.max(scores, axis=0, keepdims=True)
                grown = jnp.exp(scores - top)
                total = jnp.sum(grown, axis=0, keepdims=True)
                p = (grown * (1.0 / total)).astype(low)
                probs[pg, hp, e] = p
                outs.append(dot(v_t[e * LANES // 2 : (e + 1) * LANES // 2], p))
            pltpu.make_async_copy(probs.at[pg, hp], p_out.at[pg, hp], p_sem.at[pg, hp]).start()
            context = jnp.concatenate(outs, 0).T.astype(low)
            lanes = pl.ds(pl.multiple_of(hp * LANES, LANES), LANES)
            ctx[pg, 0, :, lanes] = context[: chip // 2]
            ctx[pg, 1, :, lanes] = context[chip // 2 :]

        mine = pl.ds(pl.multiple_of(core * half, LANES), half)
        pltpu.make_async_copy(ctx.at[pg, core], ctx_out.at[pg, :, mine], ctx_sem.at[pg]).start()
        remote(
            ctx.at[pg, 1 - core], ctx_out.at[pg, :, mine], ctx_send.at[pg], ctx_recv.at[pg], mate
        ).start()
        for copy in passed:
            copy.wait_send()

    mine = pl.ds(pl.multiple_of(core * half, LANES), half)
    for pg in range(pages):
        for which, (src, dst) in enumerate(((x, x_out), (sc, sc_out), (q, q_out), (k, k_out), (v, v_out))):
            pltpu.make_async_copy(src.at[pg], dst.at[pg], out_sem.at[pg, which]).wait()
        for hp in range(pairs):
            pltpu.make_async_copy(probs.at[pg, hp], p_out.at[pg, hp], p_sem.at[pg, hp]).wait()
        pltpu.make_async_copy(ctx.at[pg, core], ctx_out.at[pg, :, mine], ctx_sem.at[pg]).wait()
        remote(
            ctx.at[pg, 1 - core], ctx_out.at[pg, :, mine], ctx_send.at[pg], ctx_recv.at[pg], mate
        ).wait()
    for copy in to_side + to_mate:
        copy.wait_send()


def any_spec():
    return pl.BlockSpec(memory_space=pl.ANY)


def vmem_spec():
    return pl.BlockSpec(memory_space=pltpu.VMEM)


def attend(tokens, boxes, lengths, qkv_w, qkv_b, box_weight):
    pages, block, width = tokens.shape
    head_dim, pos = box_weight.shape
    half = width // 2
    pairs = half // LANES
    chip, keys = 2 * block, 4 * block
    count = pos // 8
    freqs = 10000.0 ** (-np.arange(count) / count)
    freq = jnp.asarray(np.tile(np.tile(freqs, 4)[:, None], (1, LANES)), f32)
    boxes_t = jnp.pad(boxes.astype(f32).transpose(0, 2, 1), ((0, 0), (0, 4), (0, 0)))
    zero = jnp.zeros_like(box_weight)
    box2 = jnp.concatenate(
        [jnp.concatenate([box_weight, zero], 1), jnp.concatenate([zero, box_weight], 1)], 0
    )
    struct = jax.ShapeDtypeStruct
    vmem, dma = pltpu.VMEM, pltpu.SemaphoreType.DMA
    return pl.pallas_call(
        attend_kernel,
        out_shape=(
            struct((pages, 4, block, width), low),
            struct((pages, pairs, chip, LANES), low),
            struct((pages, pairs, keys, LANES), low),
            struct((pages, pairs, keys, LANES), low),
            struct((pages, keys, LANES), f32),
            struct((pages, pairs, 2, keys, chip), low),
            struct((pages, block, width), low),
        ),
        in_specs=[any_spec(), any_spec(), pl.BlockSpec(memory_space=pltpu.SMEM), vmem_spec(), any_spec(), vmem_spec(), vmem_spec()],
        out_specs=(any_spec(),) * 7,
        scratch_shapes=[
            vmem((pages, 4, block, width), low),
            vmem((pages, 4, 8, LANES), f32),
            vmem((width, half), low),
            vmem((width, 2 * half), low),
            vmem((pages, pairs, chip, LANES), low),
            vmem((pages, pairs, keys, LANES), low),
            vmem((pages, pairs, keys, LANES), low),
            vmem((pages, keys, LANES), f32),
            vmem((pages, pairs, 2, keys, chip), low),
            vmem((pages, 2, block, half), low),
            dma((pages, 2)), dma((3,)), dma((pages, 5)), dma((pages, pairs)), dma((pages,)),
            dma((pages, 2)), dma((pages, 2)), dma((pages, 2)), dma((pages, 2)),
            dma((pages, 2)), dma((pages, 2)), dma((pages,)), dma((pages,)),
        ],
        compiler_params=pltpu.CompilerParams(
            collective_id=1, has_side_effects=True, vmem_limit_bytes=56 * 2**20
        ),
        name="attend",
    )(tokens, boxes_t, lengths, freq, qkv_w, qkv_b.reshape(1, -1), box2)


def norm_of(resid):
    center = resid - jnp.mean(resid, axis=-1, keepdims=True)
    spread = jnp.mean(center * center, axis=-1, keepdims=True)
    inverse = lax.rsqrt(spread + norm_eps)
    return center * inverse, inverse


def norm_back(grad, normed, inverse):
    mean = jnp.mean(grad, axis=-1, keepdims=True)
    along = jnp.mean(grad * normed, axis=-1, keepdims=True)
    return inverse * (grad - mean - normed * along)


def column_sum(values):
    return jnp.sum(values, axis=0, keepdims=True)


def feed_kernel(
    ctx, tokens, cotangent, out_w, up_w, down_w, out_b, gain1, shift1, up_b, down_b, gain2, shift2,
    output, dresid1, dctx, packed, g_rows,
    w_out, w_up, w_down, act, slope, norm1, inverse1, hidden, hidden_t, grow, staged, w_sem, up_sem, down_sem, pack_sem,
):
    chunks, chunk = w_up.shape[0], w_up.shape[2]
    width = ctx.shape[1]
    up_pieces = chunk // LANES
    shard = width // 8
    out_load = pltpu.make_async_copy(out_w, w_out, w_sem)
    out_load.start()

    def up_load(j):
        return pltpu.make_async_copy(
            up_w.at[:, pl.ds(pl.multiple_of(j * chunk, LANES), chunk)], w_up.at[j], up_sem.at[j]
        )

    def down_load(j):
        return pltpu.make_async_copy(
            down_w.at[pl.ds(pl.multiple_of(j * chunk, LANES), chunk)], w_down.at[j], down_sem.at[j]
        )

    for j in range(chunks):
        up_load(j).start()
        down_load(j).start()
    g_rows[...] = jnp.zeros_like(g_rows)
    out_load.wait()
    resid = tokens[...].astype(f32) + dot(ctx[...], w_out[...]) + out_b[...]
    normed, inverse = norm_of(resid)
    norm1[...] = normed
    inverse1[...] = jnp.broadcast_to(inverse, inverse1.shape)
    first = normed * gain1[...] + shift1[...]
    hidden[...] = first.astype(low)
    hidden_t[...] = first.astype(low).T
    grow[...] = first + down_b[...]

    @pl.loop(0, chunks)
    def _(j):
        up_load(j).wait()
        upper = dot(hidden[...], w_up[j]) + up_b[pl.ds(j, 1)]
        cdf = 0.5 + 0.5 * lax.erf(upper * 0.7071067811865476)
        act_low = (upper * cdf).astype(low)
        act[j] = act_low
        slope[j] = cdf + upper * (jnp.exp(upper * upper * -0.5) * 0.3989422804014327)
        down_load(j).wait()
        grow[...] += dot(act_low, w_down[j])

    normed2, inverse2 = norm_of(grow[...])
    output[...] = (normed2 * gain2[...] + shift2[...]).astype(low)
    cot = cotangent[...].astype(f32)
    g_rows[0:1] = column_sum(cot * normed2)
    g_rows[1:2] = column_sum(cot)
    dresid2 = norm_back(cot * gain2[...], normed2, inverse2)
    dffn = dresid2.astype(low)
    g_rows[2:3] = column_sum(dffn.astype(f32))
    grow[...] = dresid2
    staged[...] = dffn

    @pl.loop(0, chunks)
    def _(j):
        dffn = staged[...]
        dupper = (dot_nt(dffn, w_down[j]) * slope[j]).astype(low)
        g_rows[pl.ds(8 + j, 1), :chunk] = column_sum(dupper.astype(f32))
        grow[...] += dot_nt(dupper, w_up[j])
        grad_up = dot(hidden_t[...], dupper).astype(low)
        for piece in range(up_pieces):
            part = grad_up[:, piece * LANES : (piece + 1) * LANES].reshape(8, shard, LANES)
            packed[j, :, piece * shard : (piece + 1) * shard] = part
        grad_down = dot_tn(act[j], dffn).astype(low)
        for piece in range(up_pieces):
            row = j * up_pieces + piece
            per = up_pieces * chunks // 8
            at = pl.ds(pl.multiple_of(up_pieces * shard + (row % per) * LANES, LANES), LANES)
            for column in range(6):
                packed[column, row // per, at] = grad_down[
                    piece * LANES : (piece + 1) * LANES, column * LANES : (column + 1) * LANES
                ]

    dhidden = grow[...]
    normed = norm1[...]
    g_rows[3:4] = column_sum(dhidden * normed)
    g_rows[4:5] = column_sum(dhidden)
    back = norm_back(dhidden * gain1[...], normed, inverse1[:, :1])
    dresid1[...] = back
    dattn = back.astype(low)
    g_rows[5:6] = column_sum(dattn.astype(f32))
    dctx[...] = dot_nt(dattn, w_out[...]).astype(low)
    grad_out = dot_tn(ctx[...], dattn).astype(low)
    first_row = packed.shape[2] - shard
    for column in range(6):
        part = grad_out[:, column * LANES : (column + 1) * LANES].reshape(8, shard, LANES)
        packed[column, :, first_row:] = part


def feed(ctx, tokens, cotangent, out_w, up_w, down_w, out_b, gain1, shift1, up_b, down_b, gain2, shift2):
    rows, width = ctx.shape
    hidden_width = up_w.shape[1]
    chunks = 6
    chunk = hidden_width // chunks
    shard = width // 8
    packed_rows = (chunk // LANES) * shard + hidden_width // 8 + shard
    struct = jax.ShapeDtypeStruct
    vmem, dma = pltpu.VMEM, pltpu.SemaphoreType.DMA

    def row(vector):
        return vector.reshape(1, -1)

    return pl.pallas_call(
        feed_kernel,
        out_shape=(
            struct((rows, width), low),
            struct((rows, width), f32),
            struct((rows, width), low),
            struct((6, 8, packed_rows, LANES), low),
            struct((16, width), f32),
        ),
        in_specs=[vmem_spec()] * 3 + [any_spec()] * 3 + [vmem_spec()] * 7,
        out_specs=(vmem_spec(),) * 5,
        scratch_shapes=[
            vmem((width, width), low),
            vmem((chunks, width, chunk), low),
            vmem((chunks, chunk, width), low),
            vmem((chunks, rows, chunk), low),
            vmem((chunks, rows, chunk), f32),
            vmem((rows, width), f32),
            vmem((rows, LANES), f32),
            vmem((rows, width), low),
            vmem((width, rows), low),
            vmem((rows, width), f32),
            vmem((rows, width), low),
            dma, dma((chunks,)), dma((chunks,)), dma,
        ],
        compiler_params=pltpu.CompilerParams(vmem_limit_bytes=60 * 2**20),
        name="feed",
    )(
        ctx, tokens, cotangent, out_w, up_w, down_w, row(out_b), row(gain1), row(shift1),
        up_b.reshape(chunks, chunk), row(down_b), row(gain2), row(shift2),
    )


ORDERS = ("xaym", "ayxm", "yxam")
GROUPS = ((12, 16), (8, 12), (6, 8), (4, 6), (2, 4), (1, 2))


def flip(page, way):
    x, z = page % 2, page // 2
    if way == "x":
        return z * 2 + (1 - x)
    if way == "a":
        return (z + 1 - 2 * (z % 2)) * 2 + x
    return ((z + 2) % 4) * 2 + x


class Ways:
    def __init__(self):
        self.page, self.blk = lax.axis_index("page"), lax.axis_index("blk")
        self.core, self.half = self.blk % 2, self.blk // 2
        self.mate, self.side = (self.page, core_of(self.blk)), (self.page, side_of(self.blk))

    def partner(self, way):
        return self.side if way == "y" else (flip(self.page, way), self.blk)

    def piece(self, order, code):
        page, half = self.page, self.half
        for place, way in enumerate(ORDERS[order]):
            if code >> (3 - place) & 1:
                if way == "y":
                    half = 1 - half
                else:
                    page = flip(page, way)
        return page, half

    def everyone(self):
        return [self.partner(way) for way in "xamy"] + [self.mate]


def step_of(code):
    return 4 - code.bit_length()


class EarlySum:
    def __init__(self, ways, packed, held, mates, got, final, sems):
        self.ways, self.packed, self.held, self.mates, self.got, self.final = ways, packed, held, mates, got, final
        (self.own_sem, self.core_send, self.core_recv, self.send_sem, self.recv_sem, self.last_send,
         self.last_recv, self.end_send, self.end_recv) = sems
        self.rows = held.shape[2]

    def slices(self):
        return ((12, 16), (8, 12), (4, 8), (0, 4))

    def start(self):
        ways = self.ways
        for at, (begin, end) in enumerate(self.slices()):
            for code in range(begin, end):
                for order in range(3):
                    page, half = ways.piece(order, code)
                    rows = pl.ds(pl.multiple_of(half * self.rows, 16), self.rows)
                    remote(
                        self.packed.at[3 - 3 * ways.core + order, page, rows],
                        self.mates.at[order, code], self.core_send.at[order, at],
                        self.core_recv.at[order, at], ways.mate,
                    ).start()
                    pltpu.make_async_copy(
                        self.packed.at[3 * ways.core + order, page, rows], self.held.at[order, code],
                        self.own_sem.at[order, at],
                    ).start()

    def core_group(self, order, at):
        begin, end = self.slices()[at]
        part = self.mates.at[order, begin:end]
        return remote(part, part, self.core_send.at[order, at], self.core_recv.at[order, at], self.ways.mate)

    def own_group(self, order, at):
        begin, end = self.slices()[at]
        part = self.held.at[order, begin:end]
        return pltpu.make_async_copy(part, part, self.own_sem.at[order, at])

    def add_core(self, at):
        begin, end = self.slices()[at]
        for order in range(3):
            self.own_group(order, at).wait()
            self.core_group(order, at).wait_recv()
            self.held[order, begin:end] = self.held[order, begin:end] + self.mates[order, begin:end]

    def copy(self, order, group):
        begin, end = GROUPS[group]
        way = ORDERS[order][step_of(begin)]
        return remote(
            self.held.at[order, begin:end], self.got.at[order, begin - 1 : end - 1],
            self.send_sem.at[order, group], self.recv_sem.at[order, group], self.ways.partner(way),
        )

    def send(self, group):
        for order in range(3):
            self.copy(order, group).start()

    def receive(self, group):
        begin, end = GROUPS[group]
        base = 1 << (begin.bit_length() - 1)
        for order in range(3):
            self.copy(order, group).wait_recv()
            to = slice(begin - base, end - base)
            self.held[order, to] = self.held[order, to] + self.got[order, begin - 1 : end - 1]

    def last_copy(self, order):
        part = self.final.at[self.ways.core, order, self.ways.half]
        return remote(part, part, self.last_send.at[order], self.last_recv.at[order], self.ways.side)

    def end_copy(self, order):
        part = self.final.at[self.ways.core, order]
        return remote(part, part, self.end_send.at[order], self.end_recv.at[order], self.ways.mate)

    def share(self):
        for order in range(3):
            self.copy(order, 5).wait_recv()
            self.final[self.ways.core, order, self.ways.half] = self.held[order, 0] + self.got[order, 0]
            self.last_copy(order).start()

    def hand_over(self):
        for order in range(3):
            self.last_copy(order).wait_recv()
            self.end_copy(order).start()

    def finish(self):
        for order in range(3):
            self.end_copy(order).wait()
            self.last_copy(order).wait_send()
            for at in range(4):
                self.core_group(order, at).wait_send()
            for group in range(len(GROUPS)):
                self.copy(order, group).wait_send()


class LateSum:
    def __init__(self, ways, hp, packed, held, got, final, sems):
        self.ways, self.hp = ways, hp
        self.packed, self.held, self.got, self.final = packed, held, got, final
        (self.first_send, self.first_recv, self.send_sem, self.recv_sem, self.last_send, self.last_recv,
         self.end_send, self.end_recv) = sems
        self.rows = held.shape[3]

    def start(self):
        ways, hp = self.ways, self.hp
        for code in range(8, 16):
            for order in range(3):
                page, half = ways.piece(order, code)
                rows = pl.ds(pl.multiple_of(half * self.rows, 16), self.rows)
                remote(
                    self.packed.at[hp, order, page, rows], self.got.at[hp, order, code - 1],
                    self.first_send.at[hp, order], self.first_recv.at[hp, order],
                    ways.partner(ORDERS[order][0]),
                ).start()

    def first(self, order):
        part = self.got.at[self.hp, order, 7:15]
        return remote(
            part, part, self.first_send.at[self.hp, order], self.first_recv.at[self.hp, order],
            self.ways.partner(ORDERS[order][0]),
        )

    def copy(self, order, step):
        begin, end = 8 >> step, 16 >> step
        return remote(
            self.held.at[self.hp, order, begin:end], self.got.at[self.hp, order, begin - 1 : end - 1],
            self.send_sem.at[self.hp, order, step - 1], self.recv_sem.at[self.hp, order, step - 1],
            self.ways.partner(ORDERS[order][step]),
        )

    def advance(self, step):
        ways, hp = self.ways, self.hp
        for order in range(3):
            if step == 0:
                self.first(order).wait_recv()
                for code in (4, 5, 6, 7, 0, 1, 2, 3):
                    page, half = ways.piece(order, code)
                    rows = pl.ds(pl.multiple_of(half * self.rows, 16), self.rows)
                    self.held[hp, order, code] = self.packed[hp, order, page, rows] + self.got[hp, order, code + 7]
                    if code == 7:
                        self.copy(order, 1).start()
            elif step < 3:
                self.copy(order, step).wait_recv()
                count = 8 >> step
                self.held[hp, order, :count] = (
                    self.held[hp, order, :count] + self.got[hp, order, count - 1 : 2 * count - 1]
                )
                self.copy(order, step + 1).start()
            elif step == 3:
                self.copy(order, 3).wait_recv()
                self.final[ways.core, hp, order, ways.half] = self.held[hp, order, 0] + self.got[hp, order, 0]
                self.last_copy(order).start()
            else:
                self.last_copy(order).wait_recv()
                self.end_copy(order).start()

    def last_copy(self, order):
        part = self.final.at[self.ways.core, self.hp, order, self.ways.half]
        return remote(
            part, part, self.last_send.at[self.hp, order], self.last_recv.at[self.hp, order], self.ways.side
        )

    def end_copy(self, order):
        part = self.final.at[self.ways.core, self.hp, order]
        return remote(
            part, part, self.end_send.at[self.hp, order], self.end_recv.at[self.hp, order], self.ways.mate
        )

    def finish(self):
        for order in range(3):
            self.end_copy(order).wait()
            self.last_copy(order).wait_send()
            self.first(order).wait_send()
            for step in (1, 2, 3):
                self.copy(order, step).wait_send()


class SmallSum:
    def __init__(self, ways, value, got, sems):
        self.ways, self.value, self.got = ways, value, got
        self.send_sem, self.recv_sem = sems
        self.to = ways.everyone()

    def copy(self, step):
        return remote(
            self.value.at[step], self.got.at[step], self.send_sem.at[step], self.recv_sem.at[step], self.to[step]
        )

    def start(self):
        self.copy(0).start()

    def advance(self, step):
        self.copy(step).wait_recv()
        self.value[step + 1] = self.value[step] + self.got[step]
        if step < 4:
            self.copy(step + 1).start()

    def finish(self):
        for step in range(5):
            self.copy(step).wait_send()


def attend_back_kernel(
    summed, dctx_own, x_in, q_in, k_in, v_in, sc_in, p_in, qkv_w, box_w, dresid1, *refs
):
    if summed:
        (
            early_in, small_in,
            dx_out, early_out, late_out, small_out, tiny_out,
            x, q, k, v, sc, probs, dctx, dq, dkv, x_t, w_c, dx, dx_mate, dx_side, box_t, g_box, g_bias, late_packed,
            in_sem, p_sem, w_sem, own_sem, mate_send, mate_recv, core_send, core_recv, side_send, side_recv,
            early_held, early_mates, early_got, late_held, late_got, small_value, small_got, tiny_value, tiny_got,
            *sems,
        ) = refs
        early_sems, late_sems, small_sems, tiny_sems = sems[:9], sems[9:17], sems[17:19], sems[19:21]
    else:
        (
            dx_out, late_packed, tiny_out,
            x, q, k, v, sc, probs, dctx, dq, dkv, x_t, w_c, dx, dx_mate, dx_side, box_t, g_box, g_bias,
            in_sem, p_sem, w_sem, own_sem, mate_send, mate_recv, core_send, core_recv, side_send, side_recv,
        ) = refs
    ways = Ways()
    core, mate, side = ways.core, ways.mate, ways.side
    pages, pairs, chip, _ = q.shape
    keys = k.shape[2]
    block = chip // 2
    half = pairs * LANES
    width = x.shape[-1]
    shard = width // 8
    head = LANES // 2
    scale = 0.125

    def of_half(part, which):
        return pl.ds(pl.multiple_of(part * 2 * half + which * half, LANES), half)

    def loads(pg):
        names = ((x_in, x), (q_in, q), (k_in, k), (v_in, v), (sc_in, sc))
        return [
            pltpu.make_async_copy(src.at[pg], dst.at[pg], in_sem.at[pg, at])
            for at, (src, dst) in enumerate(names)
        ]

    def p_load(hp, pg):
        return pltpu.make_async_copy(p_in.at[pg, hp], probs.at[pg, hp], p_sem.at[pg, hp])

    w_loads = [
        pltpu.make_async_copy(qkv_w.at[:, of_half(part, core)], w_c.at[part], w_sem.at[part])
        for part in range(3)
    ]

    def own_copy(pg):
        return pltpu.make_async_copy(
            dctx_own.at[pg, :, of_half(0, core)], dctx.at[pg, core], own_sem.at[pg]
        )

    def mate_copy(pg):
        return remote(
            dctx_own.at[pg, :, of_half(0, 1 - core)], dctx.at[pg, core], mate_send.at[pg],
            mate_recv.at[pg], mate,
        )

    greet(ways.everyone() if summed else [mate, side])
    mate_copy(0).start()
    own_copy(0).start()
    for copy in loads(0):
        copy.start()
    p_load(0, 0).start()
    if summed:
        early = EarlySum(ways, early_in, early_held, early_mates, early_got, early_out, early_sems)
        small = SmallSum(ways, small_value, small_got, small_sems)
        tiny = SmallSum(ways, tiny_value, tiny_got, tiny_sems)

        def late(hp):
            return LateSum(ways, hp, late_packed, late_held, late_got, late_out, late_sems)

        early.start()
        small_value[0] = small_in[...]
        small.start()
    for pg in range(pages):
        if pg > 0:
            mate_copy(pg).start()
            own_copy(pg).start()
            for copy in loads(pg):
                copy.start()
        for hp in range(pairs):
            if pg + hp > 0:
                p_load(hp, pg).start()
    for copy in w_loads:
        copy.start()
    for e in range(2):
        box_t[e] = jnp.zeros_like(box_t[e])
        box_t[e, :, e * head : (e + 1) * head] = box_w[...].astype(f32).T.astype(low)
    g_box[...] = jnp.zeros_like(g_box)

    def take(pg):
        for copy in loads(pg):
            copy.wait()
        at = pl.ds(pl.multiple_of(pg * keys, LANES), keys)
        x_t[:, at] = x[pg].reshape(keys, width).T
        own_copy(pg).wait()
        mate_copy(pg).wait_recv()

    def one_pair(pg, hp):
        lanes = pl.ds(pl.multiple_of(hp * LANES, LANES), LANES)
        p_load(hp, pg).wait()
        both = sc[pg]
        cosine2, sine2 = turned(both)
        flat = both.T
        sine_t, cosine_t = flat[:head, :chip], flat[head:, :chip]
        basis = both.astype(low)
        basis_t = flat.astype(low)
        q_pair, k_pair, v_pair = q[pg, hp], k[pg, hp], v[pg, hp]
        q_t, k_t = q_pair.T, k_pair.T
        dc = dctx[pg, :, :, lanes].reshape(chip, LANES)
        left = lane_halves((chip, LANES))
        zero = jnp.zeros_like(dc)
        dk, dv, dqs = 0.0, 0.0, []
        for e in range(2):
            mine = left if e == 0 else jnp.logical_not(left)
            own_rows = slice(e * head, (e + 1) * head)
            p = probs[pg, hp, e]
            dc_own = jnp.where(mine, dc, zero)
            q_own = jnp.where(mine, q_pair, zero)
            dp = dot_nt(v_pair, dc_own)
            p_wide = p.astype(f32)
            delta = jnp.sum(p_wide * dp, axis=0, keepdims=True)
            ds = (p_wide * (dp - delta)).astype(low)
            dv = dv + dot(p, dc_own)
            dk_feat = dot(ds, jnp.concatenate([q_own, basis[:chip]], 1)) * scale
            dq_feat = dot(jnp.concatenate([k_t[own_rows], basis_t], 0), ds) * scale
            dk_proj = rotate_key(dk_feat[:, LANES:], cosine2, sine2).astype(low)
            a, b = dq_feat[head : 2 * head], dq_feat[2 * head :]
            dq_proj = jnp.concatenate(
                [a * cosine_t - b * sine_t, a * sine_t + b * cosine_t], 0
            ).astype(low)
            dk = dk + dk_feat[:, :LANES] + dot(dk_proj, box_t[e])
            dqs.append(dq_feat[:head] + dot(box_w[...], dq_proj))
            g_box[...] += dot(k_t[own_rows], dk_proj) + dot_nt(q_t[own_rows], dq_proj)
        at = pl.ds(pl.multiple_of(pg * keys, LANES), keys)
        at_q = pl.ds(pl.multiple_of(pg * chip, LANES), chip)
        dq[hp, at_q] = jnp.concatenate(dqs, 0).T.astype(low)
        dkv[hp, at, :LANES] = dk.astype(low)
        dkv[hp, at, LANES:] = dv.astype(low)

    def pair_grads(hp):
        dkv_all = dkv[hp]
        dq_all = dq[hp]
        g_kv = column_sum(dkv_all.astype(f32))
        g_bias[pl.ds(hp, 1)] = column_sum(dq_all.astype(f32))
        g_bias[pl.ds(hp + pairs, 1)] = g_kv[:, :LANES]
        g_bias[pl.ds(hp + 2 * pairs, 1)] = g_kv[:, LANES:]
        grad = dot(x_t[...], dkv_all).astype(low)
        x_q = jnp.concatenate([x_t[:, pg * keys : pg * keys + chip] for pg in range(pages)], 1)
        grad_q = dot(x_q, dq_all).astype(low)
        late_packed[hp, 0] = grad_q.reshape(8, shard, LANES)
        late_packed[hp, 1] = grad[:, :LANES].reshape(8, shard, LANES)
        late_packed[hp, 2] = grad[:, LANES:].reshape(8, shard, LANES)

    def core_copy(pg, at):
        return remote(
            dx.at[pg, at, 1 - core], dx_mate.at[pg, at], core_send.at[pg, at], core_recv.at[pg, at],
            mate,
        )

    def side_copy(pg):
        return remote(dx.at[pg, 1, core], dx_side.at[pg], side_send.at[pg], side_recv.at[pg], side)

    def input_part(pg):
        for at in (1, 0):
            rows = pl.ds(pl.multiple_of(pg * keys + at * chip, LANES), chip)
            dks = jnp.concatenate([dkv[hp, rows, :LANES] for hp in range(pairs)], 1)
            dvs = jnp.concatenate([dkv[hp, rows, LANES:] for hp in range(pairs)], 1)
            total = dot_nt(dks, w_c[1]) + dot_nt(dvs, w_c[2])
            if at == 0:
                rows_q = pl.ds(pl.multiple_of(pg * chip, LANES), chip)
                dqs = jnp.concatenate([dq[hp, rows_q] for hp in range(pairs)], 1)
                total = total + dot_nt(dqs, w_c[0])
            dx[pg, at] = total.astype(low).reshape(2, block, width)
            core_copy(pg, at).start()

    def pass_input(pg):
        core_copy(pg, 1).wait_recv()
        dx[pg, 1, core] = dx[pg, 1, core] + dx_mate[pg, 1]
        side_copy(pg).start()

    def early_step(at):
        if not summed:
            return
        if at == 0:
            early.add_core(0)
            early.send(0)
        elif at == 1:
            early.add_core(1)
            early.send(1)
            early.add_core(2)
            early.add_core(3)
            small.advance(0)
        elif at == 2:
            early.receive(0)
            early.send(2)
            early.send(3)
            small.advance(1)
        elif at == 3:
            early.receive(1)
            small.advance(2)
        elif at == 4:
            early.receive(2)
            early.send(4)
            small.advance(3)
        elif at == 5:
            early.receive(3)
            small.advance(4)
        elif at == 6:
            early.receive(4)
            early.send(5)
        elif at == 7:
            early.share()
        elif at == 8:
            early.hand_over()

    def bias_rows():
        for part in range(3):
            for which in range(2):
                own = jnp.where(core == which, 1.0, 0.0)
                for hp in range(pairs):
                    at = part * pairs + hp
                    yield 64 + (2 * part + which) * pairs + hp, g_bias[at : at + 1] * own

    for copy in w_loads:
        copy.wait()

    @pl.loop(0, pages - 1)
    def _(pg):
        take(pg)

        @pl.when(pg > 0)
        def _():
            pass_input(pg - 1)

        @pl.loop(0, pairs)
        def _(hp):
            for at in range(pairs * (pages - 1)):

                @pl.when(pg * pairs + hp == at)
                def _(at=at):
                    early_step(at)

            one_pair(pg, hp)

        input_part(pg)

    last = pages - 1
    take(last)
    pass_input(last - 1)

    @pl.loop(0, pairs)
    def _(hp):
        for at in range(pairs):

            @pl.when(hp == at)
            def _(at=at):
                early_step(pairs * last + at)

        one_pair(last, hp)
        pair_grads(hp)
        if summed:
            late(hp).start()

            @pl.when(hp > 0)
            def _():
                late(hp - 1).advance(0)

            @pl.when(hp == 2)
            def _():
                late(0).advance(1)

    if summed:
        tiny_value[0, : 8 * 8] = g_box[...]
        tiny_value[0, 64:] = jnp.zeros((24, LANES), f32)
        for at, row in bias_rows():
            tiny_value[0, at : at + 1] = row
        tiny.start()
    input_part(last)
    if summed:
        tiny.advance(0)
        late(2).advance(0)
        late(1).advance(1)
        late(0).advance(2)
        pass_input(last)
        tiny.advance(1)
        late(2).advance(1)
        late(1).advance(2)
        late(0).advance(3)
        tiny.advance(2)
        late(2).advance(2)
        late(1).advance(3)
        late(0).advance(4)
        tiny.advance(3)
        late(2).advance(3)
        late(1).advance(4)
        tiny.advance(4)
        late(2).advance(4)
    else:
        pass_input(last)

    for pg in range(pages):
        core_copy(pg, 0).wait_recv()
        side_copy(pg).wait_recv()
        total = dx[pg, 0, core].astype(f32) + dx_mate[pg, 0].astype(f32) + dx_side[pg].astype(f32)
        dx_out[pg] = (total + dresid1[pg]).astype(low)
        for at in range(2):
            core_copy(pg, at).wait_send()
        side_copy(pg).wait_send()
        mate_copy(pg).wait_send()
    if summed:
        small_out[...] = small_value[5]
        tiny_out[...] = tiny_value[5]
        early.finish()
        for hp in range(pairs):
            late(hp).finish()
        small.finish()
        tiny.finish()
    else:
        tiny_out[:64] = g_box[...]
        tiny_out[64:] = jnp.zeros((24, LANES), f32)
        for at, row in bias_rows():
            tiny_out[at : at + 1] = row


def attend_back(dctx, x, q, k, v, sc, probs, qkv_w, box_w, dresid1, packed, small, summed):
    pages, pairs, chip, _ = q.shape
    keys = k.shape[2]
    width = x.shape[-1]
    block = chip // 2
    half = pairs * LANES
    shard = width // 8
    wide = packed.shape[2] // 2
    struct = jax.ShapeDtypeStruct
    vmem, dma = pltpu.VMEM, pltpu.SemaphoreType.DMA
    late_packed = (pairs, 3, 8, shard, LANES)
    tiny_rows = 88
    scratch = [
        vmem((pages, 4, block, width), low),
        vmem((pages, pairs, chip, LANES), low),
        vmem((pages, pairs, keys, LANES), low),
        vmem((pages, pairs, keys, LANES), low),
        vmem((pages, keys, LANES), f32),
        vmem((pages, pairs, 2, keys, chip), low),
        vmem((pages, 2, block, half), low),
        vmem((pairs, pages * chip, LANES), low),
        vmem((pairs, pages * keys, 2 * LANES), low),
        vmem((width, pages * keys), low),
        vmem((3, width, half), low),
        vmem((pages, 2, 2, block, width), low),
        vmem((pages, 2, block, width), low),
        vmem((pages, block, width), low),
        vmem((2, LANES, LANES), low),
        vmem(box_w.shape, f32),
        vmem((3 * pairs, LANES), f32),
    ]
    copies = [
        dma((pages, 5)), dma((pages, pairs)), dma((3,)), dma((pages,)), dma((pages,)), dma((pages,)),
        dma((pages, 2)), dma((pages, 2)), dma((pages,)), dma((pages,)),
    ]
    operands = [dctx, x, q, k, v, sc, probs, qkv_w, box_w, dresid1]
    in_specs = [any_spec()] * 8 + [vmem_spec()] * 2
    if summed:
        operands += [packed, small]
        in_specs += [any_spec(), vmem_spec()]
        outs = (
            struct((pages, block, width), low),
            struct((2, 3, 2, wide, LANES), low),
            struct((2, pairs, 3, 2, shard // 2, LANES), low),
            struct(small.shape, f32),
            struct((tiny_rows, LANES), f32),
        )
        scratch += [vmem(late_packed, low)] + copies
        scratch += [
            vmem((3, 16, wide, LANES), low),
            vmem((3, 16, wide, LANES), low),
            vmem((3, 15, wide, LANES), low),
            vmem((pairs, 3, 8, shard // 2, LANES), low),
            vmem((pairs, 3, 15, shard // 2, LANES), low),
            vmem((6,) + small.shape, f32),
            vmem((5,) + small.shape, f32),
            vmem((6, tiny_rows, LANES), f32),
            vmem((5, tiny_rows, LANES), f32),
        ]
        groups = len(GROUPS)
        scratch += [dma((3, 4))] * 3 + [dma((3, groups))] * 2 + [dma((3,))] * 4
        scratch += [dma((pairs, 3))] * 2 + [dma((pairs, 3, 3))] * 2 + [dma((pairs, 3))] * 4
        scratch += [dma((5,))] * 4
    else:
        outs = (
            struct((pages, block, width), low),
            struct(late_packed, low),
            struct((tiny_rows, LANES), f32),
        )
        scratch += copies
    return pl.pallas_call(
        functools.partial(attend_back_kernel, summed),
        out_shape=outs,
        in_specs=in_specs,
        out_specs=(vmem_spec(),) * len(outs),
        scratch_shapes=scratch,
        compiler_params=pltpu.CompilerParams(
            collective_id=2, has_side_effects=True, vmem_limit_bytes=63 * 2**20
        ),
        name="attend_back",
    )(*operands)


def finish_kernel(
    early, late, small, tiny, dx, up, down, out, qkv, qkv_b, box, out_b, gain1, shift1, up_b, down_b, gain2, shift2, input_grad
):
    page = lax.axis_index("page")
    shard = out.shape[0]
    pieces = up.shape[1] // (6 * LANES)
    for which in range(2):
        for order in range(3):
            column = which * 3 + order
            rows = early[which, order].astype(f32).reshape(-1, LANES)
            for piece in range(pieces):
                at = (column * pieces + piece) * LANES
                up[:, at : at + LANES] = rows[piece * shard : (piece + 1) * shard]
            at = column * LANES
            first = pieces * shard
            down[:, at : at + LANES] = rows[first : first + down.shape[0]]
            out[:, at : at + LANES] = rows[first + down.shape[0] :]
            for part in range(3):
                at = (part * 6 + column) * LANES
                qkv[:, at : at + LANES] = late[which, order, part].astype(f32).reshape(shard, LANES)
    rows = pltpu.roll(small[:8], lax.rem(8 * shard - page * shard, 8 * shard), 1)
    for at, ref in enumerate((gain2, shift2, down_b, gain1, shift1, out_b)):
        ref[...] = rows[at, :shard]
    flat = jnp.concatenate([small[8 + at : 9 + at, : pieces * LANES] for at in range(6)], 1)
    every = flat.shape[1]
    flat = pltpu.roll(flat, lax.rem(every - page * up_b.shape[0], every), 1)
    up_b[...] = flat[0, : up_b.shape[0]]
    box[...] = tiny[pl.ds(pl.multiple_of(page * 8, 8), 8)]
    count = qkv_b.shape[0]
    first = page * count
    parts = [tiny[pl.ds(64 + first // LANES + piece, 1)] for piece in range(4)]
    rest = lax.rem(first, LANES)
    row = pltpu.roll(jnp.concatenate(parts, 1), lax.rem(4 * LANES - rest, 4 * LANES), 1)
    qkv_b[...] = row[0, :count]
    input_grad[...] = dx[...]


def finish(early, late, small, tiny, dx):
    struct = jax.ShapeDtypeStruct
    shapes = (
        (96, 3072), (384, 768), (96, 768), (96, 2304), (288,), (8, LANES), (96,), (96,), (96,), (384,), (96,), (96,), (96,),
    )
    return pl.pallas_call(
        finish_kernel,
        out_shape=tuple(struct(shape, f32) for shape in shapes) + (struct(dx.shape, low),),
        in_specs=[vmem_spec()] * 5,
        out_specs=(vmem_spec(),) * 14,
        compiler_params=pltpu.CompilerParams(vmem_limit_bytes=40 * 2**20),
        name="finish",
    )(early, late, small, tiny, dx)


def reduce_by_collectives(packed, packed_qkv, vectors):
    core = lax.axis_index("blk") % 2
    up = packed[:, :, :384].reshape(6, 8, 4, 96, LANES).transpose(1, 3, 0, 2, 4).reshape(768, 3072)
    down = packed[:, :, 384:768].transpose(1, 2, 0, 3).reshape(3072, 768)
    out = packed[:, :, 768:].transpose(1, 2, 0, 3).reshape(768, 768)
    own = packed_qkv.transpose(2, 3, 1, 0, 4).reshape(768, 3, 384)
    qkv = jnp.zeros((768, 3, 2, 384), low)
    qkv = lax.dynamic_update_slice(qkv, own[:, :, None], (0, 0, core, 0)).reshape(768, 2304)
    grads = jax.tree.map(lambda g: g.astype(f32), (qkv, out, up, down, *vectors))
    page_sums = tuple(
        lax.psum_scatter(grad, "page", scatter_dimension=0, tiled=True) for grad in grads
    )
    return jax.tree.map(
        lambda part: part.astype(f32), lax.psum(jax.tree.map(lambda g: g.astype(low), page_sums), "blk")
    )


def local(
    tokens, lengths, boxes, qkv_weight, qkv_bias, box_weight, out_weight, out_bias, norm1_gain,
    norm1_bias, up_weight, up_bias, down_weight, down_bias, norm2_gain, norm2_bias, cotangent,
):
    pages, block, width = tokens.shape
    rows = pages * block
    x, q, k, v, sc, probs, ctx = attend(tokens, boxes, lengths, qkv_weight, qkv_bias, box_weight)
    output, dresid1, dctx, packed, small = feed(
        ctx.reshape(rows, width), tokens.reshape(rows, width), cotangent.reshape(rows, width),
        out_weight, up_weight, down_weight, out_bias, norm1_gain, norm1_bias, up_bias, down_bias,
        norm2_gain, norm2_bias,
    )
    summed = lax.axis_size("page") == 8
    parts = attend_back(
        dctx.reshape(pages, block, width), x, q, k, v, sc, probs, qkv_weight, box_weight,
        dresid1.reshape(pages, block, width), packed, small, summed,
    )
    output = output.reshape(pages, block, width)
    if summed:
        dx, early, late, small, tiny = parts
        (
            up_w, down_w, out_w, qkv_w, qkv_b, box, out_b, gain1, shift1, up_b, down_b, gain2, shift2, input_grad,
        ) = finish(early, late, small, tiny, dx)
        box = box.reshape(-1)
    else:
        input_grad, packed_qkv, tiny = parts
        vectors = (
            tiny[64:82].reshape(-1), tiny[:64].reshape(-1), small[5], small[3], small[4],
            small[8:14, :512].reshape(-1), small[2], small[0], small[1],
        )
        (
            qkv_w, out_w, up_w, down_w, qkv_b, box, out_b, gain1, shift1, up_b, down_b, gain2, shift2,
        ) = reduce_by_collectives(packed, packed_qkv, vectors)
    return (
        output, input_grad, qkv_w, qkv_b, box, out_w, out_b, gain1, shift1, up_w, up_b, down_w, down_b, gain2, shift2,
    )


def solution(mesh):
    return jax.shard_map(
        local,
        mesh=mesh,
        in_specs=(
            P("page", "blk", None),
            P("page"),
            P("page", "blk", None),
            P(),
            P(),
            P(),
            P(),
            P(),
            P(),
            P(),
            P(),
            P(),
            P(),
            P(),
            P(),
            P(),
            P("page", "blk", None),
        ),
        out_specs=(
            P("page", "blk", None),
            P("page", "blk", None),
            P("page", None),
            P("page"),
            P("page"),
            P("page", None),
            P("page"),
            P("page"),
            P("page"),
            P("page", None),
            P("page"),
            P("page", None),
            P("page"),
            P("page"),
            P("page"),
        ),
        check_vma=False,
    )
```

```python
import functools

import jax
import jax.numpy as jnp
import numpy as np
from jax import lax
from jax.experimental import pallas as pl
from jax.experimental.pallas import tpu as pltpu
from jax.sharding import PartitionSpec as P

norm_eps = 1e-12
MESH = pl.DeviceIdType.MESH
LANES = 128
low = jnp.bfloat16
f32 = jnp.float32


def core_of(blk):
    return blk + 1 - 2 * (blk % 2)


def side_of(blk):
    return (blk + 2) % 4


def greet(others):
    barrier = pltpu.get_barrier_semaphore()
    for other in others:
        pl.semaphore_signal(barrier, inc=1, device_id=other, device_id_type=MESH)
    pl.semaphore_wait(barrier, len(others))


def remote(src, dst, send_sem, recv_sem, to):
    return pltpu.make_async_remote_copy(
        src_ref=src, dst_ref=dst, send_sem=send_sem, recv_sem=recv_sem, device_id=to,
        device_id_type=MESH,
    )


def dot(a, b):
    return jnp.dot(a, b, preferred_element_type=f32)


def dot_nt(a, b):
    return lax.dot_general(a, b, (((1,), (1,)), ((), ())), preferred_element_type=f32)


def dot_tn(a, b):
    return lax.dot_general(a, b, (((0,), (0,)), ((), ())), preferred_element_type=f32)


def sin_cos(theta):
    turns = jnp.floor(theta * 0.6366197723675814 + 0.5)
    rest = theta - turns * 1.5703125
    rest = rest - turns * 4.837512969970703125e-4
    rest = rest - turns * 7.54978995489188216e-8
    square = rest * rest
    sine = ((-1.9515295891e-4 * square + 8.3321608736e-3) * square - 1.6666654611e-1) * square
    sine = sine * rest + rest
    cosine = (2.443315711809948e-5 * square - 1.388731625493765e-3) * square + 4.166664568298827e-2
    cosine = cosine * square * square - 0.5 * square + 1.0
    quarter = turns.astype(jnp.int32)
    odd = (quarter & 1) == 1
    sine_at = jnp.where(odd, cosine, sine)
    cosine_at = jnp.where(odd, sine, cosine)
    sine_at = jnp.where((quarter & 2) == 2, -sine_at, sine_at)
    cosine_at = jnp.where(((quarter + 1) & 2) == 2, -cosine_at, cosine_at)
    return sine_at, cosine_at


def lane_halves(shape):
    return lax.broadcasted_iota(jnp.int32, shape, 1) < LANES // 2


def turned(both):
    swapped = pltpu.roll(both, LANES // 2, 1)
    left = lane_halves(both.shape)
    return jnp.where(left, -swapped, both), jnp.where(left, both, swapped)


def rotate_key(proj, cosine2, sine2):
    return proj * cosine2 + pltpu.roll(proj, LANES // 2, 1) * sine2


def attend_kernel(
    tokens, boxes, lengths, freq, qkv_w, qkv_b, box_w,
    x_out, q_out, k_out, v_out, sc_out, p_out, ctx_out,
    x, box, w_q, w_kv, q, k, v, sc, probs, ctx, box2,
    own_sem, w_sem, out_sem, p_sem, ctx_sem,
    mate_send, mate_recv, side_send, side_recv, pass_send, pass_recv, ctx_send, ctx_recv,
):
    page, blk = lax.axis_index("page"), lax.axis_index("blk")
    core, side_at = blk % 2, blk // 2
    mate, side = (page, core_of(blk)), (page, side_of(blk))
    pages = tokens.shape[0]
    half = w_q.shape[1]
    pairs = half // LANES
    chip = 2 * tokens.shape[1]
    keys = 2 * chip
    scale = 0.125

    def of_half(part):
        return pl.ds(pl.multiple_of(part * 2 * half + core * half, LANES), half)

    loads = [
        pltpu.make_async_copy(qkv_w.at[:, of_half(0)], w_q, w_sem.at[0]),
        pltpu.make_async_copy(qkv_w.at[:, of_half(1)], w_kv.at[:, :half], w_sem.at[1]),
        pltpu.make_async_copy(qkv_w.at[:, of_half(2)], w_kv.at[:, half:], w_sem.at[2]),
    ]
    own = []
    for pg in range(pages):
        own.append(pltpu.make_async_copy(tokens.at[pg], x.at[pg, core], own_sem.at[pg, 0]))
        own.append(pltpu.make_async_copy(boxes.at[pg], box.at[pg, core], own_sem.at[pg, 1]))
    for copy in own:
        copy.start()
    for copy in loads:
        copy.start()
    greet((mate, side))
    to_mate, to_side = [], []
    for pg in range(pages):
        for which, (src, dst) in enumerate(((tokens, x), (boxes, box))):
            to_side.append(
                remote(src.at[pg], dst.at[pg, 2 + core], side_send.at[pg, which], side_recv.at[pg, which], side)
            )
            to_side[-1].start()
            to_mate.append(
                remote(src.at[pg], dst.at[pg, core], mate_send.at[pg, which], mate_recv.at[pg, which], mate)
            )
            to_mate[-1].start()
    zero = jnp.zeros_like(box_w)
    box2[...] = jnp.concatenate(
        [jnp.concatenate([box_w[...], zero], 1), jnp.concatenate([zero, box_w[...]], 1)], 0
    )

    def bias_of(part):
        both = [
            qkv_b[(2 * part + which) * half : (2 * part + which + 1) * half].reshape(1, half)
            for which in range(2)
        ]
        return jnp.where(core == 0, both[0], both[1])

    for copy in loads:
        copy.wait()

    @pl.loop(0, pages)
    def _(pg):
        passed = []
        for which, (src, dst) in enumerate(((tokens, x), (boxes, box))):
            remote(
                src.at[pg], dst.at[pg, 2 + core], side_send.at[pg, which], side_recv.at[pg, which], side
            ).wait_recv()
            copy = remote(
                dst.at[pg, 2 + core], dst.at[pg, 2 + core], pass_send.at[pg, which],
                pass_recv.at[pg, which], mate,
            )
            copy.start()
            passed.append(copy)
            pltpu.make_async_copy(src.at[pg], dst.at[pg, core], own_sem.at[pg, which]).wait()
            remote(
                src.at[pg], dst.at[pg, core], mate_send.at[pg, which], mate_recv.at[pg, which], mate
            ).wait_recv()
        for copy in passed:
            copy.wait_recv()
        pltpu.make_async_copy(x.at[pg], x_out.at[pg], out_sem.at[pg, 0]).start()
        for at in range(4):
            rows = box[pg, at]
            spread = [
                jnp.broadcast_to(rows[c : c + 1], (freq.shape[0] // 4, LANES)) for c in range(4)
            ]
            sine, cosine = sin_cos(jnp.concatenate(spread, 0) * freq[...])
            sc[pg, at * LANES : (at + 1) * LANES] = jnp.concatenate([sine, cosine], 0).T
        pltpu.make_async_copy(sc.at[pg], sc_out.at[pg], out_sem.at[pg, 1]).start()
        x_all = x[pg].reshape(keys, x.shape[-1])
        q_all = (dot(x_all[:chip], w_q[...]) + bias_of(0)).astype(low)
        bias = jnp.concatenate([bias_of(1), bias_of(2)], 1)
        kv_all = (dot(x_all, w_kv[...]) + bias).astype(low)
        for hp in range(pairs):
            q[pg, hp] = q_all[:, hp * LANES : (hp + 1) * LANES]
            k[pg, hp] = kv_all[:, hp * LANES : (hp + 1) * LANES]
            v[pg, hp] = kv_all[:, half + hp * LANES : half + (hp + 1) * LANES]
        for which, (src, dst) in enumerate(((q, q_out), (k, k_out), (v, v_out))):
            pltpu.make_async_copy(src.at[pg], dst.at[pg], out_sem.at[pg, 2 + which]).start()
        place = lax.broadcasted_iota(jnp.int32, (keys, chip), 0) + side_at * chip
        place = jnp.where(place >= keys, place - keys, place)
        valid = place < lengths[pg]

        @pl.loop(0, pairs)
        def _(hp):
            both = sc[pg]
            cosine2, sine2 = turned(both)
            basis = both.astype(low)
            basis_q = (both[:chip] * scale).astype(low)
            left = lane_halves((chip, LANES))
            cosine_q = jnp.where(left, -cosine2[:chip], cosine2[:chip]) * scale
            sine_q = jnp.where(left, sine2[:chip], -sine2[:chip]) * scale
            q_pair, k_pair = q[pg, hp], k[pg, hp]
            q_proj = dot(q_pair, box2[...])
            k_proj = dot(k_pair, box2[...])
            v_t = v[pg, hp].T
            outs = []
            for e in range(2):
                at = slice(e * LANES, (e + 1) * LANES)
                q_pos = rotate_key(q_proj[:, at], cosine_q, sine_q).astype(low)
                k_pos = rotate_key(k_proj[:, at], cosine2, sine2).astype(low)
                mine = left if e == 0 else jnp.logical_not(left)
                q_own = jnp.where(mine, q_pair.astype(f32) * scale, 0.0).astype(low)
                scores = dot_nt(
                    jnp.concatenate([basis, k_pos], 1), jnp.concatenate([q_pos, basis_q], 1)
                )
                scores = scores + dot_nt(k_pair, q_own)
                scores = jnp.where(valid, scores, -1e30)
                top = jnp.max(scores, axis=0, keepdims=True)
                grown = jnp.exp(scores - top)
                total = jnp.sum(grown, axis=0, keepdims=True)
                p = (grown * (1.0 / total)).astype(low)
                probs[pg, hp, e] = p
                outs.append(dot(v_t[e * LANES // 2 : (e + 1) * LANES // 2], p))
            pltpu.make_async_copy(probs.at[pg, hp], p_out.at[pg, hp], p_sem.at[pg, hp]).start()
            context = jnp.concatenate(outs, 0).T.astype(low)
            lanes = pl.ds(pl.multiple_of(hp * LANES, LANES), LANES)
            ctx[pg, 0, :, lanes] = context[: chip // 2]
            ctx[pg, 1, :, lanes] = context[chip // 2 :]

        mine = pl.ds(pl.multiple_of(core * half, LANES), half)
        pltpu.make_async_copy(ctx.at[pg, core], ctx_out.at[pg, :, mine], ctx_sem.at[pg]).start()
        remote(
            ctx.at[pg, 1 - core], ctx_out.at[pg, :, mine], ctx_send.at[pg], ctx_recv.at[pg], mate
        ).start()
        for copy in passed:
            copy.wait_send()

    mine = pl.ds(pl.multiple_of(core * half, LANES), half)
    for pg in range(pages):
        for which, (src, dst) in enumerate(((x, x_out), (sc, sc_out), (q, q_out), (k, k_out), (v, v_out))):
            pltpu.make_async_copy(src.at[pg], dst.at[pg], out_sem.at[pg, which]).wait()
        for hp in range(pairs):
            pltpu.make_async_copy(probs.at[pg, hp], p_out.at[pg, hp], p_sem.at[pg, hp]).wait()
        pltpu.make_async_copy(ctx.at[pg, core], ctx_out.at[pg, :, mine], ctx_sem.at[pg]).wait()
        remote(
            ctx.at[pg, 1 - core], ctx_out.at[pg, :, mine], ctx_send.at[pg], ctx_recv.at[pg], mate
        ).wait()
    for copy in to_side + to_mate:
        copy.wait_send()


def any_spec():
    return pl.BlockSpec(memory_space=pl.ANY)


def vmem_spec():
    return pl.BlockSpec(memory_space=pltpu.VMEM)


def attend(tokens, boxes, lengths, qkv_w, qkv_b, box_weight):
    pages, block, width = tokens.shape
    head_dim, pos = box_weight.shape
    half = width // 2
    pairs = half // LANES
    chip, keys = 2 * block, 4 * block
    count = pos // 8
    freqs = 10000.0 ** (-np.arange(count) / count)
    freq = jnp.asarray(np.tile(np.tile(freqs, 4)[:, None], (1, LANES)), f32)
    boxes_t = boxes.astype(f32).transpose(0, 2, 1)
    struct = jax.ShapeDtypeStruct
    vmem, dma = pltpu.VMEM, pltpu.SemaphoreType.DMA
    return pl.pallas_call(
        attend_kernel,
        out_shape=(
            struct((pages, 4, block, width), low),
            struct((pages, pairs, chip, LANES), low),
            struct((pages, pairs, keys, LANES), low),
            struct((pages, pairs, keys, LANES), low),
            struct((pages, keys, LANES), f32),
            struct((pages, pairs, 2, keys, chip), low),
            struct((pages, block, width), low),
        ),
        in_specs=[any_spec(), any_spec(), pl.BlockSpec(memory_space=pltpu.SMEM), vmem_spec(), any_spec(), vmem_spec(), vmem_spec()],
        out_specs=(any_spec(),) * 7,
        scratch_shapes=[
            vmem((pages, 4, block, width), low),
            vmem((pages, 4, 4, LANES), f32),
            vmem((width, half), low),
            vmem((width, 2 * half), low),
            vmem((pages, pairs, chip, LANES), low),
            vmem((pages, pairs, keys, LANES), low),
            vmem((pages, pairs, keys, LANES), low),
            vmem((pages, keys, LANES), f32),
            vmem((pages, pairs, 2, keys, chip), low),
            vmem((pages, 2, block, half), low),
            vmem((2 * head_dim, 2 * pos), low),
            dma((pages, 2)), dma((3,)), dma((pages, 5)), dma((pages, pairs)), dma((pages,)),
            dma((pages, 2)), dma((pages, 2)), dma((pages, 2)), dma((pages, 2)),
            dma((pages, 2)), dma((pages, 2)), dma((pages,)), dma((pages,)),
        ],
        compiler_params=pltpu.CompilerParams(
            collective_id=1, has_side_effects=True, vmem_limit_bytes=56 * 2**20
        ),
        name="attend",
    )(tokens, boxes_t, lengths, freq, qkv_w, qkv_b, box_weight)


ORDERS = ("xaym", "ayxm", "yxam")
GROUPS = ((12, 16), (8, 12), (6, 8), (4, 6), (2, 4), (1, 2))


def flip(page, way):
    x, z = page % 2, page // 2
    if way == "x":
        return z * 2 + (1 - x)
    if way == "a":
        return (z + 1 - 2 * (z % 2)) * 2 + x
    return ((z + 2) % 4) * 2 + x


class Ways:
    def __init__(self):
        self.page, self.blk = lax.axis_index("page"), lax.axis_index("blk")
        self.core, self.half = self.blk % 2, self.blk // 2
        self.mate, self.side = (self.page, core_of(self.blk)), (self.page, side_of(self.blk))

    def partner(self, way):
        return self.side if way == "y" else (flip(self.page, way), self.blk)

    def piece(self, order, code):
        page, half = self.page, self.half
        for place, way in enumerate(ORDERS[order]):
            if code >> (3 - place) & 1:
                if way == "y":
                    half = 1 - half
                else:
                    page = flip(page, way)
        return page, half

    def everyone(self):
        return [self.partner(way) for way in "xamy"] + [self.mate]


def step_of(code):
    return 4 - code.bit_length()


class EarlySum:
    def __init__(self, ways, held, got, sems):
        self.ways, self.held, self.got = ways, held, got
        self.send_sem, self.recv_sem = sems
        self.rows = held.shape[2]

    slices = ((12, 16), (8, 12), (4, 8), (0, 4))

    def halve_cores(self, packed, mates, sems):
        ways = self.ways
        self.mates = mates
        self.own_sem, self.core_send, self.core_recv = sems
        for at, (begin, end) in enumerate(self.slices):
            for code in range(begin, end):
                for order in range(3):
                    page, half = ways.piece(order, code)
                    rows = pl.ds(pl.multiple_of(half * self.rows, 16), self.rows)
                    remote(
                        packed.at[3 - 3 * ways.core + order, page, rows], mates.at[order, code],
                        self.core_send.at[order, at], self.core_recv.at[order, at], ways.mate,
                    ).start()
                    pltpu.make_async_copy(
                        packed.at[3 * ways.core + order, page, rows], self.held.at[order, code],
                        self.own_sem.at[order, at],
                    ).start()

    def core_group(self, order, at):
        begin, end = self.slices[at]
        part = self.mates.at[order, begin:end]
        return remote(part, part, self.core_send.at[order, at], self.core_recv.at[order, at], self.ways.mate)

    def add_core(self, at):
        begin, end = self.slices[at]
        for order in range(3):
            own = self.held.at[order, begin:end]
            pltpu.make_async_copy(own, own, self.own_sem.at[order, at]).wait()
            self.core_group(order, at).wait_recv()
            self.held[order, begin:end] = self.held[order, begin:end] + self.mates[order, begin:end]

    def end_cores(self):
        for order in range(3):
            for at in range(4):
                self.core_group(order, at).wait_send()

    def copy(self, order, group):
        begin, end = GROUPS[group]
        way = ORDERS[order][step_of(begin)]
        return remote(
            self.held.at[order, begin:end], self.got.at[order, begin - 1 : end - 1],
            self.send_sem.at[order, group], self.recv_sem.at[order, group], self.ways.partner(way),
        )

    def send(self, group):
        for order in range(3):
            self.copy(order, group).start()

    def receive(self, group):
        begin, end = GROUPS[group]
        base = 1 << (begin.bit_length() - 1)
        for order in range(3):
            self.copy(order, group).wait_recv()
            to = slice(begin - base, end - base)
            self.held[order, to] = self.held[order, to] + self.got[order, begin - 1 : end - 1]

    def end_steps(self, groups):
        for order in range(3):
            for group in groups:
                self.copy(order, group).wait_send()

    def share(self, final, sems):
        self.final = final
        self.last_send, self.last_recv, self.end_send, self.end_recv = sems
        for order in range(3):
            self.copy(order, 5).wait_recv()
            final[self.ways.core, order, self.ways.half] = self.held[order, 0] + self.got[order, 0]
            self.last_copy(order).start()

    def last_copy(self, order):
        part = self.final.at[self.ways.core, order, self.ways.half]
        return remote(part, part, self.last_send.at[order], self.last_recv.at[order], self.ways.side)

    def end_copy(self, order):
        part = self.final.at[self.ways.core, order]
        return remote(part, part, self.end_send.at[order], self.end_recv.at[order], self.ways.mate)

    def hand_over(self):
        for order in range(3):
            self.last_copy(order).wait_recv()
            self.end_copy(order).start()

    def end(self):
        for order in range(3):
            self.end_copy(order).wait()
            self.last_copy(order).wait_send()


class LateSum:
    def __init__(self, ways, hp, packed, held, got, final, sems):
        self.ways, self.hp = ways, hp
        self.packed, self.held, self.got, self.final = packed, held, got, final
        (self.first_send, self.first_recv, self.send_sem, self.recv_sem, self.last_send, self.last_recv,
         self.end_send, self.end_recv) = sems
        self.rows = held.shape[3]

    def start(self):
        ways, hp = self.ways, self.hp
        for code in range(8, 16):
            for order in range(3):
                page, half = ways.piece(order, code)
                rows = pl.ds(pl.multiple_of(half * self.rows, 16), self.rows)
                remote(
                    self.packed.at[hp, order, page, rows], self.got.at[hp, order, code - 1],
                    self.first_send.at[hp, order], self.first_recv.at[hp, order],
                    ways.partner(ORDERS[order][0]),
                ).start()

    def first(self, order):
        part = self.got.at[self.hp, order, 7:15]
        return remote(
            part, part, self.first_send.at[self.hp, order], self.first_recv.at[self.hp, order],
            self.ways.partner(ORDERS[order][0]),
        )

    def copy(self, order, step):
        begin, end = 8 >> step, 16 >> step
        return remote(
            self.held.at[self.hp, order, begin:end], self.got.at[self.hp, order, begin - 1 : end - 1],
            self.send_sem.at[self.hp, order, step - 1], self.recv_sem.at[self.hp, order, step - 1],
            self.ways.partner(ORDERS[order][step]),
        )

    def advance(self, step):
        ways, hp = self.ways, self.hp
        for order in range(3):
            if step == 0:
                self.first(order).wait_recv()
                for code in (4, 5, 6, 7, 0, 1, 2, 3):
                    page, half = ways.piece(order, code)
                    rows = pl.ds(pl.multiple_of(half * self.rows, 16), self.rows)
                    self.held[hp, order, code] = self.packed[hp, order, page, rows] + self.got[hp, order, code + 7]
                    if code == 7:
                        self.copy(order, 1).start()
            elif step < 3:
                self.copy(order, step).wait_recv()
                count = 8 >> step
                self.held[hp, order, :count] = (
                    self.held[hp, order, :count] + self.got[hp, order, count - 1 : 2 * count - 1]
                )
                self.copy(order, step + 1).start()
            elif step == 3:
                self.copy(order, 3).wait_recv()
                self.final[ways.core, hp, order, ways.half] = self.held[hp, order, 0] + self.got[hp, order, 0]
                self.last_copy(order).start()
            else:
                self.last_copy(order).wait_recv()
                self.end_copy(order).start()

    def last_copy(self, order):
        part = self.final.at[self.ways.core, self.hp, order, self.ways.half]
        return remote(
            part, part, self.last_send.at[self.hp, order], self.last_recv.at[self.hp, order], self.ways.side
        )

    def end_copy(self, order):
        part = self.final.at[self.ways.core, self.hp, order]
        return remote(
            part, part, self.end_send.at[self.hp, order], self.end_recv.at[self.hp, order], self.ways.mate
        )

    def finish(self):
        for order in range(3):
            self.end_copy(order).wait()
            self.last_copy(order).wait_send()
            self.first(order).wait_send()
            for step in (1, 2, 3):
                self.copy(order, step).wait_send()


class SmallSum:
    def __init__(self, ways, value, got, sems):
        self.ways, self.value, self.got = ways, value, got
        self.send_sem, self.recv_sem = sems
        self.to = ways.everyone()

    def copy(self, step):
        return remote(
            self.value.at[step], self.got.at[step], self.send_sem.at[step], self.recv_sem.at[step], self.to[step]
        )

    def start(self):
        self.copy(0).start()

    def advance(self, step):
        self.copy(step).wait_recv()
        self.value[step + 1] = self.value[step] + self.got[step]
        if step < 4:
            self.copy(step + 1).start()

    def finish(self):
        for step in range(5):
            self.copy(step).wait_send()


def norm_of(resid):
    center = resid - jnp.mean(resid, axis=-1, keepdims=True)
    spread = jnp.mean(center * center, axis=-1, keepdims=True)
    inverse = lax.rsqrt(spread + norm_eps)
    return center * inverse, inverse


def norm_back(grad, normed, inverse):
    mean = jnp.mean(grad, axis=-1, keepdims=True)
    along = jnp.mean(grad * normed, axis=-1, keepdims=True)
    return inverse * (grad - mean - normed * along)


def column_sum(values):
    return jnp.sum(values, axis=0, keepdims=True)


def feed_kernel(
    summed, ctx, tokens, cotangent, out_w, up_w, down_w, out_b, gain1, shift1, up_b, down_b, gain2, shift2,
    output, dresid1, dctx, packed, g_rows, part_out,
    w_out, w_up, w_down, act, slope, norm1, inverse1, hidden, hidden_t, grow, staged, up_rows, w_sem, up_sem, down_sem, *refs,
):
    def row(ref):
        return ref[...].reshape(1, -1)

    if summed:
        packed_down, held, mates, got, *sems = refs
        ways = Ways()
        greet(ways.everyone())
        early = EarlySum(ways, held, got, sems[3:])
    else:
        packed_down = part_out

    def early_step(at):
        if not summed:
            return
        if at == 0:
            early.add_core(0)
            early.send(0)
        elif at == 1:
            early.add_core(1)
            early.send(1)
            early.add_core(2)
            early.add_core(3)

    chunks, chunk = w_up.shape[0], w_up.shape[2]
    width = ctx.shape[1]
    up_pieces = chunk // LANES
    shard = width // 8
    out_load = pltpu.make_async_copy(out_w, w_out, w_sem)
    out_load.start()

    def up_load(j):
        return pltpu.make_async_copy(
            up_w.at[:, pl.ds(pl.multiple_of(j * chunk, LANES), chunk)], w_up.at[j], up_sem.at[j]
        )

    def down_load(j):
        return pltpu.make_async_copy(
            down_w.at[pl.ds(pl.multiple_of(j * chunk, LANES), chunk)], w_down.at[j], down_sem.at[j]
        )

    for j in range(chunks):
        up_load(j).start()
        down_load(j).start()
    g_rows[...] = jnp.zeros_like(g_rows)
    for j in range(chunks):
        up_rows[j : j + 1] = up_b[j * chunk : (j + 1) * chunk].reshape(1, chunk)
    out_load.wait()
    resid = tokens[...].astype(f32) + dot(ctx[...], w_out[...]) + row(out_b)
    normed, inverse = norm_of(resid)
    norm1[...] = normed
    inverse1[...] = jnp.broadcast_to(inverse, inverse1.shape)
    first = normed * row(gain1) + row(shift1)
    hidden[...] = first.astype(low)
    hidden_t[...] = first.astype(low).T
    grow[...] = first + row(down_b)

    @pl.loop(0, chunks)
    def _(j):
        up_load(j).wait()
        upper = dot(hidden[...], w_up[j]) + up_rows[pl.ds(j, 1)]
        cdf = 0.5 + 0.5 * lax.erf(upper * 0.7071067811865476)
        act_low = (upper * cdf).astype(low)
        act[j] = act_low
        slope[j] = cdf + upper * (jnp.exp(upper * upper * -0.5) * 0.3989422804014327)
        down_load(j).wait()
        grow[...] += dot(act_low, w_down[j])

    normed2, inverse2 = norm_of(grow[...])
    output[...] = (normed2 * row(gain2) + row(shift2)).astype(low)
    cot = cotangent[...].astype(f32)
    g_rows[0:1] = column_sum(cot * normed2)
    g_rows[1:2] = column_sum(cot)
    dresid2 = norm_back(cot * row(gain2), normed2, inverse2)
    dffn = dresid2.astype(low)
    g_rows[2:3] = column_sum(dffn.astype(f32))
    grow[...] = dresid2
    staged[...] = dffn

    @pl.loop(0, chunks)
    def _(j):
        grad_down = dot_tn(act[j], staged[...]).astype(low)
        for piece in range(up_pieces):
            at = j * up_pieces + piece
            per = up_pieces * chunks // 8
            rows = pl.ds(pl.multiple_of((at % per) * LANES, LANES), LANES)
            for column in range(6):
                packed_down[column, at // per, rows] = grad_down[
                    piece * LANES : (piece + 1) * LANES, column * LANES : (column + 1) * LANES
                ]

    if summed:
        early.halve_cores(packed_down, mates, sems[:3])

    @pl.loop(0, chunks)
    def _(j):
        for at in range(chunks):

            @pl.when(j == at)
            def _(at=at):
                early_step(at)

        dffn = staged[...]
        dupper = (dot_nt(dffn, w_down[j]) * slope[j]).astype(low)
        g_rows[pl.ds(8 + j, 1), :chunk] = column_sum(dupper.astype(f32))
        grow[...] += dot_nt(dupper, w_up[j])
        grad_up = dot(hidden_t[...], dupper).astype(low)
        for piece in range(up_pieces):
            part = grad_up[:, piece * LANES : (piece + 1) * LANES].reshape(8, shard, LANES)
            packed[j, :, piece * shard : (piece + 1) * shard] = part

    dhidden = grow[...]
    normed = norm1[...]
    g_rows[3:4] = column_sum(dhidden * normed)
    g_rows[4:5] = column_sum(dhidden)
    back = norm_back(dhidden * row(gain1), normed, inverse1[:, :1])
    dresid1[...] = back
    dattn = back.astype(low)
    g_rows[5:6] = column_sum(dattn.astype(f32))
    dctx[...] = dot_nt(dattn, w_out[...]).astype(low)
    grad_out = dot_tn(ctx[...], dattn).astype(low)
    first_row = packed.shape[2] - shard
    for column in range(6):
        part = grad_out[:, column * LANES : (column + 1) * LANES].reshape(8, shard, LANES)
        packed[column, :, first_row:] = part
    if summed:
        early.receive(0)
        early.receive(1)
        part_out[...] = held[:, :8]
        early.end_cores()
        early.end_steps(range(2))


def feed(ctx, tokens, cotangent, out_w, up_w, down_w, vectors, summed):
    rows, width = ctx.shape
    hidden_width = up_w.shape[1]
    chunks = 6
    chunk = hidden_width // chunks
    shard = width // 8
    packed_rows = (chunk // LANES) * shard + shard
    down_rows = hidden_width // 8
    struct = jax.ShapeDtypeStruct
    vmem, dma = pltpu.VMEM, pltpu.SemaphoreType.DMA
    packed_down = (6, 8, down_rows, LANES)
    extra, params = [], {}
    if summed:
        half = down_rows // 2
        extra = [
            vmem(packed_down, low), vmem((3, 16, half, LANES), low), vmem((3, 16, half, LANES), low),
            vmem((3, 15, half, LANES), low), dma((3, 4)), dma((3, 4)), dma((3, 4)),
            dma((3, len(GROUPS))), dma((3, len(GROUPS))),
        ]
        params = dict(collective_id=3, has_side_effects=True)

    return pl.pallas_call(
        functools.partial(feed_kernel, summed),
        out_shape=(
            struct((rows, width), low),
            struct((rows, width), f32),
            struct((rows, width), low),
            struct((6, 8, packed_rows, LANES), low),
            struct((16, width), f32),
            struct((3, 8, half, LANES) if summed else packed_down, low),
        ),
        in_specs=[vmem_spec()] * 3 + [any_spec()] * 3 + [vmem_spec()] * 7,
        out_specs=(vmem_spec(),) * 6,
        scratch_shapes=[
            vmem((width, width), low),
            vmem((chunks, width, chunk), low),
            vmem((chunks, chunk, width), low),
            vmem((chunks, rows, chunk), low),
            vmem((chunks, rows, chunk), f32),
            vmem((rows, width), f32),
            vmem((rows, LANES), f32),
            vmem((rows, width), low),
            vmem((width, rows), low),
            vmem((rows, width), f32),
            vmem((rows, width), low),
            vmem((chunks, chunk), f32),
            dma, dma((chunks,)), dma((chunks,)), *extra,
        ],
        compiler_params=pltpu.CompilerParams(vmem_limit_bytes=60 * 2**20, **params),
        name="feed",
    )(ctx, tokens, cotangent, out_w, up_w, down_w, *vectors)


def attend_back_kernel(
    summed, dctx_own, x_in, q_in, k_in, v_in, sc_in, p_in, qkv_w, box_w, dresid1, *refs
):
    if summed:
        (
            early_in, down_in, small_in,
            dx_out, early_out, down_out, late_out, small_out, tiny_out,
            x, q, k, v, sc, probs, dctx, dq, dkv, x_t, w_c, dx, dx_mate, dx_side, box_t, g_box, g_bias, late_packed,
            in_sem, p_sem, w_sem, own_sem, mate_send, mate_recv, core_send, core_recv, side_send, side_recv,
            early_held, early_mates, early_got, down_held, down_got, late_held, late_got, small_value, small_got, tiny_value, tiny_got,
            *sems,
        ) = refs
        core_sems, early_sems, early_ends, down_sems, down_ends = sems[:3], sems[3:5], sems[5:9], sems[9:11], sems[11:15]
        down_load, late_sems, small_sems, tiny_sems = sems[15], sems[16:24], sems[24:26], sems[26:28]
    else:
        (
            dx_out, late_packed, tiny_out,
            x, q, k, v, sc, probs, dctx, dq, dkv, x_t, w_c, dx, dx_mate, dx_side, box_t, g_box, g_bias,
            in_sem, p_sem, w_sem, own_sem, mate_send, mate_recv, core_send, core_recv, side_send, side_recv,
        ) = refs
    ways = Ways()
    core, mate, side = ways.core, ways.mate, ways.side
    pages, pairs, chip, _ = q.shape
    keys = k.shape[2]
    block = chip // 2
    half = pairs * LANES
    width = x.shape[-1]
    shard = width // 8
    head = LANES // 2
    scale = 0.125

    def of_half(part, which):
        return pl.ds(pl.multiple_of(part * 2 * half + which * half, LANES), half)

    def loads(pg):
        names = ((x_in, x), (q_in, q), (k_in, k), (v_in, v), (sc_in, sc))
        return [
            pltpu.make_async_copy(src.at[pg], dst.at[pg], in_sem.at[pg, at])
            for at, (src, dst) in enumerate(names)
        ]

    def p_load(hp, pg):
        return pltpu.make_async_copy(p_in.at[pg, hp], probs.at[pg, hp], p_sem.at[pg, hp])

    w_loads = [
        pltpu.make_async_copy(qkv_w.at[:, of_half(part, core)], w_c.at[part], w_sem.at[part])
        for part in range(3)
    ]

    def own_copy(pg):
        return pltpu.make_async_copy(
            dctx_own.at[pg, :, of_half(0, core)], dctx.at[pg, core], own_sem.at[pg]
        )

    def mate_copy(pg):
        return remote(
            dctx_own.at[pg, :, of_half(0, 1 - core)], dctx.at[pg, core], mate_send.at[pg],
            mate_recv.at[pg], mate,
        )

    greet(ways.everyone() if summed else [mate, side])
    mate_copy(0).start()
    own_copy(0).start()
    for copy in loads(0):
        copy.start()
    p_load(0, 0).start()
    if summed:
        down_copy = pltpu.make_async_copy(down_in, down_held, down_load)
        down_copy.start()
        early = EarlySum(ways, early_held, early_got, early_sems)
        down = EarlySum(ways, down_held, down_got, down_sems)
        small = SmallSum(ways, small_value, small_got, small_sems)
        tiny = SmallSum(ways, tiny_value, tiny_got, tiny_sems)

        def late(hp):
            return LateSum(ways, hp, late_packed, late_held, late_got, late_out, late_sems)

        early.halve_cores(early_in, early_mates, core_sems)
        down_copy.wait()
        down.send(2)
        down.send(3)
        small_value[0] = small_in[...]
        small.start()
    for pg in range(pages):
        if pg > 0:
            mate_copy(pg).start()
            own_copy(pg).start()
            for copy in loads(pg):
                copy.start()
        for hp in range(pairs):
            if pg + hp > 0:
                p_load(hp, pg).start()
    for copy in w_loads:
        copy.start()
    for e in range(2):
        box_t[e] = jnp.zeros_like(box_t[e])
        box_t[e, :, e * head : (e + 1) * head] = box_w[...].astype(f32).T.astype(low)
    g_box[...] = jnp.zeros_like(g_box)

    def take(pg):
        for copy in loads(pg):
            copy.wait()
        at = pl.ds(pl.multiple_of(pg * keys, LANES), keys)
        x_t[:, at] = x[pg].reshape(keys, width).T
        own_copy(pg).wait()
        mate_copy(pg).wait_recv()

    def one_pair(pg, hp):
        lanes = pl.ds(pl.multiple_of(hp * LANES, LANES), LANES)
        p_load(hp, pg).wait()
        both = sc[pg]
        cosine2, sine2 = turned(both)
        flat = both.T
        sine_t, cosine_t = flat[:head, :chip], flat[head:, :chip]
        basis = both.astype(low)
        basis_t = flat.astype(low)
        q_pair, k_pair, v_pair = q[pg, hp], k[pg, hp], v[pg, hp]
        q_t, k_t = q_pair.T, k_pair.T
        dc = dctx[pg, :, :, lanes].reshape(chip, LANES)
        left = lane_halves((chip, LANES))
        zero = jnp.zeros_like(dc)
        dk, dv, dqs = 0.0, 0.0, []
        for e in range(2):
            mine = left if e == 0 else jnp.logical_not(left)
            own_rows = slice(e * head, (e + 1) * head)
            p = probs[pg, hp, e]
            dc_own = jnp.where(mine, dc, zero)
            q_own = jnp.where(mine, q_pair, zero)
            dp = dot_nt(v_pair, dc_own)
            p_wide = p.astype(f32)
            delta = jnp.sum(p_wide * dp, axis=0, keepdims=True)
            ds = (p_wide * (dp - delta)).astype(low)
            dv = dv + dot(p, dc_own)
            dk_feat = dot(ds, jnp.concatenate([q_own, basis[:chip]], 1)) * scale
            dq_feat = dot(jnp.concatenate([k_t[own_rows], basis_t], 0), ds) * scale
            dk_proj = rotate_key(dk_feat[:, LANES:], cosine2, sine2).astype(low)
            a, b = dq_feat[head : 2 * head], dq_feat[2 * head :]
            dq_proj = jnp.concatenate(
                [a * cosine_t - b * sine_t, a * sine_t + b * cosine_t], 0
            ).astype(low)
            dk = dk + dk_feat[:, :LANES] + dot(dk_proj, box_t[e])
            dqs.append(dq_feat[:head] + dot(box_w[...], dq_proj))
            g_box[...] += dot(k_t[own_rows], dk_proj) + dot_nt(q_t[own_rows], dq_proj)
        at = pl.ds(pl.multiple_of(pg * keys, LANES), keys)
        at_q = pl.ds(pl.multiple_of(pg * chip, LANES), chip)
        dq[hp, at_q] = jnp.concatenate(dqs, 0).T.astype(low)
        dkv[hp, at, :LANES] = dk.astype(low)
        dkv[hp, at, LANES:] = dv.astype(low)

    def pair_grads(hp):
        dkv_all = dkv[hp]
        dq_all = dq[hp]
        g_kv = column_sum(dkv_all.astype(f32))
        g_bias[pl.ds(hp, 1)] = column_sum(dq_all.astype(f32))
        g_bias[pl.ds(hp + pairs, 1)] = g_kv[:, :LANES]
        g_bias[pl.ds(hp + 2 * pairs, 1)] = g_kv[:, LANES:]
        grad = dot(x_t[...], dkv_all).astype(low)
        x_q = jnp.concatenate([x_t[:, pg * keys : pg * keys + chip] for pg in range(pages)], 1)
        grad_q = dot(x_q, dq_all).astype(low)
        late_packed[hp, 0] = grad_q.reshape(8, shard, LANES)
        late_packed[hp, 1] = grad[:, :LANES].reshape(8, shard, LANES)
        late_packed[hp, 2] = grad[:, LANES:].reshape(8, shard, LANES)

    def core_copy(pg, at):
        return remote(
            dx.at[pg, at, 1 - core], dx_mate.at[pg, at], core_send.at[pg, at], core_recv.at[pg, at],
            mate,
        )

    def side_copy(pg):
        return remote(dx.at[pg, 1, core], dx_side.at[pg], side_send.at[pg], side_recv.at[pg], side)

    def input_part(pg):
        for at in (1, 0):
            rows = pl.ds(pl.multiple_of(pg * keys + at * chip, LANES), chip)
            dks = jnp.concatenate([dkv[hp, rows, :LANES] for hp in range(pairs)], 1)
            dvs = jnp.concatenate([dkv[hp, rows, LANES:] for hp in range(pairs)], 1)
            total = dot_nt(dks, w_c[1]) + dot_nt(dvs, w_c[2])
            if at == 0:
                rows_q = pl.ds(pl.multiple_of(pg * chip, LANES), chip)
                dqs = jnp.concatenate([dq[hp, rows_q] for hp in range(pairs)], 1)
                total = total + dot_nt(dqs, w_c[0])
            dx[pg, at] = total.astype(low).reshape(2, block, width)
            core_copy(pg, at).start()

    def pass_input(pg):
        core_copy(pg, 1).wait_recv()
        dx[pg, 1, core] = dx[pg, 1, core] + dx_mate[pg, 1]
        side_copy(pg).start()

    def early_step(at):
        if not summed:
            return
        if at == 1:
            down.receive(2)
            down.receive(3)
            down.send(4)
            early.add_core(0)
            early.send(0)
            early.add_core(1)
            early.send(1)
            early.add_core(2)
            early.add_core(3)
        elif at == 2:
            down.receive(4)
            down.send(5)
        elif at == 3:
            small.advance(0)
        elif at == 4:
            early.receive(0)
            early.send(2)
            early.send(3)
        elif at == 5:
            early.receive(1)
            down.share(down_out, down_ends)
            small.advance(1)
        elif at == 6:
            early.receive(2)
            early.send(4)
            early.receive(3)
            down.hand_over()
        elif at == 7:
            early.receive(4)
            early.send(5)
            small.advance(2)
        elif at == 8:
            small.advance(3)

    def bias_rows():
        for part in range(3):
            for which in range(2):
                own = jnp.where(core == which, 1.0, 0.0)
                for hp in range(pairs):
                    at = part * pairs + hp
                    yield 64 + (2 * part + which) * pairs + hp, g_bias[at : at + 1] * own

    for copy in w_loads:
        copy.wait()

    @pl.loop(0, pages - 1)
    def _(pg):
        take(pg)

        @pl.when(pg > 0)
        def _():
            pass_input(pg - 1)

        @pl.loop(0, pairs)
        def _(hp):
            for at in range(pairs * (pages - 1)):

                @pl.when(pg * pairs + hp == at)
                def _(at=at):
                    early_step(at)

            one_pair(pg, hp)

        input_part(pg)

    last = pages - 1
    take(last)
    pass_input(last - 1)

    @pl.loop(0, pairs)
    def _(hp):
        for at in range(pairs):

            @pl.when(hp == at)
            def _(at=at):
                early_step(pairs * last + at)

        one_pair(last, hp)
        pair_grads(hp)
        if summed:
            late(hp).start()

            @pl.when(hp > 0)
            def _():
                late(hp - 1).advance(0)

            @pl.when(hp == 2)
            def _():
                late(0).advance(1)

    if summed:
        tiny_value[0, : 8 * 8] = g_box[...]
        tiny_value[0, 64:] = jnp.zeros((24, LANES), f32)
        for at, row in bias_rows():
            tiny_value[0, at : at + 1] = row
        tiny.start()
    input_part(last)
    if summed:
        early.share(early_out, early_ends)
        tiny.advance(0)
        late(2).advance(0)
        late(1).advance(1)
        late(0).advance(2)
        pass_input(last)
        small.advance(4)
        early.hand_over()
        tiny.advance(1)
        late(2).advance(1)
        late(1).advance(2)
        late(0).advance(3)
        tiny.advance(2)
        late(2).advance(2)
        late(1).advance(3)
        late(0).advance(4)
        tiny.advance(3)
        late(2).advance(3)
        late(1).advance(4)
        tiny.advance(4)
        late(2).advance(4)
    else:
        pass_input(last)

    for pg in range(pages):
        core_copy(pg, 0).wait_recv()
        side_copy(pg).wait_recv()
        total = dx[pg, 0, core].astype(f32) + dx_mate[pg, 0].astype(f32) + dx_side[pg].astype(f32)
        dx_out[pg] = (total + dresid1[pg]).astype(low)
        for at in range(2):
            core_copy(pg, at).wait_send()
        side_copy(pg).wait_send()
        mate_copy(pg).wait_send()
    if summed:
        small_out[...] = small_value[5]
        tiny_out[...] = tiny_value[5]
        early.end_cores()
        early.end_steps(range(6))
        early.end()
        down.end_steps((2, 3, 4, 5))
        down.end()
        for hp in range(pairs):
            late(hp).finish()
        small.finish()
        tiny.finish()
    else:
        tiny_out[:64] = g_box[...]
        tiny_out[64:] = jnp.zeros((24, LANES), f32)
        for at, row in bias_rows():
            tiny_out[at : at + 1] = row


def attend_back(dctx, x, q, k, v, sc, probs, qkv_w, box_w, dresid1, packed, down, small, summed):
    pages, pairs, chip, _ = q.shape
    keys = k.shape[2]
    width = x.shape[-1]
    block = chip // 2
    half = pairs * LANES
    shard = width // 8
    wide = packed.shape[2] // 2
    struct = jax.ShapeDtypeStruct
    vmem, dma = pltpu.VMEM, pltpu.SemaphoreType.DMA
    late_packed = (pairs, 3, 8, shard, LANES)
    tiny_rows = 88
    scratch = [
        vmem((pages, 4, block, width), low),
        vmem((pages, pairs, chip, LANES), low),
        vmem((pages, pairs, keys, LANES), low),
        vmem((pages, pairs, keys, LANES), low),
        vmem((pages, keys, LANES), f32),
        vmem((pages, pairs, 2, keys, chip), low),
        vmem((pages, 2, block, half), low),
        vmem((pairs, pages * chip, LANES), low),
        vmem((pairs, pages * keys, 2 * LANES), low),
        vmem((width, pages * keys), low),
        vmem((3, width, half), low),
        vmem((pages, 2, 2, block, width), low),
        vmem((pages, 2, block, width), low),
        vmem((pages, block, width), low),
        vmem((2, LANES, LANES), low),
        vmem(box_w.shape, f32),
        vmem((3 * pairs, LANES), f32),
    ]
    copies = [
        dma((pages, 5)), dma((pages, pairs)), dma((3,)), dma((pages,)), dma((pages,)), dma((pages,)),
        dma((pages, 2)), dma((pages, 2)), dma((pages,)), dma((pages,)),
    ]
    operands = [dctx, x, q, k, v, sc, probs, qkv_w, box_w, dresid1]
    in_specs = [any_spec()] * 8 + [vmem_spec()] * 2
    if summed:
        rest = down.shape[2]
        operands += [packed, down, small]
        in_specs += [any_spec(), any_spec(), vmem_spec()]
        outs = (
            struct((pages, block, width), low),
            struct((2, 3, 2, wide, LANES), low),
            struct((2, 3, 2, rest, LANES), low),
            struct((2, pairs, 3, 2, shard // 2, LANES), low),
            struct(small.shape, f32),
            struct((tiny_rows, LANES), f32),
        )
        scratch += [vmem(late_packed, low)] + copies
        scratch += [
            vmem((3, 16, wide, LANES), low),
            vmem((3, 16, wide, LANES), low),
            vmem((3, 15, wide, LANES), low),
            vmem((3, 8, rest, LANES), low),
            vmem((3, 7, rest, LANES), low),
            vmem((pairs, 3, 8, shard // 2, LANES), low),
            vmem((pairs, 3, 15, shard // 2, LANES), low),
            vmem((6,) + small.shape, f32),
            vmem((5,) + small.shape, f32),
            vmem((6, tiny_rows, LANES), f32),
            vmem((5, tiny_rows, LANES), f32),
        ]
        groups = len(GROUPS)
        scratch += [dma((3, 4))] * 3 + ([dma((3, groups))] * 2 + [dma((3,))] * 4) * 2 + [dma]
        scratch += [dma((pairs, 3))] * 2 + [dma((pairs, 3, 3))] * 2 + [dma((pairs, 3))] * 4
        scratch += [dma((5,))] * 4
    else:
        outs = (
            struct((pages, block, width), low),
            struct(late_packed, low),
            struct((tiny_rows, LANES), f32),
        )
        scratch += copies
    return pl.pallas_call(
        functools.partial(attend_back_kernel, summed),
        out_shape=outs,
        in_specs=in_specs,
        out_specs=(vmem_spec(),) * len(outs),
        scratch_shapes=scratch,
        compiler_params=pltpu.CompilerParams(
            collective_id=2, has_side_effects=True, vmem_limit_bytes=63 * 2**20
        ),
        name="attend_back",
    )(*operands)


def finish_kernel(
    early_in, rest_in, late_in, small_in, tiny_in, dx_in,
    up, down, out, qkv, qkv_b, box, out_b, gain1, shift1, up_b, down_b, gain2, shift2, input_grad,
    early, rest, late, small, tiny, sems,
):
    page = lax.axis_index("page")
    shard = out.shape[0]
    pieces = up.shape[1] // (6 * LANES)
    pairs = ((early_in, early), (rest_in, rest), (late_in, late), (small_in, small), (tiny_in, tiny), (dx_in, input_grad))
    copies = [pltpu.make_async_copy(src, dst, sems.at[at]) for at, (src, dst) in enumerate(pairs)]
    for copy in copies:
        copy.start()
    for copy in copies:
        copy.wait()
    for which in range(2):
        for order in range(3):
            column = which * 3 + order
            rows = early[which, order].astype(f32).reshape(-1, LANES)
            for piece in range(pieces):
                at = (column * pieces + piece) * LANES
                up[:, at : at + LANES] = rows[piece * shard : (piece + 1) * shard]
            at = column * LANES
            out[:, at : at + LANES] = rows[pieces * shard :]
            down[:, at : at + LANES] = rest[which, order].astype(f32).reshape(-1, LANES)
            for part in range(3):
                at = (part * 6 + column) * LANES
                qkv[:, at : at + LANES] = late[which, order, part].astype(f32).reshape(shard, LANES)
    rows = pltpu.roll(small[:8], lax.rem(8 * shard - page * shard, 8 * shard), 1)
    for at, ref in enumerate((gain2, shift2, down_b, gain1, shift1, out_b)):
        ref[...] = rows[at, :shard]
    flat = jnp.concatenate([small[8 + at : 9 + at, : pieces * LANES] for at in range(6)], 1)
    every = flat.shape[1]
    flat = pltpu.roll(flat, lax.rem(every - page * up_b.shape[0], every), 1)
    up_b[...] = flat[0, : up_b.shape[0]]
    box[...] = tiny[pl.ds(pl.multiple_of(page * 8, 8), 8)]
    count = qkv_b.shape[0]
    first = page * count
    parts = [tiny[pl.ds(64 + first // LANES + piece, 1)] for piece in range(4)]
    rest = lax.rem(first, LANES)
    row = pltpu.roll(jnp.concatenate(parts, 1), lax.rem(4 * LANES - rest, 4 * LANES), 1)
    qkv_b[...] = row[0, :count]


def finish(early, rest, late, small, tiny, dx):
    struct = jax.ShapeDtypeStruct
    shapes = (
        (96, 3072), (384, 768), (96, 768), (96, 2304), (288,), (8, LANES), (96,), (96,), (96,), (384,), (96,), (96,), (96,),
    )
    operands = (early, rest, late, small, tiny, dx)
    return pl.pallas_call(
        finish_kernel,
        out_shape=tuple(struct(shape, f32) for shape in shapes) + (struct(dx.shape, low),),
        in_specs=[any_spec()] * 6,
        out_specs=(vmem_spec(),) * 14,
        scratch_shapes=[pltpu.VMEM(operand.shape, operand.dtype) for operand in operands[:5]]
        + [pltpu.SemaphoreType.DMA((6,))],
        compiler_params=pltpu.CompilerParams(vmem_limit_bytes=63 * 2**20),
        name="finish",
    )(*operands)


def reduce_by_collectives(packed, packed_down, packed_qkv, vectors):
    core = lax.axis_index("blk") % 2
    up = packed[:, :, :384].reshape(6, 8, 4, 96, LANES).transpose(1, 3, 0, 2, 4).reshape(768, 3072)
    down = packed_down.transpose(1, 2, 0, 3).reshape(3072, 768)
    out = packed[:, :, 384:].transpose(1, 2, 0, 3).reshape(768, 768)
    own = packed_qkv.transpose(2, 3, 1, 0, 4).reshape(768, 3, 384)
    qkv = jnp.zeros((768, 3, 2, 384), low)
    qkv = lax.dynamic_update_slice(qkv, own[:, :, None], (0, 0, core, 0)).reshape(768, 2304)
    grads = jax.tree.map(lambda g: g.astype(f32), (qkv, out, up, down, *vectors))
    page_sums = tuple(
        lax.psum_scatter(grad, "page", scatter_dimension=0, tiled=True) for grad in grads
    )
    return jax.tree.map(
        lambda part: part.astype(f32), lax.psum(jax.tree.map(lambda g: g.astype(low), page_sums), "blk")
    )


def local(
    tokens, lengths, boxes, qkv_weight, qkv_bias, box_weight, out_weight, out_bias, norm1_gain,
    norm1_bias, up_weight, up_bias, down_weight, down_bias, norm2_gain, norm2_bias, cotangent,
):
    pages, block, width = tokens.shape
    rows = pages * block
    x, q, k, v, sc, probs, ctx = attend(tokens, boxes, lengths, qkv_weight, qkv_bias, box_weight)
    summed = lax.axis_size("page") == 8
    output, dresid1, dctx, packed, small, down = feed(
        ctx.reshape(rows, width), tokens.reshape(rows, width), cotangent.reshape(rows, width),
        out_weight, up_weight, down_weight,
        (out_bias, norm1_gain, norm1_bias, up_bias, down_bias, norm2_gain, norm2_bias), summed,
    )
    parts = attend_back(
        dctx.reshape(pages, block, width), x, q, k, v, sc, probs, qkv_weight, box_weight,
        dresid1.reshape(pages, block, width), packed, down, small, summed,
    )
    output = output.reshape(pages, block, width)
    if summed:
        dx, early, rest, late, small, tiny = parts
        (
            up_w, down_w, out_w, qkv_w, qkv_b, box, out_b, gain1, shift1, up_b, down_b, gain2, shift2, input_grad,
        ) = finish(early, rest, late, small, tiny, dx)
        box = box.reshape(-1)
    else:
        input_grad, packed_qkv, tiny = parts
        vectors = (
            tiny[64:82].reshape(-1), tiny[:64].reshape(-1), small[5], small[3], small[4],
            small[8:14, :512].reshape(-1), small[2], small[0], small[1],
        )
        (
            qkv_w, out_w, up_w, down_w, qkv_b, box, out_b, gain1, shift1, up_b, down_b, gain2, shift2,
        ) = reduce_by_collectives(packed, down, packed_qkv, vectors)
    return (
        output, input_grad, qkv_w, qkv_b, box, out_w, out_b, gain1, shift1, up_w, up_b, down_w, down_b, gain2, shift2,
    )


def solution(mesh):
    return jax.shard_map(
        local,
        mesh=mesh,
        in_specs=(
            P("page", "blk", None),
            P("page"),
            P("page", "blk", None),
            P(),
            P(),
            P(),
            P(),
            P(),
            P(),
            P(),
            P(),
            P(),
            P(),
            P(),
            P(),
            P(),
            P("page", "blk", None),
        ),
        out_specs=(
            P("page", "blk", None),
            P("page", "blk", None),
            P("page", None),
            P("page"),
            P("page"),
            P("page", None),
            P("page"),
            P("page"),
            P("page"),
            P("page", None),
            P("page"),
            P("page", None),
            P("page"),
            P("page"),
            P("page"),
        ),
        check_vma=False,
    )
```

```python
import functools

import jax
import jax.numpy as jnp
import numpy as np
from jax import lax
from jax.experimental import pallas as pl
from jax.experimental.pallas import tpu as pltpu
from jax.sharding import PartitionSpec as P

norm_eps = 1e-12
MESH = pl.DeviceIdType.MESH
LANES = 128
low = jnp.bfloat16
f32 = jnp.float32


def core_of(blk):
    return blk + 1 - 2 * (blk % 2)


def side_of(blk):
    return (blk + 2) % 4


def greet(others):
    barrier = pltpu.get_barrier_semaphore()
    for other in others:
        pl.semaphore_signal(barrier, inc=1, device_id=other, device_id_type=MESH)
    pl.semaphore_wait(barrier, len(others))


def remote(src, dst, send_sem, recv_sem, to):
    return pltpu.make_async_remote_copy(
        src_ref=src, dst_ref=dst, send_sem=send_sem, recv_sem=recv_sem, device_id=to,
        device_id_type=MESH,
    )


def dot(a, b):
    return jnp.dot(a, b, preferred_element_type=f32)


def dot_nt(a, b):
    return lax.dot_general(a, b, (((1,), (1,)), ((), ())), preferred_element_type=f32)


def dot_tn(a, b):
    return lax.dot_general(a, b, (((0,), (0,)), ((), ())), preferred_element_type=f32)


def sin_cos(theta):
    turns = jnp.floor(theta * 0.6366197723675814 + 0.5)
    rest = theta - turns * 1.5703125
    rest = rest - turns * 4.837512969970703125e-4
    rest = rest - turns * 7.54978995489188216e-8
    square = rest * rest
    sine = ((-1.9515295891e-4 * square + 8.3321608736e-3) * square - 1.6666654611e-1) * square
    sine = sine * rest + rest
    cosine = (2.443315711809948e-5 * square - 1.388731625493765e-3) * square + 4.166664568298827e-2
    cosine = cosine * square * square - 0.5 * square + 1.0
    quarter = turns.astype(jnp.int32)
    odd = (quarter & 1) == 1
    sine_at = jnp.where(odd, cosine, sine)
    cosine_at = jnp.where(odd, sine, cosine)
    sine_at = jnp.where((quarter & 2) == 2, -sine_at, sine_at)
    cosine_at = jnp.where(((quarter + 1) & 2) == 2, -cosine_at, cosine_at)
    return sine_at, cosine_at


def lane_halves(shape):
    return lax.broadcasted_iota(jnp.int32, shape, 1) < LANES // 2


def turned(both):
    swapped = pltpu.roll(both, LANES // 2, 1)
    left = lane_halves(both.shape)
    return jnp.where(left, -swapped, both), jnp.where(left, both, swapped)


def rotate_key(proj, cosine2, sine2):
    return proj * cosine2 + pltpu.roll(proj, LANES // 2, 1) * sine2


def attend_kernel(
    tokens, boxes, lengths, freq, qkv_w, qkv_b, box_w,
    x_t_out, q_out, k_out, v_out, sc_out, p_out, ctx_out,
    x, x_t, box, w_q, w_kv, q, k, v, sc, probs, ctx, box2,
    own_sem, w_sem, out_sem, p_sem, ctx_sem,
    mate_send, mate_recv, side_send, side_recv, pass_send, pass_recv, ctx_send, ctx_recv,
):
    page, blk = lax.axis_index("page"), lax.axis_index("blk")
    core, side_at = blk % 2, blk // 2
    mate, side = (page, core_of(blk)), (page, side_of(blk))
    pages = tokens.shape[0]
    half = w_q.shape[1]
    pairs = half // LANES
    chip = 2 * tokens.shape[1]
    keys = 2 * chip
    scale = 0.125

    def of_half(part):
        return pl.ds(pl.multiple_of(part * 2 * half + core * half, LANES), half)

    loads = [
        pltpu.make_async_copy(qkv_w.at[:, of_half(0)], w_q, w_sem.at[0]),
        pltpu.make_async_copy(qkv_w.at[:, of_half(1)], w_kv.at[:, :half], w_sem.at[1]),
        pltpu.make_async_copy(qkv_w.at[:, of_half(2)], w_kv.at[:, half:], w_sem.at[2]),
    ]
    own = []
    for pg in range(pages):
        own.append(pltpu.make_async_copy(tokens.at[pg], x.at[pg, core], own_sem.at[pg, 0]))
        own.append(pltpu.make_async_copy(boxes.at[pg], box.at[pg, core], own_sem.at[pg, 1]))
    for copy in own:
        copy.start()
    for copy in loads:
        copy.start()
    greet((mate, side))
    to_mate, to_side = [], []
    for pg in range(pages):
        for which, (src, dst) in enumerate(((tokens, x), (boxes, box))):
            to_side.append(
                remote(src.at[pg], dst.at[pg, 2 + core], side_send.at[pg, which], side_recv.at[pg, which], side)
            )
            to_side[-1].start()
            to_mate.append(
                remote(src.at[pg], dst.at[pg, core], mate_send.at[pg, which], mate_recv.at[pg, which], mate)
            )
            to_mate[-1].start()
    zero = jnp.zeros_like(box_w)
    box2[...] = jnp.concatenate(
        [jnp.concatenate([box_w[...], zero], 1), jnp.concatenate([zero, box_w[...]], 1)], 0
    )

    def bias_of(part):
        both = [
            qkv_b[(2 * part + which) * half : (2 * part + which + 1) * half].reshape(1, half)
            for which in range(2)
        ]
        return jnp.where(core == 0, both[0], both[1])

    for copy in loads:
        copy.wait()

    @pl.loop(0, pages)
    def _(pg):
        passed = []
        for which, (src, dst) in enumerate(((tokens, x), (boxes, box))):
            remote(
                src.at[pg], dst.at[pg, 2 + core], side_send.at[pg, which], side_recv.at[pg, which], side
            ).wait_recv()
            copy = remote(
                dst.at[pg, 2 + core], dst.at[pg, 2 + core], pass_send.at[pg, which],
                pass_recv.at[pg, which], mate,
            )
            copy.start()
            passed.append(copy)
            pltpu.make_async_copy(src.at[pg], dst.at[pg, core], own_sem.at[pg, which]).wait()
            remote(
                src.at[pg], dst.at[pg, core], mate_send.at[pg, which], mate_recv.at[pg, which], mate
            ).wait_recv()
        for copy in passed:
            copy.wait_recv()
        for at in range(4):
            rows = box[pg, at]
            spread = [
                jnp.broadcast_to(rows[c : c + 1], (freq.shape[0] // 4, LANES)) for c in range(4)
            ]
            sine, cosine = sin_cos(jnp.concatenate(spread, 0) * freq[...])
            sc[pg, at * LANES : (at + 1) * LANES] = jnp.concatenate([sine, cosine], 0).T
        pltpu.make_async_copy(sc.at[pg], sc_out.at[pg], out_sem.at[pg, 1]).start()
        x_all = x[pg].reshape(keys, x.shape[-1])
        x_t[pg] = x_all.T
        pltpu.make_async_copy(x_t.at[pg], x_t_out.at[pg], out_sem.at[pg, 0]).start()
        q_all = (dot(x_all[:chip], w_q[...]) + bias_of(0)).astype(low)
        bias = jnp.concatenate([bias_of(1), bias_of(2)], 1)
        kv_all = (dot(x_all, w_kv[...]) + bias).astype(low)
        for hp in range(pairs):
            q[pg, hp] = q_all[:, hp * LANES : (hp + 1) * LANES]
            k[pg, hp] = kv_all[:, hp * LANES : (hp + 1) * LANES]
            v[pg, hp] = kv_all[:, half + hp * LANES : half + (hp + 1) * LANES]
        for which, (src, dst) in enumerate(((q, q_out), (k, k_out), (v, v_out))):
            pltpu.make_async_copy(src.at[pg], dst.at[pg], out_sem.at[pg, 2 + which]).start()
        place = lax.broadcasted_iota(jnp.int32, (keys, chip), 0) + side_at * chip
        place = jnp.where(place >= keys, place - keys, place)
        valid = place < lengths[pg]

        @pl.loop(0, pairs)
        def _(hp):
            both = sc[pg]
            cosine2, sine2 = turned(both)
            basis = both.astype(low)
            basis_q = (both[:chip] * scale).astype(low)
            left = lane_halves((chip, LANES))
            cosine_q = jnp.where(left, -cosine2[:chip], cosine2[:chip]) * scale
            sine_q = jnp.where(left, sine2[:chip], -sine2[:chip]) * scale
            q_pair, k_pair = q[pg, hp], k[pg, hp]
            q_proj = dot(q_pair, box2[...])
            k_proj = dot(k_pair, box2[...])
            v_t = v[pg, hp].T
            outs = []
            for e in range(2):
                at = slice(e * LANES, (e + 1) * LANES)
                q_pos = rotate_key(q_proj[:, at], cosine_q, sine_q).astype(low)
                k_pos = rotate_key(k_proj[:, at], cosine2, sine2).astype(low)
                mine = left if e == 0 else jnp.logical_not(left)
                q_own = jnp.where(mine, q_pair.astype(f32) * scale, 0.0).astype(low)
                scores = dot_nt(
                    jnp.concatenate([basis, k_pos], 1), jnp.concatenate([q_pos, basis_q], 1)
                )
                scores = scores + dot_nt(k_pair, q_own)
                scores = jnp.where(valid, scores, -1e30)
                top = jnp.max(scores, axis=0, keepdims=True)
                grown = jnp.exp(scores - top)
                total = jnp.sum(grown, axis=0, keepdims=True)
                p = (grown * (1.0 / total)).astype(low)
                probs[pg, hp, e] = p
                outs.append(dot(v_t[e * LANES // 2 : (e + 1) * LANES // 2], p))
            pltpu.make_async_copy(probs.at[pg, hp], p_out.at[pg, hp], p_sem.at[pg, hp]).start()
            context = jnp.concatenate(outs, 0).T.astype(low)
            lanes = pl.ds(pl.multiple_of(hp * LANES, LANES), LANES)
            ctx[pg, 0, :, lanes] = context[: chip // 2]
            ctx[pg, 1, :, lanes] = context[chip // 2 :]

        mine = pl.ds(pl.multiple_of(core * half, LANES), half)
        pltpu.make_async_copy(ctx.at[pg, core], ctx_out.at[pg, :, mine], ctx_sem.at[pg]).start()
        remote(
            ctx.at[pg, 1 - core], ctx_out.at[pg, :, mine], ctx_send.at[pg], ctx_recv.at[pg], mate
        ).start()
        for copy in passed:
            copy.wait_send()

    mine = pl.ds(pl.multiple_of(core * half, LANES), half)
    for pg in range(pages):
        for which, (src, dst) in enumerate(((x_t, x_t_out), (sc, sc_out), (q, q_out), (k, k_out), (v, v_out))):
            pltpu.make_async_copy(src.at[pg], dst.at[pg], out_sem.at[pg, which]).wait()
        for hp in range(pairs):
            pltpu.make_async_copy(probs.at[pg, hp], p_out.at[pg, hp], p_sem.at[pg, hp]).wait()
        pltpu.make_async_copy(ctx.at[pg, core], ctx_out.at[pg, :, mine], ctx_sem.at[pg]).wait()
        remote(
            ctx.at[pg, 1 - core], ctx_out.at[pg, :, mine], ctx_send.at[pg], ctx_recv.at[pg], mate
        ).wait()
    for copy in to_side + to_mate:
        copy.wait_send()


def any_spec():
    return pl.BlockSpec(memory_space=pl.ANY)


def vmem_spec():
    return pl.BlockSpec(memory_space=pltpu.VMEM)


def attend(tokens, boxes, lengths, qkv_w, qkv_b, box_weight):
    pages, block, width = tokens.shape
    head_dim, pos = box_weight.shape
    half = width // 2
    pairs = half // LANES
    chip, keys = 2 * block, 4 * block
    count = pos // 8
    freqs = 10000.0 ** (-np.arange(count) / count)
    freq = jnp.asarray(np.tile(np.tile(freqs, 4)[:, None], (1, LANES)), f32)
    boxes_t = boxes.astype(f32).transpose(0, 2, 1)
    struct = jax.ShapeDtypeStruct
    vmem, dma = pltpu.VMEM, pltpu.SemaphoreType.DMA
    return pl.pallas_call(
        attend_kernel,
        out_shape=(
            struct((pages, width, keys), low),
            struct((pages, pairs, chip, LANES), low),
            struct((pages, pairs, keys, LANES), low),
            struct((pages, pairs, keys, LANES), low),
            struct((pages, keys, LANES), f32),
            struct((pages, pairs, 2, keys, chip), low),
            struct((pages, block, width), low),
        ),
        in_specs=[any_spec(), any_spec(), pl.BlockSpec(memory_space=pltpu.SMEM), vmem_spec(), any_spec(), vmem_spec(), vmem_spec()],
        out_specs=(any_spec(),) * 7,
        scratch_shapes=[
            vmem((pages, 4, block, width), low),
            vmem((pages, width, keys), low),
            vmem((pages, 4, 4, LANES), f32),
            vmem((width, half), low),
            vmem((width, 2 * half), low),
            vmem((pages, pairs, chip, LANES), low),
            vmem((pages, pairs, keys, LANES), low),
            vmem((pages, pairs, keys, LANES), low),
            vmem((pages, keys, LANES), f32),
            vmem((pages, pairs, 2, keys, chip), low),
            vmem((pages, 2, block, half), low),
            vmem((2 * head_dim, 2 * pos), low),
            dma((pages, 2)), dma((3,)), dma((pages, 5)), dma((pages, pairs)), dma((pages,)),
            dma((pages, 2)), dma((pages, 2)), dma((pages, 2)), dma((pages, 2)),
            dma((pages, 2)), dma((pages, 2)), dma((pages,)), dma((pages,)),
        ],
        compiler_params=pltpu.CompilerParams(
            collective_id=1, has_side_effects=True, vmem_limit_bytes=56 * 2**20
        ),
        name="attend",
    )(tokens, boxes_t, lengths, freq, qkv_w, qkv_b, box_weight)


ORDERS = ("xaym", "ayxm", "yxam")
GROUPS = ((12, 16), (8, 12), (6, 8), (4, 6), (2, 4), (1, 2))


def flip(page, way):
    x, z = page % 2, page // 2
    if way == "x":
        return z * 2 + (1 - x)
    if way == "a":
        return (z + 1 - 2 * (z % 2)) * 2 + x
    return ((z + 2) % 4) * 2 + x


class Ways:
    def __init__(self):
        self.page, self.blk = lax.axis_index("page"), lax.axis_index("blk")
        self.core, self.half = self.blk % 2, self.blk // 2
        self.mate, self.side = (self.page, core_of(self.blk)), (self.page, side_of(self.blk))

    def partner(self, way):
        return self.side if way == "y" else (flip(self.page, way), self.blk)

    def piece(self, order, code):
        page, half = self.page, self.half
        for place, way in enumerate(ORDERS[order]):
            if code >> (3 - place) & 1:
                if way == "y":
                    half = 1 - half
                else:
                    page = flip(page, way)
        return page, half

    def everyone(self):
        return [self.partner(way) for way in "xamy"] + [self.mate]


def step_of(code):
    return 4 - code.bit_length()


class EarlySum:
    def __init__(self, ways, packed, mates, got, final, sems):
        self.ways, self.packed, self.mates, self.got, self.final = ways, packed, mates, got, final
        (self.core_send, self.core_recv, self.send_sem, self.recv_sem, self.last_send, self.last_recv,
         self.end_send, self.end_recv) = sems
        self.rows = packed.shape[2] // 2

    slices = ((12, 16), (8, 12), (4, 8), (0, 4))

    def place(self, order, code, core, begin=0, end=None):
        page, half = self.ways.piece(order, code)
        count = (self.rows if end is None else end) - begin
        return 3 * core + order, page, pl.ds(pl.multiple_of(half * self.rows + begin, 16), count)

    def swap(self, orders, begin=0, end=None):
        ways = self.ways
        for at, (first, last) in enumerate(self.slices):
            for code in range(first, last):
                for order in orders:
                    remote(
                        self.packed.at[self.place(order, code, 1 - ways.core, begin, end)],
                        self.mates.at[order, code, begin:end], self.core_send.at[order, at],
                        self.core_recv.at[order, at], ways.mate,
                    ).start()

    def core_group(self, order, at):
        begin, end = self.slices[at]
        part = self.mates.at[order, begin:end]
        return remote(part, part, self.core_send.at[order, at], self.core_recv.at[order, at], self.ways.mate)

    def add_core(self, at):
        for order in range(3):
            self.core_group(order, at).wait_recv()
            for code in range(*self.slices[at]):
                place = self.place(order, code, self.ways.core)
                self.packed[place] = self.packed[place] + self.mates[order, code]

    def group(self, order, group):
        begin, end = GROUPS[group]
        part = self.got.at[order, begin - 1 : end - 1]
        way = ORDERS[order][step_of(begin)]
        return remote(
            part, part, self.send_sem.at[order, group], self.recv_sem.at[order, group], self.ways.partner(way)
        )

    def send(self, group):
        begin, end = GROUPS[group]
        for code in range(begin, end):
            for order in range(3):
                remote(
                    self.packed.at[self.place(order, code, self.ways.core)], self.got.at[order, code - 1],
                    self.send_sem.at[order, group], self.recv_sem.at[order, group],
                    self.ways.partner(ORDERS[order][step_of(begin)]),
                ).start()

    def receive(self, group):
        begin, end = GROUPS[group]
        base = 1 << (begin.bit_length() - 1)
        for order in range(3):
            self.group(order, group).wait_recv()
            for code in range(begin, end):
                place = self.place(order, code - base, self.ways.core)
                self.packed[place] = self.packed[place] + self.got[order, code - 1]

    def share(self):
        for order in range(3):
            self.group(order, 5).wait_recv()
            place = self.place(order, 0, self.ways.core)
            self.final[self.ways.core, order, self.ways.half] = self.packed[place] + self.got[order, 0]
            self.last_copy(order).start()

    def last_copy(self, order):
        part = self.final.at[self.ways.core, order, self.ways.half]
        return remote(part, part, self.last_send.at[order], self.last_recv.at[order], self.ways.side)

    def end_copy(self, order):
        part = self.final.at[self.ways.core, order]
        return remote(part, part, self.end_send.at[order], self.end_recv.at[order], self.ways.mate)

    def hand_over(self):
        for order in range(3):
            self.last_copy(order).wait_recv()
            self.end_copy(order).start()

    def end(self):
        for order in range(3):
            self.end_copy(order).wait()
            self.last_copy(order).wait_send()
            for at in range(4):
                self.core_group(order, at).wait_send()
            for group in range(len(GROUPS)):
                self.group(order, group).wait_send()


class LateSum:
    def __init__(self, ways, hp, packed, held, got, final, sems):
        self.ways, self.hp = ways, hp
        self.packed, self.held, self.got, self.final = packed, held, got, final
        (self.first_send, self.first_recv, self.send_sem, self.recv_sem, self.last_send, self.last_recv,
         self.end_send, self.end_recv) = sems
        self.rows = held.shape[3]

    def start(self):
        ways, hp = self.ways, self.hp
        for code in range(8, 16):
            for order in range(3):
                page, half = ways.piece(order, code)
                rows = pl.ds(pl.multiple_of(half * self.rows, 16), self.rows)
                remote(
                    self.packed.at[hp, order, page, rows], self.got.at[hp, order, code - 1],
                    self.first_send.at[hp, order], self.first_recv.at[hp, order],
                    ways.partner(ORDERS[order][0]),
                ).start()

    def first(self, order):
        part = self.got.at[self.hp, order, 7:15]
        return remote(
            part, part, self.first_send.at[self.hp, order], self.first_recv.at[self.hp, order],
            self.ways.partner(ORDERS[order][0]),
        )

    def copy(self, order, step):
        begin, end = 8 >> step, 16 >> step
        return remote(
            self.held.at[self.hp, order, begin:end], self.got.at[self.hp, order, begin - 1 : end - 1],
            self.send_sem.at[self.hp, order, step - 1], self.recv_sem.at[self.hp, order, step - 1],
            self.ways.partner(ORDERS[order][step]),
        )

    def advance(self, step):
        ways, hp = self.ways, self.hp
        for order in range(3):
            if step == 0:
                self.first(order).wait_recv()
                for code in (4, 5, 6, 7, 0, 1, 2, 3):
                    page, half = ways.piece(order, code)
                    rows = pl.ds(pl.multiple_of(half * self.rows, 16), self.rows)
                    self.held[hp, order, code] = self.packed[hp, order, page, rows] + self.got[hp, order, code + 7]
                    if code == 7:
                        self.copy(order, 1).start()
            elif step < 3:
                self.copy(order, step).wait_recv()
                count = 8 >> step
                self.held[hp, order, :count] = (
                    self.held[hp, order, :count] + self.got[hp, order, count - 1 : 2 * count - 1]
                )
                self.copy(order, step + 1).start()
            elif step == 3:
                self.copy(order, 3).wait_recv()
                self.final[ways.core, hp, order, ways.half] = self.held[hp, order, 0] + self.got[hp, order, 0]
                self.last_copy(order).start()
            else:
                self.last_copy(order).wait_recv()
                self.end_copy(order).start()

    def last_copy(self, order):
        part = self.final.at[self.ways.core, self.hp, order, self.ways.half]
        return remote(
            part, part, self.last_send.at[self.hp, order], self.last_recv.at[self.hp, order], self.ways.side
        )

    def end_copy(self, order):
        part = self.final.at[self.ways.core, self.hp, order]
        return remote(
            part, part, self.end_send.at[self.hp, order], self.end_recv.at[self.hp, order], self.ways.mate
        )

    def finish(self):
        for order in range(3):
            self.end_copy(order).wait()
            self.last_copy(order).wait_send()
            self.first(order).wait_send()
            for step in (1, 2, 3):
                self.copy(order, step).wait_send()


class SmallSum:
    def __init__(self, ways, value, got, sems):
        self.ways, self.value, self.got = ways, value, got
        self.send_sem, self.recv_sem = sems
        self.to = ways.everyone()

    def copy(self, step):
        return remote(
            self.value.at[step], self.got.at[step], self.send_sem.at[step], self.recv_sem.at[step], self.to[step]
        )

    def start(self):
        self.copy(0).start()

    def advance(self, step):
        self.copy(step).wait_recv()
        self.value[step + 1] = self.value[step] + self.got[step]
        if step < 4:
            self.copy(step + 1).start()

    def finish(self):
        for step in range(5):
            self.copy(step).wait_send()


def norm_of(resid):
    center = resid - jnp.mean(resid, axis=-1, keepdims=True)
    spread = jnp.mean(center * center, axis=-1, keepdims=True)
    inverse = lax.rsqrt(spread + norm_eps)
    return center * inverse, inverse


def norm_back(grad, normed, inverse):
    mean = jnp.mean(grad, axis=-1, keepdims=True)
    along = jnp.mean(grad * normed, axis=-1, keepdims=True)
    return inverse * (grad - mean - normed * along)


def column_sum(values):
    return jnp.sum(values, axis=0, keepdims=True)


def middle_kernel(
    summed, ctx_in, tokens_in, cotangent_in, out_w, up_w, down_w, out_b, gain1, shift1, up_b, down_b, gain2, shift2,
    x_t_in, q_in, k_in, v_in, sc_in, p_in, qkv_w, box_w, *refs
):
    if summed:
        (
            layer_out, dx_out, early_out, down_out, late_out, small_out, tiny_out,
            dresid1, dctx_own, dctx, dx_mate, dx_side,
            own_sem, mate_send, mate_recv, core_send, core_recv, side_send, side_recv,
            packed_down, packed, down_mates, early_mates, down_got, early_got, late_got,
            small_value, small_got, tiny_value, tiny_got, *sems,
        ) = refs
        down_sems, early_sems, late_sems, small_sems, tiny_sems = sems[:8], sems[8:16], sems[16:24], sems[24:26], sems[26:]
        g_rows = small_value.at[0]
    else:
        (
            layer_out, dx_out, packed_down, packed, late_out, g_rows, tiny_out,
            dresid1, dctx_own, dctx, dx_mate, dx_side,
            own_sem, mate_send, mate_recv, core_send, core_recv, side_send, side_recv,
        ) = refs
    ways = Ways()
    core, mate, side = ways.core, ways.mate, ways.side
    greet(ways.everyone() if summed else [mate, side])
    pages, block, width = dctx_own.shape
    half = width // 2
    pairs = half // LANES
    chip, keys = 2 * block, 4 * block
    shard = width // 8
    head = LANES // 2
    scale = 0.125
    chunks = 6
    chunk = up_w.shape[1] // chunks
    up_pieces = chunk // LANES
    if summed:
        down = EarlySum(ways, packed_down, down_mates, down_got, down_out, down_sems)
        early = EarlySum(ways, packed, early_mates, early_got, early_out, early_sems)
        small = SmallSum(ways, small_value, small_got, small_sems)
        tiny = SmallSum(ways, tiny_value, tiny_got, tiny_sems)
        first_chunk = chunks // 2 * (1 - core)
    else:
        first_chunk = 0

    def row(ref):
        return ref[...].reshape(1, -1)

    def of_half(part, which):
        return pl.ds(pl.multiple_of(part * 2 * half + which * half, LANES), half)

    def own_copy(pg):
        return pltpu.make_async_copy(
            dctx_own.at[pg, :, of_half(0, core)], dctx.at[pg, core], own_sem.at[pg]
        )

    def mate_copy(pg):
        return remote(
            dctx_own.at[pg, :, of_half(0, 1 - core)], dctx.at[pg, core], mate_send.at[pg],
            mate_recv.at[pg], mate,
        )

    def send_dctx():
        for pg in range(pages):
            mate_copy(pg).start()
            own_copy(pg).start()

    def feed_step(at):
        if not summed:
            return
        if at == 1:
            down.add_core(0)
            down.send(0)
        elif at == 3:
            down.add_core(1)
            down.send(1)
            down.add_core(2)
            down.add_core(3)

    def back_step(at):
        if not summed:
            return
        if at == 0:
            down.receive(0)
            down.send(2)
            down.send(3)
            early.add_core(0)
            early.send(0)
            early.add_core(1)
            early.send(1)
            early.add_core(2)
            early.add_core(3)
        elif at == 1:
            down.receive(1)
        elif at == 2:
            small.advance(0)
        elif at == 3:
            down.receive(2)
            down.receive(3)
            down.send(4)
        elif at == 4:
            small.advance(1)
        elif at == 5:
            early.receive(0)
            early.send(2)
            early.send(3)
        elif at == 6:
            down.receive(4)
            down.send(5)
            early.receive(1)
        elif at == 7:
            small.advance(2)
            early.receive(2)
            early.receive(3)
            early.send(4)
        elif at == 8:
            small.advance(3)
            down.share()
            early.receive(4)
            early.send(5)

    def feed_phase(
        ctx, tokens, cotangent, output, w_out, w_up, w_down, act, slope, norm1, inverse1, hidden, hidden_t, grow,
        staged, up_rows, in_sem, w_sem, up_sem, down_sem,
    ):
        out_load = pltpu.make_async_copy(out_w, w_out, w_sem)
        out_load.start()
        rows_in = [
            pltpu.make_async_copy(src, dst, in_sem.at[at])
            for at, (src, dst) in enumerate(((ctx_in, ctx), (tokens_in, tokens), (cotangent_in, cotangent)))
        ]
        for copy in rows_in:
            copy.start()

        def up_load(j):
            return pltpu.make_async_copy(
                up_w.at[:, pl.ds(pl.multiple_of(j * chunk, LANES), chunk)], w_up.at[j], up_sem.at[j]
            )

        def down_load(j):
            return pltpu.make_async_copy(
                down_w.at[pl.ds(pl.multiple_of(j * chunk, LANES), chunk)], w_down.at[j], down_sem.at[j]
            )

        for j in range(chunks):
            up_load(j).start()
            down_load(j).start()
        g_rows[...] = jnp.zeros_like(g_rows)
        for j in range(chunks):
            up_rows[j : j + 1] = up_b[j * chunk : (j + 1) * chunk].reshape(1, chunk)
        out_load.wait()
        for copy in rows_in:
            copy.wait()
        resid = tokens[...].astype(f32) + dot(ctx[...], w_out[...]) + row(out_b)
        normed, inverse = norm_of(resid)
        norm1[...] = normed
        inverse1[...] = jnp.broadcast_to(inverse, inverse1.shape)
        first = normed * row(gain1) + row(shift1)
        hidden[...] = first.astype(low)
        hidden_t[...] = first.astype(low).T
        grow[...] = first + row(down_b)

        @pl.loop(0, chunks)
        def _(j):
            up_load(j).wait()
            upper = dot(hidden[...], w_up[j]) + up_rows[pl.ds(j, 1)]
            cdf = 0.5 + 0.5 * lax.erf(upper * 0.7071067811865476)
            act_low = (upper * cdf).astype(low)
            act[j] = act_low
            slope[j] = (cdf + upper * (jnp.exp(upper * upper * -0.5) * 0.3989422804014327)).astype(low)
            down_load(j).wait()
            grow[...] += dot(act_low, w_down[j])

        normed2, inverse2 = norm_of(grow[...])
        output[...] = (normed2 * row(gain2) + row(shift2)).astype(low)
        output_copy = pltpu.make_async_copy(output, layer_out, w_sem)
        output_copy.start()
        cot = cotangent[...].astype(f32)
        g_rows[0:1] = column_sum(cot * normed2)
        g_rows[1:2] = column_sum(cot)
        dresid2 = norm_back(cot * row(gain2), normed2, inverse2)
        dffn = dresid2.astype(low)
        g_rows[2:3] = column_sum(dffn.astype(f32))
        grow[...] = dresid2
        staged[...] = dffn

        @pl.loop(0, chunks)
        def _(j):
            grad_down = dot_tn(act[j], staged[...]).astype(low)
            for piece in range(up_pieces):
                at = j * up_pieces + piece
                per = up_pieces * chunks // 8
                rows = pl.ds(pl.multiple_of((at % per) * LANES, LANES), LANES)
                for column in range(6):
                    packed_down[column, at // per, rows] = grad_down[
                        piece * LANES : (piece + 1) * LANES, column * LANES : (column + 1) * LANES
                    ]

        if summed:
            down.swap(range(3))
        up_end = up_pieces * shard // 2
        per_half = up_end + shard // 2

        @pl.loop(0, chunks)
        def _(step):
            for at in range(chunks):

                @pl.when(step == at)
                def _(at=at):
                    feed_step(at)

            j = lax.rem(step + first_chunk, chunks)
            dffn = staged[...]
            dupper = (dot_nt(dffn, w_down[j]) * slope[j].astype(f32)).astype(low)
            g_rows[pl.ds(8 + j, 1), :chunk] = column_sum(dupper.astype(f32))
            grow[...] += dot_nt(dupper, w_up[j])
            grad_up = dot(hidden_t[...], dupper).astype(low)
            for piece in range(up_pieces):
                part = grad_up[:, piece * LANES : (piece + 1) * LANES].reshape(8, shard, LANES)
                at = piece // (up_pieces // 2) * per_half + piece % (up_pieces // 2) * shard
                packed[j, :, at : at + shard] = part
            if summed:

                for order in range(3):

                    @pl.when(step == order)
                    def _(order=order):
                        early.swap([order], 0, up_end)

        dhidden = grow[...]
        normed = norm1[...]
        g_rows[3:4] = column_sum(dhidden * normed)
        g_rows[4:5] = column_sum(dhidden)
        back = norm_back(dhidden * row(gain1), normed, inverse1[:, :1])
        dresid1[...] = back.reshape(dresid1.shape)
        dattn = back.astype(low)
        g_rows[5:6] = column_sum(dattn.astype(f32))
        dctx_own[...] = dot_nt(dattn, w_out[...]).astype(low).reshape(dctx_own.shape)
        send_dctx()
        grad_out = dot_tn(ctx[...], dattn).astype(low)
        for column in range(6):
            part = grad_out[:, column * LANES : (column + 1) * LANES].reshape(8, shard, LANES)
            for half in range(2):
                at = half * per_half + up_end
                packed[column, :, at : at + shard // 2] = part[:, half * shard // 2 : (half + 1) * shard // 2]
        if summed:
            small.start()
            early.swap(range(3), up_end, per_half)
        output_copy.wait()

    def back_phase(
        x_t, q, k, v, sc, probs, dq, dkv, w_c, dx, box_t, g_box, g_bias, late_packed, late_held, in_sem, p_sem, w_sem
    ):
        def loads(pg):
            names = ((q_in, q), (k_in, k), (v_in, v), (sc_in, sc))
            copies = [
                pltpu.make_async_copy(src.at[pg], dst.at[pg], in_sem.at[pg, at])
                for at, (src, dst) in enumerate(names)
            ]
            at = pl.ds(pl.multiple_of(pg * keys, LANES), keys)
            copies.append(pltpu.make_async_copy(x_t_in.at[pg], x_t.at[:, at], in_sem.at[pg, 4]))
            return copies

        def p_load(hp, pg):
            return pltpu.make_async_copy(p_in.at[pg, hp], probs.at[pg, hp], p_sem.at[pg, hp])

        w_loads = [
            pltpu.make_async_copy(qkv_w.at[:, of_half(part, core)], w_c.at[part], w_sem.at[part])
            for part in range(3)
        ]
        for pg in range(pages):
            for copy in loads(pg):
                copy.start()
            for hp in range(pairs):
                p_load(hp, pg).start()
        for copy in w_loads:
            copy.start()

        def late(hp):
            return LateSum(ways, hp, late_packed, late_held, late_got, late_out, late_sems)

        for e in range(2):
            box_t[e] = jnp.zeros_like(box_t[e])
            box_t[e, :, e * head : (e + 1) * head] = box_w[...].astype(f32).T.astype(low)
        g_box[...] = jnp.zeros_like(g_box)

        def take(pg):
            for copy in loads(pg):
                copy.wait()
            own_copy(pg).wait()
            mate_copy(pg).wait_recv()

        def one_pair(pg, hp):
            lanes = pl.ds(pl.multiple_of(hp * LANES, LANES), LANES)
            p_load(hp, pg).wait()
            both = sc[pg]
            cosine2, sine2 = turned(both)
            flat = both.T
            sine_t, cosine_t = flat[:head, :chip], flat[head:, :chip]
            basis = both.astype(low)
            basis_t = flat.astype(low)
            q_pair, k_pair, v_pair = q[pg, hp], k[pg, hp], v[pg, hp]
            q_t, k_t = q_pair.T, k_pair.T
            dc = dctx[pg, :, :, lanes].reshape(chip, LANES)
            left = lane_halves((chip, LANES))
            zero = jnp.zeros_like(dc)
            dk, dv, dqs = 0.0, 0.0, []
            for e in range(2):
                mine = left if e == 0 else jnp.logical_not(left)
                own_rows = slice(e * head, (e + 1) * head)
                p = probs[pg, hp, e]
                dc_own = jnp.where(mine, dc, zero)
                q_own = jnp.where(mine, q_pair, zero)
                dp = dot_nt(v_pair, dc_own)
                p_wide = p.astype(f32)
                delta = jnp.sum(p_wide * dp, axis=0, keepdims=True)
                ds = (p_wide * (dp - delta)).astype(low)
                dv = dv + dot(p, dc_own)
                dk_feat = dot(ds, jnp.concatenate([q_own, basis[:chip]], 1)) * scale
                dq_feat = dot(jnp.concatenate([k_t[own_rows], basis_t], 0), ds) * scale
                dk_proj = rotate_key(dk_feat[:, LANES:], cosine2, sine2).astype(low)
                a, b = dq_feat[head : 2 * head], dq_feat[2 * head :]
                dq_proj = jnp.concatenate(
                    [a * cosine_t - b * sine_t, a * sine_t + b * cosine_t], 0
                ).astype(low)
                dk = dk + dk_feat[:, :LANES] + dot(dk_proj, box_t[e])
                dqs.append(dq_feat[:head] + dot(box_w[...], dq_proj))
                g_box[...] += dot(k_t[own_rows], dk_proj) + dot_nt(q_t[own_rows], dq_proj)
            at = pl.ds(pl.multiple_of(pg * keys, LANES), keys)
            at_q = pl.ds(pl.multiple_of(pg * chip, LANES), chip)
            dq[hp, at_q] = jnp.concatenate(dqs, 0).T.astype(low)
            dkv[hp, at, :LANES] = dk.astype(low)
            dkv[hp, at, LANES:] = dv.astype(low)

        def pair_grads(hp):
            dkv_all = dkv[hp]
            dq_all = dq[hp]
            g_kv = column_sum(dkv_all.astype(f32))
            g_bias[pl.ds(hp, 1)] = column_sum(dq_all.astype(f32))
            g_bias[pl.ds(hp + pairs, 1)] = g_kv[:, :LANES]
            g_bias[pl.ds(hp + 2 * pairs, 1)] = g_kv[:, LANES:]
            grad = dot(x_t[...], dkv_all).astype(low)
            x_q = jnp.concatenate([x_t[:, pg * keys : pg * keys + chip] for pg in range(pages)], 1)
            grad_q = dot(x_q, dq_all).astype(low)
            late_packed[hp, 0] = grad_q.reshape(8, shard, LANES)
            late_packed[hp, 1] = grad[:, :LANES].reshape(8, shard, LANES)
            late_packed[hp, 2] = grad[:, LANES:].reshape(8, shard, LANES)

        def core_copy(pg, at):
            return remote(
                dx.at[pg, at, 1 - core], dx_mate.at[pg, at], core_send.at[pg, at], core_recv.at[pg, at],
                mate,
            )

        def side_copy(pg):
            return remote(dx.at[pg, 1, core], dx_side.at[pg], side_send.at[pg], side_recv.at[pg], side)

        def input_part(pg):
            for at in (1, 0):
                rows = pl.ds(pl.multiple_of(pg * keys + at * chip, LANES), chip)
                dks = jnp.concatenate([dkv[hp, rows, :LANES] for hp in range(pairs)], 1)
                dvs = jnp.concatenate([dkv[hp, rows, LANES:] for hp in range(pairs)], 1)
                total = dot_nt(dks, w_c[1]) + dot_nt(dvs, w_c[2])
                if at == 0:
                    rows_q = pl.ds(pl.multiple_of(pg * chip, LANES), chip)
                    dqs = jnp.concatenate([dq[hp, rows_q] for hp in range(pairs)], 1)
                    total = total + dot_nt(dqs, w_c[0])
                dx[pg, at] = total.astype(low).reshape(2, block, width)
                core_copy(pg, at).start()

        def pass_input(pg):
            core_copy(pg, 1).wait_recv()
            dx[pg, 1, core] = dx[pg, 1, core] + dx_mate[pg, 1]
            side_copy(pg).start()

        def bias_rows():
            for part in range(3):
                for which in range(2):
                    own = jnp.where(core == which, 1.0, 0.0)
                    for hp in range(pairs):
                        at = part * pairs + hp
                        yield 64 + (2 * part + which) * pairs + hp, g_bias[at : at + 1] * own

        @pl.loop(0, pages - 1)
        def _(pg):
            take(pg)

            @pl.when(pg > 0)
            def _():
                pass_input(pg - 1)

            @pl.loop(0, pairs)
            def _(hp):
                for at in range(pairs * (pages - 1)):

                    @pl.when(pg * pairs + hp == at)
                    def _(at=at):
                        back_step(at)

                one_pair(pg, hp)

            @pl.when(pg == 0)
            def _():
                for copy in w_loads:
                    copy.wait()

            input_part(pg)

        last = pages - 1
        take(last)
        pass_input(last - 1)

        @pl.loop(0, pairs)
        def _(hp):
            for at in range(pairs):

                @pl.when(hp == at)
                def _(at=at):
                    back_step(pairs * last + at)

            one_pair(last, hp)
            pair_grads(hp)
            if summed:
                late(hp).start()

                @pl.when(hp > 0)
                def _():
                    late(hp - 1).advance(0)

                @pl.when(hp == 2)
                def _():
                    late(0).advance(1)

        if summed:
            tiny_value[0, : 8 * 8] = g_box[...]
            tiny_value[0, 64:] = jnp.zeros((24, LANES), f32)
            for at, row in bias_rows():
                tiny_value[0, at : at + 1] = row
            tiny.start()
        input_part(last)
        if summed:
            pass_input(last)
            tiny.advance(0)
            late(2).advance(0)
            late(1).advance(1)
            down.hand_over()
            early.share()
            late(0).advance(2)
            small.advance(4)
            tiny.advance(1)
            late(2).advance(1)
            late(1).advance(2)
            late(0).advance(3)
            tiny.advance(2)
            late(2).advance(2)
            late(1).advance(3)
            late(0).advance(4)
            early.hand_over()
            tiny.advance(3)
            late(2).advance(3)
            late(1).advance(4)
            tiny.advance(4)
            late(2).advance(4)
        else:
            pass_input(last)

        for pg in range(pages):
            core_copy(pg, 0).wait_recv()
            side_copy(pg).wait_recv()
            total = dx[pg, 0, core].astype(f32) + dx_mate[pg, 0].astype(f32) + dx_side[pg].astype(f32)
            dx_out[pg] = (total + dresid1[pg]).astype(low)
            for at in range(2):
                core_copy(pg, at).wait_send()
            side_copy(pg).wait_send()
            mate_copy(pg).wait_send()
        if summed:
            small_out[...] = small_value[5]
            tiny_out[...] = tiny_value[5]
            early.end()
            down.end()
            for hp in range(pairs):
                late(hp).finish()
            small.finish()
            tiny.finish()
        else:
            late_out[...] = late_packed[...]
            tiny_out[:64] = g_box[...]
            tiny_out[64:] = jnp.zeros((24, LANES), f32)
            for at, row in bias_rows():
                tiny_out[at : at + 1] = row

    vmem, dma = pltpu.VMEM, pltpu.SemaphoreType.DMA
    rows = pages * block
    pl.run_scoped(
        feed_phase,
        vmem((rows, width), low),
        vmem((rows, width), low),
        vmem((rows, width), low),
        vmem((rows, width), low),
        vmem((width, width), low),
        vmem((chunks, width, chunk), low),
        vmem((chunks, chunk, width), low),
        vmem((chunks, rows, chunk), low),
        vmem((chunks, rows, chunk), low),
        vmem((rows, width), f32),
        vmem((rows, LANES), f32),
        vmem((rows, width), low),
        vmem((width, rows), low),
        vmem((rows, width), f32),
        vmem((rows, width), low),
        vmem((chunks, chunk), f32),
        dma((3,)), dma, dma((chunks,)), dma((chunks,)),
    )
    late_shape = (pairs, 3, 8, shard, LANES)
    pl.run_scoped(
        back_phase,
        vmem((width, pages * keys), low),
        vmem((pages, pairs, chip, LANES), low),
        vmem((pages, pairs, keys, LANES), low),
        vmem((pages, pairs, keys, LANES), low),
        vmem((pages, keys, LANES), f32),
        vmem((pages, pairs, 2, keys, chip), low),
        vmem((pairs, pages * chip, LANES), low),
        vmem((pairs, pages * keys, 2 * LANES), low),
        vmem((3, width, half), low),
        vmem((pages, 2, 2, block, width), low),
        vmem((2, LANES, LANES), low),
        vmem(box_w.shape, f32),
        vmem((3 * pairs, LANES), f32),
        vmem(late_shape, low),
        vmem((pairs, 3, 8, shard // 2, LANES), low),
        dma((pages, 5)), dma((pages, pairs)), dma((3,)),
    )


def middle(rows_in, weights, vectors, saved, qkv_w, box_w, summed):
    pages, block, width = rows_in[0].shape[0] // 128, 128, rows_in[0].shape[1]
    rows = pages * block
    half = width // 2
    pairs = half // LANES
    shard = width // 8
    hidden_width = weights[1].shape[1]
    down_rows = hidden_width // 8
    packed_rows = down_rows + shard
    tiny_rows = 88
    small = (16, width)
    struct = jax.ShapeDtypeStruct
    vmem, dma = pltpu.VMEM, pltpu.SemaphoreType.DMA
    outs = [struct((rows, width), low), struct((pages, block, width), low)]
    scratch = [
        vmem((pages, block, width), f32),
        vmem((pages, block, width), low),
        vmem((pages, 2, block, half), low),
        vmem((pages, 2, block, width), low),
        vmem((pages, block, width), low),
        dma((pages,)), dma((pages,)), dma((pages,)), dma((pages, 2)), dma((pages, 2)), dma((pages,)), dma((pages,)),
    ]
    if summed:
        outs += [
            struct((2, 3, 2, packed_rows // 2, LANES), low),
            struct((2, 3, 2, down_rows // 2, LANES), low),
            struct((2, pairs, 3, 2, shard // 2, LANES), low),
            struct(small, f32),
            struct((tiny_rows, LANES), f32),
        ]
        scratch += [
            vmem((6, 8, down_rows, LANES), low),
            vmem((6, 8, packed_rows, LANES), low),
            vmem((3, 16, down_rows // 2, LANES), low),
            vmem((3, 16, packed_rows // 2, LANES), low),
            vmem((3, 15, down_rows // 2, LANES), low),
            vmem((3, 15, packed_rows // 2, LANES), low),
            vmem((pairs, 3, 15, shard // 2, LANES), low),
            vmem((6,) + small, f32),
            vmem((5,) + small, f32),
            vmem((6, tiny_rows, LANES), f32),
            vmem((5, tiny_rows, LANES), f32),
        ]
        groups = len(GROUPS)
        scratch += ([dma((3, 4))] * 2 + [dma((3, groups))] * 2 + [dma((3,))] * 4) * 2
        scratch += [dma((pairs, 3))] * 2 + [dma((pairs, 3, 3))] * 2 + [dma((pairs, 3))] * 4
        scratch += [dma((5,))] * 4
    else:
        outs += [
            struct((6, 8, down_rows, LANES), low),
            struct((6, 8, packed_rows, LANES), low),
            struct((pairs, 3, 8, shard, LANES), low),
            struct(small, f32),
            struct((tiny_rows, LANES), f32),
        ]
    return pl.pallas_call(
        functools.partial(middle_kernel, summed),
        out_shape=tuple(outs),
        in_specs=[any_spec()] * 6 + [vmem_spec()] * 7 + [any_spec()] * 7 + [vmem_spec()],
        out_specs=(any_spec(),) + (vmem_spec(),) * 6,
        scratch_shapes=scratch,
        compiler_params=pltpu.CompilerParams(
            collective_id=2, has_side_effects=True, vmem_limit_bytes=63 * 2**20
        ),
        name="middle",
    )(*rows_in, *weights, *vectors, *saved, qkv_w, box_w)


def finish_kernel(
    early_in, rest_in, late_in, small_in, tiny_in, dx_in, layer_in,
    up, down, out, qkv, qkv_b, box, out_b, gain1, shift1, up_b, down_b, gain2, shift2, input_grad, layer_out,
    early, rest, late, small, tiny, sems,
):
    page = lax.axis_index("page")
    shard = out.shape[0]
    pieces = up.shape[1] // (6 * LANES)
    pairs = (
        (early_in, early), (rest_in, rest), (late_in, late), (small_in, small), (tiny_in, tiny), (dx_in, input_grad),
        (layer_in, layer_out),
    )
    copies = [pltpu.make_async_copy(src, dst, sems.at[at]) for at, (src, dst) in enumerate(pairs)]
    for copy in copies:
        copy.start()
    for copy in copies:
        copy.wait()
    for which in range(2):
        for order in range(3):
            column = which * 3 + order
            rows = early[which, order].astype(f32)
            at = column * LANES
            per = pieces // 2
            for half in range(2):
                for piece in range(per):
                    up_at = (column * pieces + half * per + piece) * LANES
                    up[:, up_at : up_at + LANES] = rows[half, piece * shard : (piece + 1) * shard]
                out[half * shard // 2 : (half + 1) * shard // 2, at : at + LANES] = rows[half, per * shard :]
            down[:, at : at + LANES] = rest[which, order].astype(f32).reshape(-1, LANES)
            for part in range(3):
                at = (part * 6 + column) * LANES
                qkv[:, at : at + LANES] = late[which, order, part].astype(f32).reshape(shard, LANES)
    rows = pltpu.roll(small[:8], lax.rem(8 * shard - page * shard, 8 * shard), 1)
    for at, ref in enumerate((gain2, shift2, down_b, gain1, shift1, out_b)):
        ref[...] = rows[at, :shard]
    flat = jnp.concatenate([small[8 + at : 9 + at, : pieces * LANES] for at in range(6)], 1)
    every = flat.shape[1]
    flat = pltpu.roll(flat, lax.rem(every - page * up_b.shape[0], every), 1)
    up_b[...] = flat[0, : up_b.shape[0]]
    box[...] = tiny[pl.ds(pl.multiple_of(page * 8, 8), 8)]
    count = qkv_b.shape[0]
    first = page * count
    parts = [tiny[pl.ds(64 + first // LANES + piece, 1)] for piece in range(4)]
    rest = lax.rem(first, LANES)
    row = pltpu.roll(jnp.concatenate(parts, 1), lax.rem(4 * LANES - rest, 4 * LANES), 1)
    qkv_b[...] = row[0, :count]


def finish(early, rest, late, small, tiny, dx, layer):
    struct = jax.ShapeDtypeStruct
    shapes = (
        (96, 3072), (384, 768), (96, 768), (96, 2304), (288,), (8, LANES), (96,), (96,), (96,), (384,), (96,), (96,), (96,),
    )
    operands = (early, rest, late, small, tiny, dx, layer)
    return pl.pallas_call(
        finish_kernel,
        out_shape=tuple(struct(shape, f32) for shape in shapes) + (struct(dx.shape, low), struct(layer.shape, low)),
        in_specs=[any_spec()] * 7,
        out_specs=(vmem_spec(),) * 15,
        scratch_shapes=[pltpu.VMEM(operand.shape, operand.dtype) for operand in operands[:5]]
        + [pltpu.SemaphoreType.DMA((7,))],
        compiler_params=pltpu.CompilerParams(vmem_limit_bytes=63 * 2**20),
        name="finish",
    )(*operands)


def reduce_by_collectives(packed, packed_down, packed_qkv, vectors):
    core = lax.axis_index("blk") % 2
    packed = packed.reshape(6, 8, 2, 240, LANES)
    up = packed[:, :, :, :192].reshape(6, 8, 4, 96, LANES).transpose(1, 3, 0, 2, 4).reshape(768, 3072)
    down = packed_down.transpose(1, 2, 0, 3).reshape(3072, 768)
    out = packed[:, :, :, 192:].transpose(1, 2, 3, 0, 4).reshape(768, 768)
    own = packed_qkv.transpose(2, 3, 1, 0, 4).reshape(768, 3, 384)
    qkv = jnp.zeros((768, 3, 2, 384), low)
    qkv = lax.dynamic_update_slice(qkv, own[:, :, None], (0, 0, core, 0)).reshape(768, 2304)
    grads = jax.tree.map(lambda g: g.astype(f32), (qkv, out, up, down, *vectors))
    page_sums = tuple(
        lax.psum_scatter(grad, "page", scatter_dimension=0, tiled=True) for grad in grads
    )
    return jax.tree.map(
        lambda part: part.astype(f32), lax.psum(jax.tree.map(lambda g: g.astype(low), page_sums), "blk")
    )


def local(
    tokens, lengths, boxes, qkv_weight, qkv_bias, box_weight, out_weight, out_bias, norm1_gain,
    norm1_bias, up_weight, up_bias, down_weight, down_bias, norm2_gain, norm2_bias, cotangent,
):
    pages, block, width = tokens.shape
    rows = pages * block
    *saved, ctx = attend(tokens, boxes, lengths, qkv_weight, qkv_bias, box_weight)
    summed = lax.axis_size("page") == 8
    output, input_grad, *parts = middle(
        [part.reshape(rows, width) for part in (ctx, tokens, cotangent)], (out_weight, up_weight, down_weight),
        (out_bias, norm1_gain, norm1_bias, up_bias, down_bias, norm2_gain, norm2_bias), saved,
        qkv_weight, box_weight, summed,
    )
    if summed:
        early, rest, late, small, tiny = parts
        (
            up_w, down_w, out_w, qkv_w, qkv_b, box, out_b, gain1, shift1, up_b, down_b, gain2, shift2, input_grad,
            output,
        ) = finish(early, rest, late, small, tiny, input_grad, output)
        box = box.reshape(-1)
    else:
        down, packed, packed_qkv, small, tiny = parts
        vectors = (
            tiny[64:82].reshape(-1), tiny[:64].reshape(-1), small[5], small[3], small[4],
            small[8:14, :512].reshape(-1), small[2], small[0], small[1],
        )
        (
            qkv_w, out_w, up_w, down_w, qkv_b, box, out_b, gain1, shift1, up_b, down_b, gain2, shift2,
        ) = reduce_by_collectives(packed, down, packed_qkv, vectors)
    return (
        output.reshape(pages, block, width), input_grad, qkv_w, qkv_b, box, out_w, out_b, gain1, shift1, up_w, up_b, down_w, down_b, gain2, shift2,
    )


def solution(mesh):
    return jax.shard_map(
        local,
        mesh=mesh,
        in_specs=(
            P("page", "blk", None),
            P("page"),
            P("page", "blk", None),
            P(),
            P(),
            P(),
            P(),
            P(),
            P(),
            P(),
            P(),
            P(),
            P(),
            P(),
            P(),
            P(),
            P("page", "blk", None),
        ),
        out_specs=(
            P("page", "blk", None),
            P("page", "blk", None),
            P("page", None),
            P("page"),
            P("page"),
            P("page", None),
            P("page"),
            P("page"),
            P("page"),
            P("page", None),
            P("page"),
            P("page", None),
            P("page"),
            P("page"),
            P("page"),
        ),
        check_vma=False,
    )
```

```python
import functools

import jax
import jax.numpy as jnp
import numpy as np
from jax import lax
from jax.experimental import pallas as pl
from jax.experimental.pallas import tpu as pltpu
from jax.sharding import PartitionSpec as P

norm_eps = 1e-12
MESH = pl.DeviceIdType.MESH
LANES = 128
low = jnp.bfloat16
f32 = jnp.float32


def core_of(blk):
    return blk + 1 - 2 * (blk % 2)


def side_of(blk):
    return (blk + 2) % 4


def greet(others):
    barrier = pltpu.get_barrier_semaphore()
    for other in others:
        pl.semaphore_signal(barrier, inc=1, device_id=other, device_id_type=MESH)
    pl.semaphore_wait(barrier, len(others))


def remote(src, dst, send_sem, recv_sem, to):
    return pltpu.make_async_remote_copy(
        src_ref=src, dst_ref=dst, send_sem=send_sem, recv_sem=recv_sem, device_id=to,
        device_id_type=MESH,
    )


def dot(a, b):
    return jnp.dot(a, b, preferred_element_type=f32)


def dot_nt(a, b):
    return lax.dot_general(a, b, (((1,), (1,)), ((), ())), preferred_element_type=f32)


def dot_tn(a, b):
    return lax.dot_general(a, b, (((0,), (0,)), ((), ())), preferred_element_type=f32)


def sin_cos(theta):
    turns = jnp.floor(theta * 0.6366197723675814 + 0.5)
    rest = theta - turns * 1.5703125
    rest = rest - turns * 4.837512969970703125e-4
    rest = rest - turns * 7.54978995489188216e-8
    square = rest * rest
    sine = ((-1.9515295891e-4 * square + 8.3321608736e-3) * square - 1.6666654611e-1) * square
    sine = sine * rest + rest
    cosine = (2.443315711809948e-5 * square - 1.388731625493765e-3) * square + 4.166664568298827e-2
    cosine = cosine * square * square - 0.5 * square + 1.0
    quarter = turns.astype(jnp.int32)
    odd = (quarter & 1) == 1
    sine_at = jnp.where(odd, cosine, sine)
    cosine_at = jnp.where(odd, sine, cosine)
    sine_at = jnp.where((quarter & 2) == 2, -sine_at, sine_at)
    cosine_at = jnp.where(((quarter + 1) & 2) == 2, -cosine_at, cosine_at)
    return sine_at, cosine_at


def lane_halves(shape):
    return lax.broadcasted_iota(jnp.int32, shape, 1) < LANES // 2


def turned(both):
    swapped = pltpu.roll(both, LANES // 2, 1)
    left = lane_halves(both.shape)
    return jnp.where(left, -swapped, both), jnp.where(left, both, swapped)


def rotate_key(proj, cosine2, sine2):
    return proj * cosine2 + pltpu.roll(proj, LANES // 2, 1) * sine2


def any_spec():
    return pl.BlockSpec(memory_space=pl.ANY)


def vmem_spec():
    return pl.BlockSpec(memory_space=pltpu.VMEM)


GROUPS = ((12, 16), (8, 12), (6, 8), (4, 6), (2, 4), (1, 2))


def flip(page, way):
    x, z = page % 2, page // 2
    if way == "x":
        return z * 2 + (1 - x)
    if way == "a":
        return (z + 1 - 2 * (z % 2)) * 2 + x
    return ((z + 2) % 4) * 2 + x


DOWN_ORDERS = ("xyam", "axym", "yaxm")
EARLY_ORDERS = ("xaym", "axym", "yxam")
LATE_ORDERS = ("xyam", "xyam", "axym")
PLAN = {
    "f2": ("Dc0", "Ds0", "Dc1", "Ds1"),
    "f3": ("Dc2", "Dc3"),
    "fe": ("Dr0", "Ds3", "Ds2"),
    "fw": ("Ss",),
    "b0": ("Ec2", "Ec3", "Ec0", "Es0", "Ec1", "Es1", "Dr3", "Dr1"),
    "b1": ("Dr2",),
    "b2": ("Sa0",),
    "b4": ("Er0", "Es2", "Ds4", "Es3", "X0p"),
    "q1": ("Sa1", "Er1"),
    "g0": ("L0s", "X1p"),
    "g1": ("Er2", "X0fin", "Es4"),
    "p2": ("Dr4", "Ds5", "Sa2", "X1fin", "Ts"),
    "tail": ("Er3", "L1s", "X2p", "Er4", "L2s", "Es5", "Sa3", "L0a0", "Sa4", "Ta0", "Dsh", "X2fin", "L1a0", "Dho", "L2a0", "L0a1", "Dfin", "L1a1", "Ta1", "L2a1", "Esh", "L0a2", "L1a2", "L2a2", "Ta2", "L0a3", "Eho", "L1a3", "Ta3", "Efin", "L2a3", "Ta4", "L0fin", "L1fin", "L2fin"),
}


class Ways:
    def __init__(self):
        self.page, self.blk = lax.axis_index("page"), lax.axis_index("blk")
        self.core, self.half = self.blk % 2, self.blk // 2
        self.mate, self.side = (self.page, core_of(self.blk)), (self.page, side_of(self.blk))

    def partner(self, ways):
        page, blk = self.page, self.blk
        for way in ways:
            if way == "y":
                blk = side_of(blk)
            elif way == "c":
                blk = core_of(blk)
            else:
                page = flip(page, way)
        return page, blk

    def piece(self, order, code):
        page, half = self.page, self.half
        for place, way in enumerate(order):
            if code >> (3 - place) & 1:
                if way == "y":
                    half = 1 - half
                else:
                    page = flip(page, way)
        return page, half

    def everyone(self):
        return [self.partner(ways) for ways in ("x", "a", "m", "y", "c", "yc")]


def step_of(code):
    return 4 - code.bit_length()


class EarlySum:
    def __init__(self, ways, orders, packed, mates, got, final, sems):
        self.ways, self.orders = ways, orders
        self.packed, self.mates, self.got, self.final = packed, mates, got, final
        (self.core_send, self.core_recv, self.send_sem, self.recv_sem, self.last_send, self.last_recv,
         self.end_send, self.end_recv) = sems
        self.rows = packed.shape[2] // 2

    slices = ((12, 16), (8, 12), (4, 8), (0, 4))

    def place(self, order, code, core, begin=0, end=None):
        page, half = self.ways.piece(self.orders[order], code)
        count = (self.rows if end is None else end) - begin
        return 3 * core + order, page, pl.ds(pl.multiple_of(half * self.rows + begin, 16), count)

    def swap(self, orders, begin=0, end=None):
        ways = self.ways
        for at, (first, last) in enumerate(self.slices):
            for code in range(first, last):
                for order in orders:
                    remote(
                        self.packed.at[self.place(order, code, 1 - ways.core, begin, end)],
                        self.mates.at[order, code, begin:end], self.core_send.at[order, at],
                        self.core_recv.at[order, at], ways.mate,
                    ).start()

    def core_group(self, order, at):
        begin, end = self.slices[at]
        part = self.mates.at[order, begin:end]
        return remote(part, part, self.core_send.at[order, at], self.core_recv.at[order, at], self.ways.mate)

    def add_core(self, at):
        for order in range(3):
            self.core_group(order, at).wait_recv()
            for code in range(*self.slices[at]):
                place = self.place(order, code, self.ways.core)
                self.packed[place] = self.packed[place] + self.mates[order, code]

    def group(self, order, group):
        begin, end = GROUPS[group]
        part = self.got.at[order, begin - 1 : end - 1]
        way = self.orders[order][step_of(begin)]
        return remote(
            part, part, self.send_sem.at[order, group], self.recv_sem.at[order, group], self.ways.partner(way)
        )

    def send(self, group):
        begin, end = GROUPS[group]
        for code in range(begin, end):
            for order in range(3):
                remote(
                    self.packed.at[self.place(order, code, self.ways.core)], self.got.at[order, code - 1],
                    self.send_sem.at[order, group], self.recv_sem.at[order, group],
                    self.ways.partner(self.orders[order][step_of(begin)]),
                ).start()

    def receive(self, group):
        begin, end = GROUPS[group]
        base = 1 << (begin.bit_length() - 1)
        for order in range(3):
            self.group(order, group).wait_recv()
            for code in range(begin, end):
                place = self.place(order, code - base, self.ways.core)
                self.packed[place] = self.packed[place] + self.got[order, code - 1]

    def share(self):
        for order in range(3):
            self.group(order, 5).wait_recv()
            place = self.place(order, 0, self.ways.core)
            self.final[self.ways.core, order, self.ways.half] = self.packed[place] + self.got[order, 0]
            self.last_copy(order).start()

    def last_copy(self, order):
        part = self.final.at[self.ways.core, order, self.ways.half]
        return remote(part, part, self.last_send.at[order], self.last_recv.at[order], self.ways.side)

    def end_copy(self, order):
        part = self.final.at[self.ways.core, order]
        return remote(part, part, self.end_send.at[order], self.end_recv.at[order], self.ways.mate)

    def hand_over(self):
        for order in range(3):
            self.last_copy(order).wait_recv()
            self.end_copy(order).start()

    def end(self):
        for order in range(3):
            self.end_copy(order).wait()
            self.last_copy(order).wait_send()
            for at in range(4):
                self.core_group(order, at).wait_send()
            for group in range(len(GROUPS)):
                self.group(order, group).wait_send()


class LateSum:
    def __init__(self, ways, orders, hp, packed, held, got, final, sems):
        self.ways, self.orders, self.hp = ways, orders, hp
        self.packed, self.held, self.got, self.final = packed, held, got, final
        self.first_send, self.first_recv, self.send_sem, self.recv_sem, self.last_send, self.last_recv = sems
        self.rows = held.shape[3]

    def part(self, order, code):
        page, half = self.ways.piece(self.orders[order], code)
        return self.hp, order, page, pl.ds(pl.multiple_of(half * self.rows, 16), self.rows)

    def start(self):
        hp = self.hp
        for code in (12, 13, 14, 15, 8, 9, 10, 11):
            for order in range(3):
                remote(
                    self.packed.at[self.part(order, code)], self.got.at[hp, order, code - 1],
                    self.first_send.at[hp, order], self.first_recv.at[hp, order],
                    self.ways.partner(self.orders[order][0]),
                ).start()

    def first(self, order):
        part = self.got.at[self.hp, order, 7:15]
        return remote(
            part, part, self.first_send.at[self.hp, order], self.first_recv.at[self.hp, order],
            self.ways.partner(self.orders[order][0]),
        )

    def copy(self, order, step):
        begin, end = 8 >> step, 16 >> step
        return remote(
            self.held.at[self.hp, order, begin:end], self.got.at[self.hp, order, begin - 1 : end - 1],
            self.send_sem.at[self.hp, order, step - 1], self.recv_sem.at[self.hp, order, step - 1],
            self.ways.partner(self.orders[order][step]),
        )

    def shares(self):
        ways, hp = self.ways, self.hp
        part = self.final.at[ways.core, hp, ways.half]
        for which, to in enumerate((ways.side, ways.mate, ways.partner("yc"))):
            yield remote(part, part, self.last_send.at[hp, which], self.last_recv.at[hp, which], to)

    def advance(self, step):
        ways, hp = self.ways, self.hp
        for order in range(3):
            if step == 0:
                self.first(order).wait_recv()
                for code in (4, 5, 6, 7, 0, 1, 2, 3):
                    self.held[hp, order, code] = self.packed[self.part(order, code)] + self.got[hp, order, code + 7]
                    if code == 7:
                        self.copy(order, 1).start()
            elif step < 3:
                self.copy(order, step).wait_recv()
                count = 8 >> step
                self.held[hp, order, :count] = (
                    self.held[hp, order, :count] + self.got[hp, order, count - 1 : 2 * count - 1]
                )
                self.copy(order, step + 1).start()
            else:
                self.copy(order, 3).wait_recv()
                self.final[ways.core, hp, ways.half, order] = self.held[hp, order, 0] + self.got[hp, order, 0]
        if step == 3:
            for copy in self.shares():
                copy.start()

    def finish(self):
        for copy in self.shares():
            copy.wait()
        for order in range(3):
            self.first(order).wait_send()
            for step in (1, 2, 3):
                self.copy(order, step).wait_send()


class SmallSum:
    rounds = "xamyc"

    def __init__(self, ways, value, got, sems):
        self.ways, self.value, self.got = ways, value, got
        self.send_sem, self.recv_sem = sems

    def copy(self, step):
        return remote(
            self.value.at[step], self.got.at[step], self.send_sem.at[step], self.recv_sem.at[step],
            self.ways.partner(self.rounds[step]),
        )

    def start(self):
        self.copy(0).start()

    def advance(self, step):
        self.copy(step).wait_recv()
        self.value[step + 1] = self.value[step] + self.got[step]
        if step < 4:
            self.copy(step + 1).start()

    def finish(self):
        for step in range(5):
            self.copy(step).wait_send()


def norm_of(resid):
    center = resid - jnp.mean(resid, axis=-1, keepdims=True)
    spread = jnp.mean(center * center, axis=-1, keepdims=True)
    inverse = lax.rsqrt(spread + norm_eps)
    return center * inverse, inverse


def norm_back(grad, normed, inverse):
    mean = jnp.mean(grad, axis=-1, keepdims=True)
    along = jnp.mean(grad * normed, axis=-1, keepdims=True)
    return inverse * (grad - mean - normed * along)


def column_sum(values):
    return jnp.sum(values, axis=0, keepdims=True)


def layer_kernel(
    summed, tokens_in, boxes, cotangent_in, out_w, up_w, down_w, qkv_w, lengths, freq, out_b, gain1, shift1, up_b,
    down_b, gain2, shift2, qkv_b, box_w,
    x_t_hbm, q_hbm, k_hbm, v_hbm, sc_hbm, p_hbm, layer_out, dx_out, *refs
):
    if summed:
        (
            early_out, down_out, late_out, small_out, tiny_out,
            x, box, ctx_own, dresid1, dctx_own, dctx, dx_mate, dx_side,
            x_mate_send, x_mate_recv, x_side_send, x_side_recv, x_pass_send, x_pass_recv, ctx_send, ctx_recv,
            own_sem, mate_send, mate_recv, core_send, core_recv, side_send, side_recv,
            packed_down, packed, down_mates, early_mates, down_got, early_got, late_got,
            small_value, small_got, tiny_value, tiny_got, *sems,
        ) = refs
        down_sems, early_sems, late_sems, small_sems, tiny_sems = sems[:8], sems[8:16], sems[16:22], sems[22:24], sems[24:]
        g_rows = small_value.at[0]
    else:
        (
            packed_down, packed, late_out, g_rows, tiny_out,
            x, box, ctx_own, dresid1, dctx_own, dctx, dx_mate, dx_side,
            x_mate_send, x_mate_recv, x_side_send, x_side_recv, x_pass_send, x_pass_recv, ctx_send, ctx_recv,
            own_sem, mate_send, mate_recv, core_send, core_recv, side_send, side_recv,
        ) = refs
    ways = Ways()
    core, mate, side = ways.core, ways.mate, ways.side
    greet(ways.everyone() if summed else [mate, side])
    pages, block, width = dctx_own.shape
    half = width // 2
    pairs = half // LANES
    chip, keys = 2 * block, 4 * block
    shard = width // 8
    head = LANES // 2
    scale = 0.125
    chunks = 6
    chunk = up_w.shape[1] // chunks
    up_pieces = chunk // LANES
    if summed:
        down = EarlySum(ways, DOWN_ORDERS, packed_down, down_mates, down_got, down_out, down_sems)
        early = EarlySum(ways, EARLY_ORDERS, packed, early_mates, early_got, early_out, early_sems)
        small = SmallSum(ways, small_value, small_got, small_sems)
        tiny = SmallSum(ways, tiny_value, tiny_got, tiny_sems)
        first_chunk = chunks // 2 * (1 - core)
    else:
        first_chunk = 0

    def row(ref):
        return ref[...].reshape(1, -1)

    def of_half(part, which):
        return pl.ds(pl.multiple_of(part * 2 * half + which * half, LANES), half)

    def own_copy(pg):
        return pltpu.make_async_copy(
            dctx_own.at[pg, :, of_half(0, core)], dctx.at[pg, core], own_sem.at[pg]
        )

    def mate_copy(pg):
        return remote(
            dctx_own.at[pg, :, of_half(0, 1 - core)], dctx.at[pg, core], mate_send.at[pg],
            mate_recv.at[pg], mate,
        )

    def send_dctx():
        for pg in range(pages):
            mate_copy(pg).start()
            own_copy(pg).start()

    moves = {}
    if summed:
        for name, chain in (("D", down), ("E", early)):
            for at in range(6):
                moves["%ss%d" % (name, at)] = functools.partial(chain.send, at)
                moves["%sr%d" % (name, at)] = functools.partial(chain.receive, at)
            for at in range(4):
                moves["%sc%d" % (name, at)] = functools.partial(chain.add_core, at)
            moves[name + "sh"], moves[name + "ho"], moves[name + "fin"] = chain.share, chain.hand_over, chain.end
        for name, chain in (("S", small), ("T", tiny)):
            moves[name + "s"] = chain.start
            for at in range(5):
                moves["%sa%d" % (name, at)] = functools.partial(chain.advance, at)

    def at_place(place):
        if summed:
            for name in PLAN.get(place, ()):
                moves[name]()

    def at_step(step, places):
        for at, place in enumerate(places):
            if place in PLAN and summed:
                pl.when(step == at)(functools.partial(at_place, place))

    def feed_loads(cotangent, w_out, w_up, w_down, w_sem, up_sem, down_sem):
        rows_in = pltpu.make_async_copy(cotangent_in, cotangent, w_sem.at[0])
        out_load = pltpu.make_async_copy(out_w, w_out, w_sem.at[1])

        def up_load(j):
            return pltpu.make_async_copy(
                up_w.at[:, pl.ds(pl.multiple_of(j * chunk, LANES), chunk)], w_up.at[j], up_sem.at[j]
            )

        def down_load(j):
            return pltpu.make_async_copy(
                down_w.at[pl.ds(pl.multiple_of(j * chunk, LANES), chunk)], w_down.at[j], down_sem.at[j]
            )

        return rows_in, out_load, up_load, down_load

    def attend_phase(
        start_loads, x_t, w_q, w_kv, q, k, v, sc, probs, ctx, box2, own_load, w_sem, out_sem, p_sem, ctx_sem
    ):
        loads = [
            pltpu.make_async_copy(qkv_w.at[:, of_half(0, core)], w_q, w_sem.at[0]),
            pltpu.make_async_copy(qkv_w.at[:, of_half(1, core)], w_kv.at[:, :half], w_sem.at[1]),
            pltpu.make_async_copy(qkv_w.at[:, of_half(2, core)], w_kv.at[:, half:], w_sem.at[2]),
        ]
        own = []
        for pg in range(pages):
            own.append(pltpu.make_async_copy(tokens_in.at[pg], x.at[pg, core], own_load.at[pg, 0]))
            own.append(pltpu.make_async_copy(boxes.at[pg], box.at[pg, core], own_load.at[pg, 1]))
        for copy in own:
            copy.start()
        for copy in loads:
            copy.start()
        to_mate, to_side = [], []
        for pg in range(pages):
            for which, (src, dst) in enumerate(((tokens_in, x), (boxes, box))):
                to_side.append(
                    remote(src.at[pg], dst.at[pg, 2 + core], x_side_send.at[pg, which], x_side_recv.at[pg, which], side)
                )
                to_side[-1].start()
                to_mate.append(
                    remote(src.at[pg], dst.at[pg, core], x_mate_send.at[pg, which], x_mate_recv.at[pg, which], mate)
                )
                to_mate[-1].start()
        start_loads()
        saved = ((x_t, x_t_hbm), (sc, sc_hbm), (q, q_hbm), (k, k_hbm), (v, v_hbm))
        zero = jnp.zeros_like(box_w)
        box2[...] = jnp.concatenate(
            [jnp.concatenate([box_w[...], zero], 1), jnp.concatenate([zero, box_w[...]], 1)], 0
        )

        def bias_of(part):
            both = [
                qkv_b[(2 * part + which) * half : (2 * part + which + 1) * half].reshape(1, half)
                for which in range(2)
            ]
            return jnp.where(core == 0, both[0], both[1])

        for copy in loads:
            copy.wait()

        both_in = ((tokens_in, x), (boxes, box))

        def sines(pg, side_place):
            for at in (2 * side_place, 2 * side_place + 1):
                rows = box[pg, at]
                spread = [
                    jnp.broadcast_to(rows[c : c + 1], (freq.shape[0] // 4, LANES)) for c in range(4)
                ]
                sine, cosine = sin_cos(jnp.concatenate(spread, 0) * freq[...])
                sc[pg, at * LANES : (at + 1) * LANES] = jnp.concatenate([sine, cosine], 0).T

        def project(pg, side_place):
            rows = slice(side_place * chip, (side_place + 1) * chip)
            part = x[pg, 2 * side_place : 2 * side_place + 2].reshape(chip, width)
            x_t[pg, :, rows] = part.T
            bias = jnp.concatenate([bias_of(1), bias_of(2)], 1)
            kv_part = (dot(part, w_kv[...]) + bias).astype(low)
            for hp in range(pairs):
                k[pg, hp, rows] = kv_part[:, hp * LANES : (hp + 1) * LANES]
                v[pg, hp, rows] = kv_part[:, half + hp * LANES : half + (hp + 1) * LANES]
            if side_place == 0:
                q_part = (dot(part, w_q[...]) + bias_of(0)).astype(low)
                for hp in range(pairs):
                    q[pg, hp] = q_part[:, hp * LANES : (hp + 1) * LANES]
            sines(pg, side_place)

        @pl.loop(0, pages)
        def _(pg):
            for which, (src, dst) in enumerate(both_in):
                pltpu.make_async_copy(src.at[pg], dst.at[pg, core], own_load.at[pg, which]).wait()
                remote(
                    src.at[pg], dst.at[pg, core], x_mate_send.at[pg, which], x_mate_recv.at[pg, which], mate
                ).wait_recv()
            project(pg, 0)

        @pl.loop(0, pages)
        def _(pg):
            passed = []
            for which, (src, dst) in enumerate(both_in):
                remote(
                    src.at[pg], dst.at[pg, 2 + core], x_side_send.at[pg, which], x_side_recv.at[pg, which], side
                ).wait_recv()
                copy = remote(
                    dst.at[pg, 2 + core], dst.at[pg, 2 + core], x_pass_send.at[pg, which],
                    x_pass_recv.at[pg, which], mate,
                )
                copy.start()
                passed.append(copy)
            for copy in passed:
                copy.wait_recv()
            project(pg, 1)
            for which, (src, dst) in enumerate(saved):
                pltpu.make_async_copy(src.at[pg], dst.at[pg], out_sem.at[pg, which]).start()
            place = lax.broadcasted_iota(jnp.int32, (keys, chip), 0) + ways.half * chip
            place = jnp.where(place >= keys, place - keys, place)
            valid = place < lengths[pg]

            @pl.loop(0, pairs)
            def _(hp):
                both = sc[pg]
                cosine2, sine2 = turned(both)
                basis = both.astype(low)
                basis_q = (both[:chip] * scale).astype(low)
                left = lane_halves((chip, LANES))
                cosine_q = jnp.where(left, -cosine2[:chip], cosine2[:chip]) * scale
                sine_q = jnp.where(left, sine2[:chip], -sine2[:chip]) * scale
                q_pair, k_pair = q[pg, hp], k[pg, hp]
                q_proj = dot(q_pair, box2[...])
                k_proj = dot(k_pair, box2[...])
                v_t = v[pg, hp].T
                outs = []
                for e in range(2):
                    at = slice(e * LANES, (e + 1) * LANES)
                    q_pos = rotate_key(q_proj[:, at], cosine_q, sine_q).astype(low)
                    k_pos = rotate_key(k_proj[:, at], cosine2, sine2).astype(low)
                    mine = left if e == 0 else jnp.logical_not(left)
                    q_own = jnp.where(mine, q_pair.astype(f32) * scale, 0.0).astype(low)
                    scores = dot_nt(
                        jnp.concatenate([basis, k_pos], 1), jnp.concatenate([q_pos, basis_q], 1)
                    )
                    scores = scores + dot_nt(k_pair, q_own)
                    scores = jnp.where(valid, scores, -1e30)
                    top = jnp.max(scores, axis=0, keepdims=True)
                    grown = jnp.exp(scores - top)
                    total = jnp.sum(grown, axis=0, keepdims=True)
                    p = (grown * (1.0 / total)).astype(low)
                    probs[pg, hp, e] = p
                    outs.append(dot(v_t[e * LANES // 2 : (e + 1) * LANES // 2], p))
                pltpu.make_async_copy(probs.at[pg, hp], p_hbm.at[pg, hp], p_sem.at[pg, hp]).start()
                context = jnp.concatenate(outs, 0).T.astype(low)
                lanes = pl.ds(pl.multiple_of(hp * LANES, LANES), LANES)
                ctx[pg, 0, :, lanes] = context[: chip // 2]
                ctx[pg, 1, :, lanes] = context[chip // 2 :]

            mine = pl.ds(pl.multiple_of(core * half, LANES), half)
            pltpu.make_async_copy(ctx.at[pg, core], ctx_own.at[pg, :, mine], ctx_sem.at[pg]).start()
            remote(
                ctx.at[pg, 1 - core], ctx_own.at[pg, :, mine], ctx_send.at[pg], ctx_recv.at[pg], mate
            ).start()
            for copy in passed:
                copy.wait_send()

        mine = pl.ds(pl.multiple_of(core * half, LANES), half)
        for pg in range(pages):
            for which, (src, dst) in enumerate(saved):
                pltpu.make_async_copy(src.at[pg], dst.at[pg], out_sem.at[pg, which]).wait()
            for hp in range(pairs):
                pltpu.make_async_copy(probs.at[pg, hp], p_hbm.at[pg, hp], p_sem.at[pg, hp]).wait()
            pltpu.make_async_copy(ctx.at[pg, core], ctx_own.at[pg, :, mine], ctx_sem.at[pg]).wait()
            remote(
                ctx.at[pg, 1 - core], ctx_own.at[pg, :, mine], ctx_send.at[pg], ctx_recv.at[pg], mate
            ).wait_send()
        for copy in to_side + to_mate:
            copy.wait_send()

    def feed_phase(
        cotangent, w_out, w_up, w_down, w_sem, up_sem, down_sem, output, act, slope, norm1, inverse1, hidden, hidden_t,
        grow, staged, up_rows, out_sem,
    ):
        rows_in, out_load, up_load, down_load = feed_loads(cotangent, w_out, w_up, w_down, w_sem, up_sem, down_sem)
        g_rows[...] = jnp.zeros_like(g_rows)
        for j in range(chunks):
            up_rows[j : j + 1] = up_b[j * chunk : (j + 1) * chunk].reshape(1, chunk)
        out_load.wait()
        rows_in.wait()
        for pg in range(pages):
            other = pl.ds(pl.multiple_of((1 - core) * (width // 2), LANES), width // 2)
            part = ctx_own.at[pg, :, other]
            remote(part, part, ctx_send.at[pg], ctx_recv.at[pg], mate).wait_recv()
        ctx = ctx_own[...].reshape(pages * block, width)
        tokens = jnp.concatenate([x[pg, core] for pg in range(pages)], 0)
        resid = tokens.astype(f32) + dot(ctx, w_out[...]) + row(out_b)
        normed, inverse = norm_of(resid)
        norm1[...] = normed
        inverse1[...] = jnp.broadcast_to(inverse, inverse1.shape)
        first = normed * row(gain1) + row(shift1)
        hidden[...] = first.astype(low)
        hidden_t[...] = first.astype(low).T
        grow[...] = first + row(down_b)

        @pl.loop(0, chunks)
        def _(j):
            up_load(j).wait()
            upper = dot(hidden[...], w_up[j]) + up_rows[pl.ds(j, 1)]
            cdf = 0.5 + 0.5 * lax.erf(upper * 0.7071067811865476)
            act_low = (upper * cdf).astype(low)
            act[j] = act_low
            slope[j] = (cdf + upper * (jnp.exp(upper * upper * -0.5) * 0.3989422804014327)).astype(low)
            down_load(j).wait()
            grow[...] += dot(act_low, w_down[j])

        normed2, inverse2 = norm_of(grow[...])
        output[...] = (normed2 * row(gain2) + row(shift2)).astype(low)
        output_copy = pltpu.make_async_copy(output, layer_out, out_sem)
        output_copy.start()
        cot = cotangent[...].astype(f32)
        g_rows[0:1] = column_sum(cot * normed2)
        g_rows[1:2] = column_sum(cot)
        dresid2 = norm_back(cot * row(gain2), normed2, inverse2)
        dffn = dresid2.astype(low)
        g_rows[2:3] = column_sum(dffn.astype(f32))
        grow[...] = dresid2
        staged[...] = dffn

        @pl.loop(0, chunks)
        def _(j):
            grad_down = dot_tn(act[j], staged[...]).astype(low)
            for piece in range(up_pieces):
                at = j * up_pieces + piece
                per = up_pieces * chunks // 8
                rows = pl.ds(pl.multiple_of((at % per) * LANES, LANES), LANES)
                for column in range(6):
                    packed_down[column, at // per, rows] = grad_down[
                        piece * LANES : (piece + 1) * LANES, column * LANES : (column + 1) * LANES
                    ]

        if summed:
            down.swap(range(3))
        up_end = up_pieces * shard // 2
        per_half = up_end + shard // 2

        @pl.loop(0, chunks)
        def _(step):
            at_step(step, ["f%d" % at for at in range(chunks)])
            j = lax.rem(step + first_chunk, chunks)
            dffn = staged[...]
            dupper = (dot_nt(dffn, w_down[j]) * slope[j].astype(f32)).astype(low)
            g_rows[pl.ds(8 + j, 1), :chunk] = column_sum(dupper.astype(f32))
            grow[...] += dot_nt(dupper, w_up[j])
            grad_up = dot(hidden_t[...], dupper).astype(low)
            for piece in range(up_pieces):
                part = grad_up[:, piece * LANES : (piece + 1) * LANES].reshape(8, shard, LANES)
                at = piece // (up_pieces // 2) * per_half + piece % (up_pieces // 2) * shard
                packed[j, :, at : at + shard] = part
            if summed:

                for order in range(3):

                    @pl.when(step == order)
                    def _(order=order):
                        early.swap([order], 0, up_end)

        dhidden = grow[...]
        normed = norm1[...]
        g_rows[3:4] = column_sum(dhidden * normed)
        g_rows[4:5] = column_sum(dhidden)
        back = norm_back(dhidden * row(gain1), normed, inverse1[:, :1])
        dresid1[...] = back.reshape(dresid1.shape)
        dattn = back.astype(low)
        g_rows[5:6] = column_sum(dattn.astype(f32))
        dctx_own[...] = dot_nt(dattn, w_out[...]).astype(low).reshape(dctx_own.shape)
        send_dctx()
        at_place("fe")
        grad_out = dot_tn(ctx_own[...].reshape(pages * block, width), dattn).astype(low)
        for column in range(6):
            part = grad_out[:, column * LANES : (column + 1) * LANES].reshape(8, shard, LANES)
            for half in range(2):
                at = half * per_half + up_end
                packed[column, :, at : at + shard // 2] = part[:, half * shard // 2 : (half + 1) * shard // 2]
        if summed:
            early.swap(range(3), up_end, per_half)
        at_place("fw")
        output_copy.wait()

    def back_phase(
        x_t, q, k, v, sc, probs, dq, dkv, w_c, dx, box_t, g_box, g_bias, late_packed, late_held, in_sem, p_sem, w_sem
    ):
        def loads(pg):
            names = ((q_hbm, q), (k_hbm, k), (v_hbm, v), (sc_hbm, sc))
            copies = [
                pltpu.make_async_copy(src.at[pg], dst.at[pg], in_sem.at[pg, at])
                for at, (src, dst) in enumerate(names)
            ]
            at = pl.ds(pl.multiple_of(pg * keys, LANES), keys)
            copies.append(pltpu.make_async_copy(x_t_hbm.at[pg], x_t.at[:, at], in_sem.at[pg, 4]))
            return copies

        def p_load(hp, pg):
            return pltpu.make_async_copy(p_hbm.at[pg, hp], probs.at[pg, hp], p_sem.at[pg, hp])

        w_loads = [
            pltpu.make_async_copy(qkv_w.at[:, of_half(part, core)], w_c.at[part], w_sem.at[part])
            for part in range(3)
        ]
        for pg in range(pages):
            for copy in loads(pg):
                copy.start()
            for hp in range(pairs):
                p_load(hp, pg).start()
        for copy in w_loads:
            copy.start()

        def late(hp):
            return LateSum(ways, LATE_ORDERS, hp, late_packed, late_held, late_got, late_out, late_sems)

        for e in range(2):
            box_t[e] = jnp.zeros_like(box_t[e])
            box_t[e, :, e * head : (e + 1) * head] = box_w[...].astype(f32).T.astype(low)
        g_box[...] = jnp.zeros_like(g_box)

        def take(pg):
            for copy in loads(pg):
                copy.wait()
            own_copy(pg).wait()
            mate_copy(pg).wait_recv()

        def one_pair(pg, hp):
            lanes = pl.ds(pl.multiple_of(hp * LANES, LANES), LANES)
            p_load(hp, pg).wait()
            both = sc[pg]
            cosine2, sine2 = turned(both)
            flat = both.T
            sine_t, cosine_t = flat[:head, :chip], flat[head:, :chip]
            basis = both.astype(low)
            basis_t = flat.astype(low)
            q_pair, k_pair, v_pair = q[pg, hp], k[pg, hp], v[pg, hp]
            q_t, k_t = q_pair.T, k_pair.T
            dc = dctx[pg, :, :, lanes].reshape(chip, LANES)
            left = lane_halves((chip, LANES))
            zero = jnp.zeros_like(dc)
            dk, dv, dqs = 0.0, 0.0, []
            for e in range(2):
                mine = left if e == 0 else jnp.logical_not(left)
                own_rows = slice(e * head, (e + 1) * head)
                p = probs[pg, hp, e]
                dc_own = jnp.where(mine, dc, zero)
                q_own = jnp.where(mine, q_pair, zero)
                dp = dot_nt(v_pair, dc_own)
                p_wide = p.astype(f32)
                delta = jnp.sum(p_wide * dp, axis=0, keepdims=True)
                ds = (p_wide * (dp - delta)).astype(low)
                dv = dv + dot(p, dc_own)
                dk_feat = dot(ds, jnp.concatenate([q_own, basis[:chip]], 1)) * scale
                dq_feat = dot(jnp.concatenate([k_t[own_rows], basis_t], 0), ds) * scale
                dk_proj = rotate_key(dk_feat[:, LANES:], cosine2, sine2).astype(low)
                a, b = dq_feat[head : 2 * head], dq_feat[2 * head :]
                dq_proj = jnp.concatenate(
                    [a * cosine_t - b * sine_t, a * sine_t + b * cosine_t], 0
                ).astype(low)
                dk = dk + dk_feat[:, :LANES] + dot(dk_proj, box_t[e])
                dqs.append(dq_feat[:head] + dot(box_w[...], dq_proj))
                g_box[...] += dot(k_t[own_rows], dk_proj) + dot_nt(q_t[own_rows], dq_proj)
            at = pl.ds(pl.multiple_of(pg * keys, LANES), keys)
            at_q = pl.ds(pl.multiple_of(pg * chip, LANES), chip)
            dq[hp, at_q] = jnp.concatenate(dqs, 0).T.astype(low)
            dkv[hp, at, :LANES] = dk.astype(low)
            dkv[hp, at, LANES:] = dv.astype(low)

        def pair_grads(hp):
            dkv_all = dkv[hp]
            dq_all = dq[hp]
            g_kv = column_sum(dkv_all.astype(f32))
            g_bias[pl.ds(hp, 1)] = column_sum(dq_all.astype(f32))
            g_bias[pl.ds(hp + pairs, 1)] = g_kv[:, :LANES]
            g_bias[pl.ds(hp + 2 * pairs, 1)] = g_kv[:, LANES:]
            grad = dot(x_t[...], dkv_all).astype(low)
            x_q = jnp.concatenate([x_t[:, pg * keys : pg * keys + chip] for pg in range(pages)], 1)
            grad_q = dot(x_q, dq_all).astype(low)
            late_packed[hp, 0] = grad_q.reshape(8, shard, LANES)
            late_packed[hp, 1] = grad[:, :LANES].reshape(8, shard, LANES)
            late_packed[hp, 2] = grad[:, LANES:].reshape(8, shard, LANES)

        def core_copy(pg, at):
            return remote(
                dx.at[pg, at, 1 - core], dx_mate.at[pg, at], core_send.at[pg, at], core_recv.at[pg, at],
                mate,
            )

        def side_copy(pg):
            return remote(dx.at[pg, 1, core], dx_side.at[pg], side_send.at[pg], side_recv.at[pg], side)

        def input_part(pg):
            for at in (1, 0):
                rows = pl.ds(pl.multiple_of(pg * keys + at * chip, LANES), chip)
                dks = jnp.concatenate([dkv[hp, rows, :LANES] for hp in range(pairs)], 1)
                dvs = jnp.concatenate([dkv[hp, rows, LANES:] for hp in range(pairs)], 1)
                total = dot_nt(dks, w_c[1]) + dot_nt(dvs, w_c[2])
                if at == 0:
                    rows_q = pl.ds(pl.multiple_of(pg * chip, LANES), chip)
                    dqs = jnp.concatenate([dq[hp, rows_q] for hp in range(pairs)], 1)
                    total = total + dot_nt(dqs, w_c[0])
                dx[pg, at] = total.astype(low).reshape(2, block, width)
                core_copy(pg, at).start()

        def pass_input(pg):
            core_copy(pg, 1).wait_recv()
            dx[pg, 1, core] = dx[pg, 1, core] + dx_mate[pg, 1]
            side_copy(pg).start()

        def bias_rows():
            for part in range(3):
                for which in range(2):
                    own = jnp.where(core == which, 1.0, 0.0)
                    for hp in range(pairs):
                        at = part * pairs + hp
                        yield 64 + (2 * part + which) * pairs + hp, g_bias[at : at + 1] * own

        def finish_input(pg):
            core_copy(pg, 0).wait_recv()
            side_copy(pg).wait_recv()
            total = dx[pg, 0, core].astype(f32) + dx_mate[pg, 0].astype(f32) + dx_side[pg].astype(f32)
            dx_out[pg] = (total + dresid1[pg]).astype(low)

        for pg in range(pages):
            moves["X%dp" % pg] = functools.partial(pass_input, pg)
            moves["X%dfin" % pg] = functools.partial(finish_input, pg)
        if summed:
            for hp in range(pairs):
                chain = late(hp)
                moves["L%ds" % hp], moves["L%dfin" % hp] = chain.start, chain.finish
                for at in range(4):
                    moves["L%da%d" % (hp, at)] = functools.partial(chain.advance, at)

        @pl.loop(0, pages - 1)
        def _(pg):
            take(pg)

            @pl.loop(0, pairs)
            def _(hp):
                at_step(pg * pairs + hp, ["b%d" % at for at in range(6)])
                one_pair(pg, hp)

            at_step(pg, ["p0", "p1"])

            @pl.when(pg == 0)
            def _():
                for copy in w_loads:
                    copy.wait()

            input_part(pg)
            at_step(pg, ["q0", "q1"])

        last = pages - 1
        take(last)

        @pl.loop(0, pairs)
        def _(hp):
            at_step(hp, ["b6", "b7", "b8"])
            one_pair(last, hp)
            pair_grads(hp)
            at_step(hp, ["g0", "g1"])

        if summed:
            tiny_value[0, : 8 * 8] = g_box[...]
            tiny_value[0, 64:] = jnp.zeros((24, LANES), f32)
            for at, row in bias_rows():
                tiny_value[0, at : at + 1] = row
        at_place("p2")
        input_part(last)
        at_place("tail")
        if not summed:
            for pg in range(pages):
                pass_input(pg)
            for pg in range(pages):
                finish_input(pg)
        for pg in range(pages):
            for at in range(2):
                core_copy(pg, at).wait_send()
            side_copy(pg).wait_send()
            mate_copy(pg).wait_send()
        if summed:
            small_out[...] = small_value[5]
            tiny_out[...] = tiny_value[5]
            small.finish()
            tiny.finish()
        else:
            late_out[...] = late_packed[...]
            tiny_out[:64] = g_box[...]
            tiny_out[64:] = jnp.zeros((24, LANES), f32)
            for at, row in bias_rows():
                tiny_out[at : at + 1] = row

    vmem, dma = pltpu.VMEM, pltpu.SemaphoreType.DMA
    rows = pages * block
    def forward(*weights):
        rows_in, out_load, up_load, down_load = feed_loads(*weights)

        def start_loads():
            out_load.start()
            rows_in.start()
            for j in range(chunks):
                up_load(j).start()
                down_load(j).start()

        pl.run_scoped(
            functools.partial(attend_phase, start_loads),
            vmem((pages, width, keys), low),
            vmem((width, half), low),
            vmem((width, 2 * half), low),
            vmem((pages, pairs, chip, LANES), low),
            vmem((pages, pairs, keys, LANES), low),
            vmem((pages, pairs, keys, LANES), low),
            vmem((pages, keys, LANES), f32),
            vmem((pages, pairs, 2, keys, chip), low),
            vmem((pages, 2, block, half), low),
            vmem((2 * box_w.shape[0], 2 * box_w.shape[1]), low),
            dma((pages, 2)), dma((3,)), dma((pages, 5)), dma((pages, pairs)), dma((pages,)),
        )
        pl.run_scoped(
            functools.partial(feed_phase, *weights),
            vmem((rows, width), low),
            vmem((chunks, rows, chunk), low),
            vmem((chunks, rows, chunk), low),
            vmem((rows, width), f32),
            vmem((rows, LANES), f32),
            vmem((rows, width), low),
            vmem((width, rows), low),
            vmem((rows, width), f32),
            vmem((rows, width), low),
            vmem((chunks, chunk), f32),
            dma,
        )

    pl.run_scoped(
        forward,
        vmem((rows, width), low),
        vmem((width, width), low),
        vmem((chunks, width, chunk), low),
        vmem((chunks, chunk, width), low),
        dma((2,)), dma((chunks,)), dma((chunks,)),
    )
    late_shape = (pairs, 3, 8, shard, LANES)
    pl.run_scoped(
        back_phase,
        vmem((width, pages * keys), low),
        vmem((pages, pairs, chip, LANES), low),
        vmem((pages, pairs, keys, LANES), low),
        vmem((pages, pairs, keys, LANES), low),
        vmem((pages, keys, LANES), f32),
        vmem((pages, pairs, 2, keys, chip), low),
        vmem((pairs, pages * chip, LANES), low),
        vmem((pairs, pages * keys, 2 * LANES), low),
        vmem((3, width, half), low),
        vmem((pages, 2, 2, block, width), low),
        vmem((2, LANES, LANES), low),
        vmem(box_w.shape, f32),
        vmem((3 * pairs, LANES), f32),
        vmem(late_shape, low),
        vmem((pairs, 3, 8, shard // 2, LANES), low),
        dma((pages, 5)), dma((pages, pairs)), dma((3,)),
    )


def layer(tokens, boxes, lengths, cotangent, weights, vectors, qkv_w, qkv_b, box_w, summed):
    pages, block, width = tokens.shape
    head_dim, pos = box_w.shape
    count = pos // 8
    freqs = 10000.0 ** (-np.arange(count) / count)
    freq = jnp.asarray(np.tile(np.tile(freqs, 4)[:, None], (1, LANES)), f32)
    boxes_t = boxes.astype(f32).transpose(0, 2, 1)
    chip, keys = 2 * block, 4 * block
    rows = pages * block
    half = width // 2
    pairs = half // LANES
    shard = width // 8
    hidden_width = weights[1].shape[1]
    down_rows = hidden_width // 8
    packed_rows = down_rows + shard
    tiny_rows = 88
    small = (16, width)
    struct = jax.ShapeDtypeStruct
    vmem, dma = pltpu.VMEM, pltpu.SemaphoreType.DMA
    outs = [
        struct((pages, width, keys), low),
        struct((pages, pairs, chip, LANES), low),
        struct((pages, pairs, keys, LANES), low),
        struct((pages, pairs, keys, LANES), low),
        struct((pages, keys, LANES), f32),
        struct((pages, pairs, 2, keys, chip), low),
        struct((rows, width), low),
        struct((pages, block, width), low),
    ]
    scratch = [
        vmem((pages, 4, block, width), low),
        vmem((pages, 4, 4, LANES), f32),
        vmem((pages, block, width), low),
        vmem((pages, block, width), f32),
        vmem((pages, block, width), low),
        vmem((pages, 2, block, half), low),
        vmem((pages, 2, block, width), low),
        vmem((pages, block, width), low),
        *[dma((pages, 2))] * 6, dma((pages,)), dma((pages,)),
        dma((pages,)), dma((pages,)), dma((pages,)), dma((pages, 2)), dma((pages, 2)), dma((pages,)), dma((pages,)),
    ]
    if summed:
        outs += [
            struct((2, 3, 2, packed_rows // 2, LANES), low),
            struct((2, 3, 2, down_rows // 2, LANES), low),
            struct((2, pairs, 2, 3, shard // 2, LANES), low),
            struct(small, f32),
            struct((tiny_rows, LANES), f32),
        ]
        scratch += [
            vmem((6, 8, down_rows, LANES), low),
            vmem((6, 8, packed_rows, LANES), low),
            vmem((3, 16, down_rows // 2, LANES), low),
            vmem((3, 16, packed_rows // 2, LANES), low),
            vmem((3, 15, down_rows // 2, LANES), low),
            vmem((3, 15, packed_rows // 2, LANES), low),
            vmem((pairs, 3, 15, shard // 2, LANES), low),
            vmem((6,) + small, f32),
            vmem((5,) + small, f32),
            vmem((6, tiny_rows, LANES), f32),
            vmem((5, tiny_rows, LANES), f32),
        ]
        groups = len(GROUPS)
        scratch += ([dma((3, 4))] * 2 + [dma((3, groups))] * 2 + [dma((3,))] * 4) * 2
        scratch += [dma((pairs, 3))] * 2 + [dma((pairs, 3, 3))] * 2 + [dma((pairs, 3))] * 2
        scratch += [dma((5,))] * 4
    else:
        outs += [
            struct((6, 8, down_rows, LANES), low),
            struct((6, 8, packed_rows, LANES), low),
            struct((pairs, 3, 8, shard, LANES), low),
            struct(small, f32),
            struct((tiny_rows, LANES), f32),
        ]
    return pl.pallas_call(
        functools.partial(layer_kernel, summed),
        out_shape=tuple(outs),
        in_specs=[any_spec()] * 7 + [pl.BlockSpec(memory_space=pltpu.SMEM)] + [vmem_spec()] * 10,
        out_specs=(any_spec(),) * 7 + (vmem_spec(),) * 6,
        scratch_shapes=scratch,
        compiler_params=pltpu.CompilerParams(
            collective_id=2, has_side_effects=True, vmem_limit_bytes=63 * 2**20
        ),
        name="layer",
    )(
        tokens, boxes_t, cotangent.reshape(rows, width), *weights, qkv_w, lengths, freq, *vectors, qkv_b, box_w
    )[6:]


def finish_kernel(
    early_in, rest_in, late_in, small_in, tiny_in, dx_in, layer_in,
    up_out, down_out, out_out, qkv_out, qkv_b, box, out_b, gain1, shift1, up_b, down_b, gain2, shift2, input_grad,
    layer_out, early, rest, late, small, tiny, up, down, out, qkv, sems, out_sems,
):
    page = lax.axis_index("page")
    shard = out.shape[0]
    pieces = up.shape[1] // (6 * LANES)
    pairs = (
        (early_in, early), (rest_in, rest), (late_in, late), (small_in, small), (tiny_in, tiny), (dx_in, input_grad),
        (layer_in, layer_out),
    )
    copies = [pltpu.make_async_copy(src, dst, sems.at[at]) for at, (src, dst) in enumerate(pairs)]
    for copy in copies:
        copy.start()
    results = ((up, up_out), (down, down_out), (out, out_out), (qkv, qkv_out))
    done = [pltpu.make_async_copy(src, dst, out_sems.at[at]) for at, (src, dst) in enumerate(results)]
    columns = [(which, order) for which in range(2) for order in range(3)]
    per = pieces // 2
    copies[0].wait()
    for column, (which, order) in enumerate(columns):
        rows = early[which, order].astype(f32)
        at = column * LANES
        for half in range(2):
            for piece in range(per):
                up_at = (column * pieces + half * per + piece) * LANES
                up[:, up_at : up_at + LANES] = rows[half, piece * shard : (piece + 1) * shard]
            out[half * shard // 2 : (half + 1) * shard // 2, at : at + LANES] = rows[half, per * shard :]
    done[0].start()
    done[2].start()
    copies[1].wait()
    for column, (which, order) in enumerate(columns):
        at = column * LANES
        down[:, at : at + LANES] = rest[which, order].astype(f32).reshape(-1, LANES)
    done[1].start()
    copies[2].wait()
    for column, (which, order) in enumerate(columns):
        for part in range(3):
            at = (part * 6 + column) * LANES
            qkv[:, at : at + LANES] = late[which, order, :, part].astype(f32).reshape(shard, LANES)
    done[3].start()
    copies[3].wait()
    copies[4].wait()
    rows = pltpu.roll(small[:8], lax.rem(8 * shard - page * shard, 8 * shard), 1)
    for at, ref in enumerate((gain2, shift2, down_b, gain1, shift1, out_b)):
        ref[...] = rows[at, :shard]
    flat = jnp.concatenate([small[8 + at : 9 + at, : pieces * LANES] for at in range(6)], 1)
    every = flat.shape[1]
    flat = pltpu.roll(flat, lax.rem(every - page * up_b.shape[0], every), 1)
    up_b[...] = flat[0, : up_b.shape[0]]
    box[...] = tiny[pl.ds(pl.multiple_of(page * 8, 8), 8)]
    count = qkv_b.shape[0]
    first = page * count
    parts = [tiny[pl.ds(64 + first // LANES + piece, 1)] for piece in range(4)]
    rest = lax.rem(first, LANES)
    row = pltpu.roll(jnp.concatenate(parts, 1), lax.rem(4 * LANES - rest, 4 * LANES), 1)
    qkv_b[...] = row[0, :count]
    for copy in copies[5:] + done:
        copy.wait()


def finish(early, rest, late, small, tiny, dx, layer):
    struct = jax.ShapeDtypeStruct
    shapes = (
        (96, 3072), (384, 768), (96, 768), (96, 2304), (288,), (8, LANES), (96,), (96,), (96,), (384,), (96,), (96,), (96,),
    )
    operands = (early, rest, late, small, tiny, dx, layer)
    return pl.pallas_call(
        finish_kernel,
        out_shape=tuple(struct(shape, f32) for shape in shapes) + (struct(dx.shape, low), struct(layer.shape, low)),
        in_specs=[any_spec()] * 7,
        out_specs=(any_spec(),) * 4 + (vmem_spec(),) * 11,
        scratch_shapes=[pltpu.VMEM(operand.shape, operand.dtype) for operand in operands[:5]]
        + [pltpu.VMEM(shape, f32) for shape in shapes[:4]]
        + [pltpu.SemaphoreType.DMA((7,)), pltpu.SemaphoreType.DMA((4,))],
        compiler_params=pltpu.CompilerParams(vmem_limit_bytes=63 * 2**20),
        name="finish",
    )(*operands)


def reduce_by_collectives(packed, packed_down, packed_qkv, vectors):
    core = lax.axis_index("blk") % 2
    packed = packed.reshape(6, 8, 2, 240, LANES)
    up = packed[:, :, :, :192].reshape(6, 8, 4, 96, LANES).transpose(1, 3, 0, 2, 4).reshape(768, 3072)
    down = packed_down.transpose(1, 2, 0, 3).reshape(3072, 768)
    out = packed[:, :, :, 192:].transpose(1, 2, 3, 0, 4).reshape(768, 768)
    own = packed_qkv.transpose(2, 3, 1, 0, 4).reshape(768, 3, 384)
    qkv = jnp.zeros((768, 3, 2, 384), low)
    qkv = lax.dynamic_update_slice(qkv, own[:, :, None], (0, 0, core, 0)).reshape(768, 2304)
    grads = jax.tree.map(lambda g: g.astype(f32), (qkv, out, up, down, *vectors))
    page_sums = tuple(
        lax.psum_scatter(grad, "page", scatter_dimension=0, tiled=True) for grad in grads
    )
    return jax.tree.map(
        lambda part: part.astype(f32), lax.psum(jax.tree.map(lambda g: g.astype(low), page_sums), "blk")
    )


def local(
    tokens, lengths, boxes, qkv_weight, qkv_bias, box_weight, out_weight, out_bias, norm1_gain,
    norm1_bias, up_weight, up_bias, down_weight, down_bias, norm2_gain, norm2_bias, cotangent,
):
    pages, block, width = tokens.shape
    rows = pages * block
    summed = lax.axis_size("page") == 8
    output, input_grad, *parts = layer(
        tokens, boxes, lengths, cotangent, (out_weight, up_weight, down_weight),
        (out_bias, norm1_gain, norm1_bias, up_bias, down_bias, norm2_gain, norm2_bias),
        qkv_weight, qkv_bias, box_weight, summed,
    )
    if summed:
        early, rest, late, small, tiny = parts
        (
            up_w, down_w, out_w, qkv_w, qkv_b, box, out_b, gain1, shift1, up_b, down_b, gain2, shift2, input_grad,
            output,
        ) = finish(early, rest, late, small, tiny, input_grad, output)
        box = box.reshape(-1)
    else:
        down, packed, packed_qkv, small, tiny = parts
        vectors = (
            tiny[64:82].reshape(-1), tiny[:64].reshape(-1), small[5], small[3], small[4],
            small[8:14, :512].reshape(-1), small[2], small[0], small[1],
        )
        (
            qkv_w, out_w, up_w, down_w, qkv_b, box, out_b, gain1, shift1, up_b, down_b, gain2, shift2,
        ) = reduce_by_collectives(packed, down, packed_qkv, vectors)
    return (
        output.reshape(pages, block, width), input_grad, qkv_w, qkv_b, box, out_w, out_b, gain1, shift1, up_w, up_b, down_w, down_b, gain2, shift2,
    )


def solution(mesh):
    return jax.shard_map(
        local,
        mesh=mesh,
        in_specs=(
            P("page", "blk", None),
            P("page"),
            P("page", "blk", None),
            P(),
            P(),
            P(),
            P(),
            P(),
            P(),
            P(),
            P(),
            P(),
            P(),
            P(),
            P(),
            P(),
            P("page", "blk", None),
        ),
        out_specs=(
            P("page", "blk", None),
            P("page", "blk", None),
            P("page", None),
            P("page"),
            P("page"),
            P("page", None),
            P("page"),
            P("page"),
            P("page"),
            P("page", None),
            P("page"),
            P("page", None),
            P("page"),
            P("page"),
            P("page"),
        ),
        check_vma=False,
    )
```

```python
import functools

import jax
import jax.numpy as jnp
import numpy as np
from jax import lax
from jax.experimental import pallas as pl
from jax.experimental.pallas import tpu as pltpu
from jax.sharding import PartitionSpec as P

norm_eps = 1e-12
MESH = pl.DeviceIdType.MESH
LANES = 128
low = jnp.bfloat16
f32 = jnp.float32


def core_of(blk):
    return blk + 1 - 2 * (blk % 2)


def side_of(blk):
    return (blk + 2) % 4


def greet(others):
    barrier = pltpu.get_barrier_semaphore()
    for other in others:
        pl.semaphore_signal(barrier, inc=1, device_id=other, device_id_type=MESH)
    pl.semaphore_wait(barrier, len(others))


def remote(src, dst, send_sem, recv_sem, to):
    return pltpu.make_async_remote_copy(
        src_ref=src, dst_ref=dst, send_sem=send_sem, recv_sem=recv_sem, device_id=to,
        device_id_type=MESH,
    )


def dot(a, b):
    return jnp.dot(a, b, preferred_element_type=f32)


def dot_nt(a, b):
    return lax.dot_general(a, b, (((1,), (1,)), ((), ())), preferred_element_type=f32)


def dot_tn(a, b):
    return lax.dot_general(a, b, (((0,), (0,)), ((), ())), preferred_element_type=f32)


def sin_cos(theta):
    turns = jnp.floor(theta * 0.6366197723675814 + 0.5)
    rest = theta - turns * 1.5703125
    rest = rest - turns * 4.837512969970703125e-4
    rest = rest - turns * 7.54978995489188216e-8
    square = rest * rest
    sine = ((-1.9515295891e-4 * square + 8.3321608736e-3) * square - 1.6666654611e-1) * square
    sine = sine * rest + rest
    cosine = (2.443315711809948e-5 * square - 1.388731625493765e-3) * square + 4.166664568298827e-2
    cosine = cosine * square * square - 0.5 * square + 1.0
    quarter = turns.astype(jnp.int32)
    odd = (quarter & 1) == 1
    sine_at = jnp.where(odd, cosine, sine)
    cosine_at = jnp.where(odd, sine, cosine)
    sine_at = jnp.where((quarter & 2) == 2, -sine_at, sine_at)
    cosine_at = jnp.where(((quarter + 1) & 2) == 2, -cosine_at, cosine_at)
    return sine_at, cosine_at


def lane_halves(shape):
    return lax.broadcasted_iota(jnp.int32, shape, 1) < LANES // 2


def turned(both):
    swapped = pltpu.roll(both, LANES // 2, 1)
    left = lane_halves(both.shape)
    return jnp.where(left, -swapped, both), jnp.where(left, both, swapped)


def rotate_key(proj, cosine2, sine2):
    return proj * cosine2 + pltpu.roll(proj, LANES // 2, 1) * sine2


def any_spec():
    return pl.BlockSpec(memory_space=pl.ANY)


def vmem_spec():
    return pl.BlockSpec(memory_space=pltpu.VMEM)


GROUPS = ((12, 16), (8, 12), (6, 8), (4, 6), (2, 4), (1, 2))


def flip(page, way):
    x, z = page % 2, page // 2
    if way == "x":
        return z * 2 + (1 - x)
    if way == "a":
        return (z + 1 - 2 * (z % 2)) * 2 + x
    return ((z + 2) % 4) * 2 + x


DOWN_ORDERS = ("xaym", "ayxm", "yxam")
EARLY_ORDERS = ("xaym", "axym", "yxam")
LATE_ORDERS = ("xyam", "axym", "xyam")
PLAN = {
    "f0": ("Dc0", "Ds0"),
    "f1": ("Dc1", "Ds1", "Dc2"),
    "f2": ("Dc3",),
    "fe": ("Dr0", "Ds2", "Ds3"),
    "fw": ("Ss",),
    "b0": ("Ec2", "Ec0", "Es0", "Ec3", "Ec1", "Es1", "Dr1", "Dr2"),
    "b2": ("Sa0", "Dr3"),
    "b4": ("Er0", "Es2", "Ds4", "Es3", "X0p"),
    "q1": ("Sa1", "Er1"),
    "g0": ("X1p",),
    "g1": ("L1s", "X0fin", "Er2", "Es4"),
    "p2": ("Dr4", "Ts", "Ds5", "L2s", "X1fin", "Sa2"),
    "tail": ("Er3", "X2p", "Er4", "L0s", "Es5", "Sa3", "L1a0", "Sa4", "Ta0", "Dsh", "X2fin", "L2a0", "Dho", "L0a0", "L1a1", "Dfin", "L2a1", "Ta1", "L0a1", "Esh", "L1a2", "L2a2", "L0a2", "Ta2", "L1a3", "Eho", "L2a3", "Ta3", "Efin", "L0a3", "Ta4", "L1fin", "L2fin", "L0fin"),
}


class Ways:
    def __init__(self):
        self.page, self.blk = lax.axis_index("page"), lax.axis_index("blk")
        self.core, self.half = self.blk % 2, self.blk // 2
        self.mate, self.side = (self.page, core_of(self.blk)), (self.page, side_of(self.blk))

    def partner(self, ways):
        page, blk = self.page, self.blk
        for way in ways:
            if way == "y":
                blk = side_of(blk)
            elif way == "c":
                blk = core_of(blk)
            else:
                page = flip(page, way)
        return page, blk

    def piece(self, order, code):
        page, half = self.page, self.half
        for place, way in enumerate(order):
            if code >> (3 - place) & 1:
                if way == "y":
                    half = 1 - half
                else:
                    page = flip(page, way)
        return page, half

    def everyone(self):
        return [self.partner(ways) for ways in ("x", "a", "m", "y", "c", "yc")]


def step_of(code):
    return 4 - code.bit_length()


class EarlySum:
    def __init__(self, ways, orders, packed, mates, got, final, sems):
        self.ways, self.orders = ways, orders
        self.packed, self.mates, self.got, self.final = packed, mates, got, final
        (self.core_send, self.core_recv, self.send_sem, self.recv_sem, self.last_send, self.last_recv,
         self.end_send, self.end_recv) = sems
        self.rows = packed.shape[2] // 2

    slices = ((12, 16), (8, 12), (4, 8), (0, 4))

    def place(self, order, code, core, begin=0, end=None):
        page, half = self.ways.piece(self.orders[order], code)
        count = (self.rows if end is None else end) - begin
        return 3 * core + order, page, pl.ds(pl.multiple_of(half * self.rows + begin, 16), count)

    def swap(self, orders, begin=0, end=None):
        ways = self.ways
        for at, (first, last) in enumerate(self.slices):
            for code in range(first, last):
                for order in orders:
                    remote(
                        self.packed.at[self.place(order, code, 1 - ways.core, begin, end)],
                        self.mates.at[order, code, begin:end], self.core_send.at[order, at],
                        self.core_recv.at[order, at], ways.mate,
                    ).start()

    def core_group(self, order, at):
        begin, end = self.slices[at]
        part = self.mates.at[order, begin:end]
        return remote(part, part, self.core_send.at[order, at], self.core_recv.at[order, at], self.ways.mate)

    def add_core(self, at):
        for order in range(3):
            self.core_group(order, at).wait_recv()
            for code in range(*self.slices[at]):
                place = self.place(order, code, self.ways.core)
                self.packed[place] = self.packed[place] + self.mates[order, code]

    def group(self, order, group):
        begin, end = GROUPS[group]
        part = self.got.at[order, begin - 1 : end - 1]
        way = self.orders[order][step_of(begin)]
        return remote(
            part, part, self.send_sem.at[order, group], self.recv_sem.at[order, group], self.ways.partner(way)
        )

    def send(self, group):
        begin, end = GROUPS[group]
        for code in range(begin, end):
            for order in range(3):
                remote(
                    self.packed.at[self.place(order, code, self.ways.core)], self.got.at[order, code - 1],
                    self.send_sem.at[order, group], self.recv_sem.at[order, group],
                    self.ways.partner(self.orders[order][step_of(begin)]),
                ).start()

    def receive(self, group):
        begin, end = GROUPS[group]
        base = 1 << (begin.bit_length() - 1)
        for order in range(3):
            self.group(order, group).wait_recv()
            for code in range(begin, end):
                place = self.place(order, code - base, self.ways.core)
                self.packed[place] = self.packed[place] + self.got[order, code - 1]

    def share(self):
        for order in range(3):
            self.group(order, 5).wait_recv()
            place = self.place(order, 0, self.ways.core)
            self.final[self.ways.core, order, self.ways.half] = self.packed[place] + self.got[order, 0]
            self.last_copy(order).start()

    def last_copy(self, order):
        part = self.final.at[self.ways.core, order, self.ways.half]
        return remote(part, part, self.last_send.at[order], self.last_recv.at[order], self.ways.side)

    def end_copy(self, order):
        part = self.final.at[self.ways.core, order]
        return remote(part, part, self.end_send.at[order], self.end_recv.at[order], self.ways.mate)

    def hand_over(self):
        for order in range(3):
            self.last_copy(order).wait_recv()
            self.end_copy(order).start()

    def end(self):
        for order in range(3):
            self.end_copy(order).wait()
            self.last_copy(order).wait_send()
            for at in range(4):
                self.core_group(order, at).wait_send()
            for group in range(len(GROUPS)):
                self.group(order, group).wait_send()


class LateSum:
    def __init__(self, ways, orders, hp, packed, held, got, final, sems):
        self.ways, self.orders, self.hp = ways, orders, hp
        self.packed, self.held, self.got, self.final = packed, held, got, final
        self.first_send, self.first_recv, self.send_sem, self.recv_sem, self.last_send, self.last_recv = sems
        self.rows = held.shape[3]

    def part(self, order, code):
        page, half = self.ways.piece(self.orders[order], code)
        return self.hp, order, page, pl.ds(pl.multiple_of(half * self.rows, 16), self.rows)

    def start(self):
        hp = self.hp
        for code in (12, 13, 14, 15, 8, 9, 10, 11):
            for order in range(3):
                remote(
                    self.packed.at[self.part(order, code)], self.got.at[hp, order, code - 1],
                    self.first_send.at[hp, order], self.first_recv.at[hp, order],
                    self.ways.partner(self.orders[order][0]),
                ).start()

    def first(self, order):
        part = self.got.at[self.hp, order, 7:15]
        return remote(
            part, part, self.first_send.at[self.hp, order], self.first_recv.at[self.hp, order],
            self.ways.partner(self.orders[order][0]),
        )

    def copy(self, order, step):
        begin, end = 8 >> step, 16 >> step
        return remote(
            self.held.at[self.hp, order, begin:end], self.got.at[self.hp, order, begin - 1 : end - 1],
            self.send_sem.at[self.hp, order, step - 1], self.recv_sem.at[self.hp, order, step - 1],
            self.ways.partner(self.orders[order][step]),
        )

    def shares(self):
        ways, hp = self.ways, self.hp
        part = self.final.at[ways.core, hp, ways.half]
        for which, to in enumerate((ways.side, ways.mate, ways.partner("yc"))):
            yield remote(part, part, self.last_send.at[hp, which], self.last_recv.at[hp, which], to)

    def advance(self, step):
        ways, hp = self.ways, self.hp
        for order in range(3):
            if step == 0:
                self.first(order).wait_recv()
                for code in (4, 5, 6, 7, 0, 1, 2, 3):
                    self.held[hp, order, code] = self.packed[self.part(order, code)] + self.got[hp, order, code + 7]
                    if code == 7:
                        self.copy(order, 1).start()
            elif step < 3:
                self.copy(order, step).wait_recv()
                count = 8 >> step
                self.held[hp, order, :count] = (
                    self.held[hp, order, :count] + self.got[hp, order, count - 1 : 2 * count - 1]
                )
                self.copy(order, step + 1).start()
            else:
                self.copy(order, 3).wait_recv()
                self.final[ways.core, hp, ways.half, order] = self.held[hp, order, 0] + self.got[hp, order, 0]
        if step == 3:
            for copy in self.shares():
                copy.start()

    def finish(self):
        for copy in self.shares():
            copy.wait()
        for order in range(3):
            self.first(order).wait_send()
            for step in (1, 2, 3):
                self.copy(order, step).wait_send()


class SmallSum:
    rounds = "xamyc"

    def __init__(self, ways, value, got, sems):
        self.ways, self.value, self.got = ways, value, got
        self.send_sem, self.recv_sem = sems

    def copy(self, step):
        return remote(
            self.value.at[step], self.got.at[step], self.send_sem.at[step], self.recv_sem.at[step],
            self.ways.partner(self.rounds[step]),
        )

    def start(self):
        self.copy(0).start()

    def advance(self, step):
        self.copy(step).wait_recv()
        self.value[step + 1] = self.value[step] + self.got[step]
        if step < 4:
            self.copy(step + 1).start()

    def finish(self):
        for step in range(5):
            self.copy(step).wait_send()


def norm_of(resid):
    center = resid - jnp.mean(resid, axis=-1, keepdims=True)
    spread = jnp.mean(center * center, axis=-1, keepdims=True)
    inverse = lax.rsqrt(spread + norm_eps)
    return center * inverse, inverse


def norm_back(grad, normed, inverse):
    mean = jnp.mean(grad, axis=-1, keepdims=True)
    along = jnp.mean(grad * normed, axis=-1, keepdims=True)
    return inverse * (grad - mean - normed * along)


def column_sum(values):
    return jnp.sum(values, axis=0, keepdims=True)


def layer_kernel(
    summed, tokens_in, boxes, cotangent_in, out_w, up_w, down_w, qkv_w, lengths, freq, out_b, gain1, shift1, up_b,
    down_b, gain2, shift2, qkv_b, box_w,
    x_t_hbm, q_hbm, k_hbm, v_hbm, sc_hbm, p_hbm, layer_out, dx_out, *refs
):
    if summed:
        (
            early_out, down_out, late_out, small_out, tiny_out,
            x, box, ctx_own, dresid1, dctx_own, dctx, dx_mate, dx_side,
            x_mate_send, x_mate_recv, x_side_send, x_side_recv, x_pass_send, x_pass_recv, ctx_send, ctx_recv,
            own_sem, mate_send, mate_recv, core_send, core_recv, side_send, side_recv,
            packed_down, packed, down_mates, early_mates, down_got, early_got, late_got,
            small_value, small_got, tiny_value, tiny_got, *sems,
        ) = refs
        down_sems, early_sems, late_sems, small_sems, tiny_sems = sems[:8], sems[8:16], sems[16:22], sems[22:24], sems[24:]
        g_rows = small_value.at[0]
    else:
        (
            packed_down, packed, late_out, g_rows, tiny_out,
            x, box, ctx_own, dresid1, dctx_own, dctx, dx_mate, dx_side,
            x_mate_send, x_mate_recv, x_side_send, x_side_recv, x_pass_send, x_pass_recv, ctx_send, ctx_recv,
            own_sem, mate_send, mate_recv, core_send, core_recv, side_send, side_recv,
        ) = refs
    ways = Ways()
    core, mate, side = ways.core, ways.mate, ways.side
    greet(ways.everyone() if summed else [mate, side])
    pages, block, width = dctx_own.shape
    half = width // 2
    pairs = half // LANES
    chip, keys = 2 * block, 4 * block
    shard = width // 8
    head = LANES // 2
    scale = 0.125
    chunks = 6
    chunk = up_w.shape[1] // chunks
    up_pieces = chunk // LANES
    if summed:
        down = EarlySum(ways, DOWN_ORDERS, packed_down, down_mates, down_got, down_out, down_sems)
        early = EarlySum(ways, EARLY_ORDERS, packed, early_mates, early_got, early_out, early_sems)
        small = SmallSum(ways, small_value, small_got, small_sems)
        tiny = SmallSum(ways, tiny_value, tiny_got, tiny_sems)
        first_chunk = chunks // 2 * (1 - core)
    else:
        first_chunk = 0

    def row(ref):
        return ref[...].reshape(1, -1)

    def of_half(part, which):
        return pl.ds(pl.multiple_of(part * 2 * half + which * half, LANES), half)

    def own_copy(pg):
        return pltpu.make_async_copy(
            dctx_own.at[pg, :, of_half(0, core)], dctx.at[pg, core], own_sem.at[pg]
        )

    def mate_copy(pg):
        return remote(
            dctx_own.at[pg, :, of_half(0, 1 - core)], dctx.at[pg, core], mate_send.at[pg],
            mate_recv.at[pg], mate,
        )

    def send_dctx():
        for pg in range(pages):
            mate_copy(pg).start()
            own_copy(pg).start()

    moves = {}
    if summed:
        for name, chain in (("D", down), ("E", early)):
            for at in range(6):
                moves["%ss%d" % (name, at)] = functools.partial(chain.send, at)
                moves["%sr%d" % (name, at)] = functools.partial(chain.receive, at)
            for at in range(4):
                moves["%sc%d" % (name, at)] = functools.partial(chain.add_core, at)
            moves[name + "sh"], moves[name + "ho"], moves[name + "fin"] = chain.share, chain.hand_over, chain.end
        for name, chain in (("S", small), ("T", tiny)):
            moves[name + "s"] = chain.start
            for at in range(5):
                moves["%sa%d" % (name, at)] = functools.partial(chain.advance, at)

    def at_place(place):
        if summed:
            for name in PLAN.get(place, ()):
                moves[name]()

    def at_step(step, places):
        for at, place in enumerate(places):
            if place in PLAN and summed:
                pl.when(step == at)(functools.partial(at_place, place))

    def feed_loads(cotangent, w_out, w_up, w_down, w_sem, up_sem, down_sem):
        rows_in = pltpu.make_async_copy(cotangent_in, cotangent, w_sem.at[0])
        out_load = pltpu.make_async_copy(out_w, w_out, w_sem.at[1])

        def up_load(j):
            return pltpu.make_async_copy(
                up_w.at[:, pl.ds(pl.multiple_of(j * chunk, LANES), chunk)], w_up.at[j], up_sem.at[j]
            )

        def down_load(j):
            return pltpu.make_async_copy(
                down_w.at[pl.ds(pl.multiple_of(j * chunk, LANES), chunk)], w_down.at[j], down_sem.at[j]
            )

        return rows_in, out_load, up_load, down_load

    def attend_phase(
        start_loads, x_t, w_q, w_kv, q, k, v, sc, probs, ctx, box2, raw, own_load, w_sem, out_sem, p_sem, ctx_sem
    ):
        loads = [
            pltpu.make_async_copy(qkv_w.at[:, of_half(0, core)], w_q, w_sem.at[0]),
            pltpu.make_async_copy(qkv_w.at[:, of_half(1, core)], w_kv.at[:, :half], w_sem.at[1]),
            pltpu.make_async_copy(qkv_w.at[:, of_half(2, core)], w_kv.at[:, half:], w_sem.at[2]),
        ]
        own = []
        for pg in range(pages):
            own.append(pltpu.make_async_copy(tokens_in.at[pg], x.at[pg, core], own_load.at[pg, 0]))
            own.append(pltpu.make_async_copy(boxes.at[pg], box.at[pg, core], own_load.at[pg, 1]))
        for copy in own:
            copy.start()
        for copy in loads:
            copy.start()
        to_mate, to_side = [], []
        for pg in range(pages):
            for which, (src, dst) in enumerate(((tokens_in, x), (boxes, box))):
                to_side.append(
                    remote(src.at[pg], dst.at[pg, 2 + core], x_side_send.at[pg, which], x_side_recv.at[pg, which], side)
                )
                to_side[-1].start()
                to_mate.append(
                    remote(src.at[pg], dst.at[pg, core], x_mate_send.at[pg, which], x_mate_recv.at[pg, which], mate)
                )
                to_mate[-1].start()
        start_loads()
        saved = ((x_t, x_t_hbm), (sc, sc_hbm), (q, q_hbm), (k, k_hbm), (v, v_hbm))
        zero = jnp.zeros_like(box_w)
        box2[...] = jnp.concatenate(
            [jnp.concatenate([box_w[...], zero], 1), jnp.concatenate([zero, box_w[...]], 1)], 0
        )

        def bias_of(part):
            both = [
                qkv_b[(2 * part + which) * half : (2 * part + which + 1) * half].reshape(1, half)
                for which in range(2)
            ]
            return jnp.where(core == 0, both[0], both[1])

        for copy in loads:
            copy.wait()

        both_in = ((tokens_in, x), (boxes, box))

        def sines(pg, side_place):
            for at in (2 * side_place, 2 * side_place + 1):
                rows = box[pg, at].astype(f32)
                spread = [
                    jnp.broadcast_to(rows[c : c + 1], (freq.shape[0] // 4, LANES)) for c in range(4)
                ]
                sine, cosine = sin_cos(jnp.concatenate(spread, 0) * freq[...])
                sc[pg, at * LANES : (at + 1) * LANES] = jnp.concatenate([sine, cosine], 0).T

        def project(pg, side_place):
            rows = slice(side_place * chip, (side_place + 1) * chip)
            part = x[pg, 2 * side_place : 2 * side_place + 2].reshape(chip, width)
            x_t[pg, :, rows] = part.T
            bias = jnp.concatenate([bias_of(1), bias_of(2)], 1)
            kv_part = (dot(part, w_kv[...]) + bias).astype(low)
            for hp in range(pairs):
                k[pg, hp, rows] = kv_part[:, hp * LANES : (hp + 1) * LANES]
                v[pg, hp, rows] = kv_part[:, half + hp * LANES : half + (hp + 1) * LANES]
            if side_place == 0:
                q_part = (dot(part, w_q[...]) + bias_of(0)).astype(low)
                for hp in range(pairs):
                    q[pg, hp] = q_part[:, hp * LANES : (hp + 1) * LANES]
            sines(pg, side_place)

        @pl.loop(0, pages)
        def _(pg):
            for which, (src, dst) in enumerate(both_in):
                pltpu.make_async_copy(src.at[pg], dst.at[pg, core], own_load.at[pg, which]).wait()
                remote(
                    src.at[pg], dst.at[pg, core], x_mate_send.at[pg, which], x_mate_recv.at[pg, which], mate
                ).wait_recv()
            project(pg, 0)

        @pl.loop(0, pages)
        def _(pg):
            passed = []
            for which, (src, dst) in enumerate(both_in):
                remote(
                    src.at[pg], dst.at[pg, 2 + core], x_side_send.at[pg, which], x_side_recv.at[pg, which], side
                ).wait_recv()
                copy = remote(
                    dst.at[pg, 2 + core], dst.at[pg, 2 + core], x_pass_send.at[pg, which],
                    x_pass_recv.at[pg, which], mate,
                )
                copy.start()
                passed.append(copy)
            for copy in passed:
                copy.wait_recv()
            project(pg, 1)
            for which, (src, dst) in enumerate(saved):
                pltpu.make_async_copy(src.at[pg], dst.at[pg], out_sem.at[pg, which]).start()
            place = lax.broadcasted_iota(jnp.int32, (keys, chip), 0) + ways.half * chip
            place = jnp.where(place >= keys, place - keys, place)
            valid = place < lengths[pg]

            both = sc[pg]
            cosine2, sine2 = turned(both)
            basis = both.astype(low)
            basis_q = (both[:chip] * scale).astype(low)
            left = lane_halves((chip, LANES))
            cosine_q = jnp.where(left, -cosine2[:chip], cosine2[:chip]) * scale
            sine_q = jnp.where(left, sine2[:chip], -sine2[:chip]) * scale
            for hp in range(pairs):
                q_pair, k_pair = q[pg, hp], k[pg, hp]
                q_proj = dot(q_pair, box2[...])
                k_proj = dot(k_pair, box2[...])
                for e in range(2):
                    at = slice(e * LANES, (e + 1) * LANES)
                    q_pos = rotate_key(q_proj[:, at], cosine_q, sine_q).astype(low)
                    k_pos = rotate_key(k_proj[:, at], cosine2, sine2).astype(low)
                    mine = left if e == 0 else jnp.logical_not(left)
                    q_own = jnp.where(mine, q_pair.astype(f32) * scale, 0.0).astype(low)
                    scores = dot_nt(
                        jnp.concatenate([basis, k_pos], 1), jnp.concatenate([q_pos, basis_q], 1)
                    )
                    scores = scores + dot_nt(k_pair, q_own)
                    raw[2 * hp + e] = jnp.where(valid, scores, -1e30)
            for hp in range(pairs):
                for e in range(2):
                    scores = raw[2 * hp + e]
                    top = jnp.max(scores, axis=0, keepdims=True)
                    grown = jnp.exp(scores - top)
                    total = jnp.sum(grown, axis=0, keepdims=True)
                    probs[pg, hp, e] = (grown * (1.0 / total)).astype(low)
                pltpu.make_async_copy(probs.at[pg, hp], p_hbm.at[pg, hp], p_sem.at[pg, hp]).start()
            for hp in range(pairs):
                v_t = v[pg, hp].T
                outs = [dot(v_t[e * head : (e + 1) * head], probs[pg, hp, e]) for e in range(2)]
                context = jnp.concatenate(outs, 0).T.astype(low)
                lanes = slice(hp * LANES, (hp + 1) * LANES)
                ctx[pg, 0, :, lanes] = context[: chip // 2]
                ctx[pg, 1, :, lanes] = context[chip // 2 :]

            mine = pl.ds(pl.multiple_of(core * half, LANES), half)
            pltpu.make_async_copy(ctx.at[pg, core], ctx_own.at[pg, :, mine], ctx_sem.at[pg]).start()
            remote(
                ctx.at[pg, 1 - core], ctx_own.at[pg, :, mine], ctx_send.at[pg], ctx_recv.at[pg], mate
            ).start()
            for copy in passed:
                copy.wait_send()

        mine = pl.ds(pl.multiple_of(core * half, LANES), half)
        for pg in range(pages):
            for which, (src, dst) in enumerate(saved):
                pltpu.make_async_copy(src.at[pg], dst.at[pg], out_sem.at[pg, which]).wait()
            for hp in range(pairs):
                pltpu.make_async_copy(probs.at[pg, hp], p_hbm.at[pg, hp], p_sem.at[pg, hp]).wait()
            pltpu.make_async_copy(ctx.at[pg, core], ctx_own.at[pg, :, mine], ctx_sem.at[pg]).wait()
            remote(
                ctx.at[pg, 1 - core], ctx_own.at[pg, :, mine], ctx_send.at[pg], ctx_recv.at[pg], mate
            ).wait_send()
        for copy in to_side + to_mate:
            copy.wait_send()

    def feed_phase(
        cotangent, w_out, w_up, w_down, w_sem, up_sem, down_sem, output, act, slope, norm1, inverse1, hidden, hidden_t,
        grow, staged, up_rows, out_sem,
    ):
        rows_in, out_load, up_load, down_load = feed_loads(cotangent, w_out, w_up, w_down, w_sem, up_sem, down_sem)
        g_rows[...] = jnp.zeros_like(g_rows)
        for j in range(chunks):
            up_rows[j : j + 1] = up_b[j * chunk : (j + 1) * chunk].reshape(1, chunk)
        out_load.wait()
        rows_in.wait()
        for pg in range(pages):
            other = pl.ds(pl.multiple_of((1 - core) * (width // 2), LANES), width // 2)
            part = ctx_own.at[pg, :, other]
            remote(part, part, ctx_send.at[pg], ctx_recv.at[pg], mate).wait_recv()
        ctx = ctx_own[...].reshape(pages * block, width)
        tokens = jnp.concatenate([x[pg, core] for pg in range(pages)], 0)
        resid = tokens.astype(f32) + dot(ctx, w_out[...]) + row(out_b)
        normed, inverse = norm_of(resid)
        norm1[...] = normed
        inverse1[...] = jnp.broadcast_to(inverse, inverse1.shape)
        first = normed * row(gain1) + row(shift1)
        hidden[...] = first.astype(low)
        hidden_t[...] = first.astype(low).T
        grow[...] = first + row(down_b)

        for j in range(chunks):
            up_load(j).wait()
            down_load(j).wait()

        @pl.loop(0, chunks // 2)
        def _(step):
            for j in (2 * step, 2 * step + 1):
                upper = dot(hidden[...], w_up[j]) + up_rows[pl.ds(j, 1)]
                cdf = 0.5 + 0.5 * lax.erf(upper * 0.7071067811865476)
                act[j] = (upper * cdf).astype(low)
                slope[j] = (cdf + upper * (jnp.exp(upper * upper * -0.5) * 0.3989422804014327)).astype(low)

        @pl.loop(0, chunks // 2)
        def _(step):
            grow[...] += dot(act[2 * step], w_down[2 * step]) + dot(act[2 * step + 1], w_down[2 * step + 1])

        normed2, inverse2 = norm_of(grow[...])
        output[...] = (normed2 * row(gain2) + row(shift2)).astype(low)
        output_copy = pltpu.make_async_copy(output, layer_out, out_sem)
        output_copy.start()
        cot = cotangent[...].astype(f32)
        g_rows[0:1] = column_sum(cot * normed2)
        g_rows[1:2] = column_sum(cot)
        dresid2 = norm_back(cot * row(gain2), normed2, inverse2)
        dffn = dresid2.astype(low)
        g_rows[2:3] = column_sum(dffn.astype(f32))
        grow[...] = dresid2
        staged[...] = dffn

        @pl.loop(0, chunks)
        def _(j):
            grad_down = dot_tn(act[j], staged[...]).astype(low)
            for piece in range(up_pieces):
                at = j * up_pieces + piece
                per = up_pieces * chunks // 8
                rows = pl.ds(pl.multiple_of((at % per) * LANES, LANES), LANES)
                for column in range(6):
                    packed_down[column, at // per, rows] = grad_down[
                        piece * LANES : (piece + 1) * LANES, column * LANES : (column + 1) * LANES
                    ]

        if summed:
            down.swap(range(3))
        up_end = up_pieces * shard // 2
        per_half = up_end + shard // 2

        @pl.loop(0, chunks // 2)
        def _(step):
            dffn = staged[...]
            for j in (2 * step, 2 * step + 1):
                act[j] = (dot_nt(dffn, w_down[j]) * slope[j].astype(f32)).astype(low)

        @pl.loop(0, chunks)
        def _(step):
            at_step(step, ["f%d" % at for at in range(chunks)])
            j = lax.rem(step + first_chunk, chunks)
            dupper = act[j]
            g_rows[pl.ds(8 + j, 1), :chunk] = column_sum(dupper.astype(f32))
            grow[...] += dot_nt(dupper, w_up[j])
            grad_up = dot(hidden_t[...], dupper).astype(low)
            for piece in range(up_pieces):
                part = grad_up[:, piece * LANES : (piece + 1) * LANES].reshape(8, shard, LANES)
                at = piece // (up_pieces // 2) * per_half + piece % (up_pieces // 2) * shard
                packed[j, :, at : at + shard] = part
            if summed:

                for order in range(3):

                    @pl.when(step == order)
                    def _(order=order):
                        early.swap([order], 0, up_end)

        dhidden = grow[...]
        normed = norm1[...]
        g_rows[3:4] = column_sum(dhidden * normed)
        g_rows[4:5] = column_sum(dhidden)
        back = norm_back(dhidden * row(gain1), normed, inverse1[:, :1])
        dresid1[...] = back.reshape(dresid1.shape)
        dattn = back.astype(low)
        g_rows[5:6] = column_sum(dattn.astype(f32))
        dctx_own[...] = dot_nt(dattn, w_out[...]).astype(low).reshape(dctx_own.shape)
        send_dctx()
        at_place("fe")
        grad_out = dot_tn(ctx_own[...].reshape(pages * block, width), dattn).astype(low)
        for column in range(6):
            part = grad_out[:, column * LANES : (column + 1) * LANES].reshape(8, shard, LANES)
            for half in range(2):
                at = half * per_half + up_end
                packed[column, :, at : at + shard // 2] = part[:, half * shard // 2 : (half + 1) * shard // 2]
        if summed:
            early.swap(range(3), up_end, per_half)
        at_place("fw")
        output_copy.wait()

    def back_phase(
        x_t, q, k, v, sc, probs, dq, dkv, w_c, dx, box_t, g_box, g_bias, late_packed, late_held, in_sem, p_sem, w_sem
    ):
        def loads(pg):
            names = ((q_hbm, q), (k_hbm, k), (v_hbm, v), (sc_hbm, sc))
            copies = [
                pltpu.make_async_copy(src.at[pg], dst.at[pg], in_sem.at[pg, at])
                for at, (src, dst) in enumerate(names)
            ]
            at = pl.ds(pl.multiple_of(pg * keys, LANES), keys)
            copies.append(pltpu.make_async_copy(x_t_hbm.at[pg], x_t.at[:, at], in_sem.at[pg, 4]))
            return copies

        def p_load(hp, pg):
            return pltpu.make_async_copy(p_hbm.at[pg, hp], probs.at[pg, hp], p_sem.at[pg, hp])

        w_loads = [
            pltpu.make_async_copy(qkv_w.at[:, of_half(part, core)], w_c.at[part], w_sem.at[part])
            for part in range(3)
        ]
        for pg in range(pages):
            for copy in loads(pg):
                copy.start()
            for hp in range(pairs):
                p_load(hp, pg).start()
        for copy in w_loads:
            copy.start()

        def late(hp):
            return LateSum(ways, LATE_ORDERS, hp, late_packed, late_held, late_got, late_out, late_sems)

        for e in range(2):
            box_t[e] = jnp.zeros_like(box_t[e])
            box_t[e, :, e * head : (e + 1) * head] = box_w[...].astype(f32).T.astype(low)
        g_box[...] = jnp.zeros_like(g_box)

        def take(pg):
            for copy in loads(pg):
                copy.wait()
            own_copy(pg).wait()
            mate_copy(pg).wait_recv()

        def one_pair(pg, hp):
            lanes = pl.ds(pl.multiple_of(hp * LANES, LANES), LANES)
            p_load(hp, pg).wait()
            both = sc[pg]
            cosine2, sine2 = turned(both)
            flat = both.T
            sine_t, cosine_t = flat[:head, :chip], flat[head:, :chip]
            basis = both.astype(low)
            basis_t = flat.astype(low)
            q_pair, k_pair, v_pair = q[pg, hp], k[pg, hp], v[pg, hp]
            q_t, k_t = q_pair.T, k_pair.T
            dc = dctx[pg, :, :, lanes].reshape(chip, LANES)
            left = lane_halves((chip, LANES))
            zero = jnp.zeros_like(dc)
            dk, dv, dqs = 0.0, 0.0, []
            for e in range(2):
                mine = left if e == 0 else jnp.logical_not(left)
                own_rows = slice(e * head, (e + 1) * head)
                p = probs[pg, hp, e]
                dc_own = jnp.where(mine, dc, zero)
                q_own = jnp.where(mine, q_pair, zero)
                dp = dot_nt(v_pair, dc_own)
                p_wide = p.astype(f32)
                delta = jnp.sum(p_wide * dp, axis=0, keepdims=True)
                ds = (p_wide * (dp - delta)).astype(low)
                dv = dv + dot(p, dc_own)
                dk_feat = dot(ds, jnp.concatenate([q_own, basis[:chip]], 1)) * scale
                dq_feat = dot(jnp.concatenate([k_t[own_rows], basis_t], 0), ds) * scale
                dk_proj = rotate_key(dk_feat[:, LANES:], cosine2, sine2).astype(low)
                a, b = dq_feat[head : 2 * head], dq_feat[2 * head :]
                dq_proj = jnp.concatenate(
                    [a * cosine_t - b * sine_t, a * sine_t + b * cosine_t], 0
                ).astype(low)
                dk = dk + dk_feat[:, :LANES] + dot(dk_proj, box_t[e])
                dqs.append(dq_feat[:head] + dot(box_w[...], dq_proj))
                g_box[...] += dot(k_t[own_rows], dk_proj) + dot_nt(q_t[own_rows], dq_proj)
            at = pl.ds(pl.multiple_of(pg * keys, LANES), keys)
            at_q = pl.ds(pl.multiple_of(pg * chip, LANES), chip)
            dq[hp, at_q] = jnp.concatenate(dqs, 0).T.astype(low)
            dkv[hp, at, :LANES] = dk.astype(low)
            dkv[hp, at, LANES:] = dv.astype(low)

        def pair_grads(hp):
            dkv_all = dkv[hp]
            dq_all = dq[hp]
            g_kv = column_sum(dkv_all.astype(f32))
            g_bias[pl.ds(hp, 1)] = column_sum(dq_all.astype(f32))
            g_bias[pl.ds(hp + pairs, 1)] = g_kv[:, :LANES]
            g_bias[pl.ds(hp + 2 * pairs, 1)] = g_kv[:, LANES:]
            grad = dot(x_t[...], dkv_all).astype(low)
            x_q = jnp.concatenate([x_t[:, pg * keys : pg * keys + chip] for pg in range(pages)], 1)
            grad_q = dot(x_q, dq_all).astype(low)
            late_packed[hp, 0] = grad_q.reshape(8, shard, LANES)
            late_packed[hp, 1] = grad[:, :LANES].reshape(8, shard, LANES)
            late_packed[hp, 2] = grad[:, LANES:].reshape(8, shard, LANES)

        def core_copy(pg, at):
            return remote(
                dx.at[pg, at, 1 - core], dx_mate.at[pg, at], core_send.at[pg, at], core_recv.at[pg, at],
                mate,
            )

        def side_copy(pg):
            return remote(dx.at[pg, 1, core], dx_side.at[pg], side_send.at[pg], side_recv.at[pg], side)

        def input_part(pg):
            for at in (1, 0):
                rows = pl.ds(pl.multiple_of(pg * keys + at * chip, LANES), chip)
                dks = jnp.concatenate([dkv[hp, rows, :LANES] for hp in range(pairs)], 1)
                dvs = jnp.concatenate([dkv[hp, rows, LANES:] for hp in range(pairs)], 1)
                total = dot_nt(dks, w_c[1]) + dot_nt(dvs, w_c[2])
                if at == 0:
                    rows_q = pl.ds(pl.multiple_of(pg * chip, LANES), chip)
                    dqs = jnp.concatenate([dq[hp, rows_q] for hp in range(pairs)], 1)
                    total = total + dot_nt(dqs, w_c[0])
                dx[pg, at] = total.astype(low).reshape(2, block, width)
                core_copy(pg, at).start()

        def pass_input(pg):
            core_copy(pg, 1).wait_recv()
            dx[pg, 1, core] = dx[pg, 1, core] + dx_mate[pg, 1]
            side_copy(pg).start()

        def bias_rows():
            for part in range(3):
                for which in range(2):
                    own = jnp.where(core == which, 1.0, 0.0)
                    for hp in range(pairs):
                        at = part * pairs + hp
                        yield 64 + (2 * part + which) * pairs + hp, g_bias[at : at + 1] * own

        def finish_input(pg):
            core_copy(pg, 0).wait_recv()
            side_copy(pg).wait_recv()
            total = dx[pg, 0, core].astype(f32) + dx_mate[pg, 0].astype(f32) + dx_side[pg].astype(f32)
            dx_out[pg] = (total + dresid1[pg]).astype(low)

        for pg in range(pages):
            moves["X%dp" % pg] = functools.partial(pass_input, pg)
            moves["X%dfin" % pg] = functools.partial(finish_input, pg)
        if summed:
            for hp in range(pairs):
                chain = late(hp)
                moves["L%ds" % hp], moves["L%dfin" % hp] = chain.start, chain.finish
                for at in range(4):
                    moves["L%da%d" % (hp, at)] = functools.partial(chain.advance, at)

        @pl.loop(0, pages - 1)
        def _(pg):
            take(pg)

            @pl.loop(0, pairs)
            def _(hp):
                at_step(pg * pairs + hp, ["b%d" % at for at in range(6)])
                one_pair(pg, hp)

            at_step(pg, ["p0", "p1"])

            @pl.when(pg == 0)
            def _():
                for copy in w_loads:
                    copy.wait()

            input_part(pg)
            at_step(pg, ["q0", "q1"])

        last = pages - 1
        take(last)

        @pl.loop(0, pairs)
        def _(hp):
            at_step(hp, ["b6", "b7", "b8"])
            one_pair(last, hp)
            pair_grads(hp)
            at_step(hp, ["g0", "g1"])

        if summed:
            tiny_value[0, : 8 * 8] = g_box[...]
            tiny_value[0, 64:] = jnp.zeros((24, LANES), f32)
            for at, row in bias_rows():
                tiny_value[0, at : at + 1] = row
        at_place("p2")
        input_part(last)
        at_place("tail")
        if not summed:
            for pg in range(pages):
                pass_input(pg)
            for pg in range(pages):
                finish_input(pg)
        for pg in range(pages):
            for at in range(2):
                core_copy(pg, at).wait_send()
            side_copy(pg).wait_send()
            mate_copy(pg).wait_send()
        if summed:
            small_out[...] = small_value[5]
            tiny_out[...] = tiny_value[5]
            small.finish()
            tiny.finish()
        else:
            late_out[...] = late_packed[...]
            tiny_out[:64] = g_box[...]
            tiny_out[64:] = jnp.zeros((24, LANES), f32)
            for at, row in bias_rows():
                tiny_out[at : at + 1] = row

    vmem, dma = pltpu.VMEM, pltpu.SemaphoreType.DMA
    rows = pages * block
    def forward(*weights):
        rows_in, out_load, up_load, down_load = feed_loads(*weights)

        def start_loads():
            out_load.start()
            rows_in.start()
            for j in range(chunks):
                up_load(j).start()
                down_load(j).start()

        pl.run_scoped(
            functools.partial(attend_phase, start_loads),
            vmem((pages, width, keys), low),
            vmem((width, half), low),
            vmem((width, 2 * half), low),
            vmem((pages, pairs, chip, LANES), low),
            vmem((pages, pairs, keys, LANES), low),
            vmem((pages, pairs, keys, LANES), low),
            vmem((pages, keys, LANES), f32),
            vmem((pages, pairs, 2, keys, chip), low),
            vmem((pages, 2, block, half), low),
            vmem((2 * box_w.shape[0], 2 * box_w.shape[1]), low),
            vmem((2 * pairs, keys, chip), f32),
            dma((pages, 2)), dma((3,)), dma((pages, 5)), dma((pages, pairs)), dma((pages,)),
        )
        pl.run_scoped(
            functools.partial(feed_phase, *weights),
            vmem((rows, width), low),
            vmem((chunks, rows, chunk), low),
            vmem((chunks, rows, chunk), low),
            vmem((rows, width), f32),
            vmem((rows, LANES), f32),
            vmem((rows, width), low),
            vmem((width, rows), low),
            vmem((rows, width), f32),
            vmem((rows, width), low),
            vmem((chunks, chunk), f32),
            dma,
        )

    pl.run_scoped(
        forward,
        vmem((rows, width), low),
        vmem((width, width), low),
        vmem((chunks, width, chunk), low),
        vmem((chunks, chunk, width), low),
        dma((2,)), dma((chunks,)), dma((chunks,)),
    )
    late_shape = (pairs, 3, 8, shard, LANES)
    pl.run_scoped(
        back_phase,
        vmem((width, pages * keys), low),
        vmem((pages, pairs, chip, LANES), low),
        vmem((pages, pairs, keys, LANES), low),
        vmem((pages, pairs, keys, LANES), low),
        vmem((pages, keys, LANES), f32),
        vmem((pages, pairs, 2, keys, chip), low),
        vmem((pairs, pages * chip, LANES), low),
        vmem((pairs, pages * keys, 2 * LANES), low),
        vmem((3, width, half), low),
        vmem((pages, 2, 2, block, width), low),
        vmem((2, LANES, LANES), low),
        vmem(box_w.shape, f32),
        vmem((3 * pairs, LANES), f32),
        vmem(late_shape, low),
        vmem((pairs, 3, 8, shard // 2, LANES), low),
        dma((pages, 5)), dma((pages, pairs)), dma((3,)),
    )


def layer(tokens, boxes, lengths, cotangent, weights, vectors, qkv_w, qkv_b, box_w, summed):
    pages, block, width = tokens.shape
    head_dim, pos = box_w.shape
    count = pos // 8
    freqs = 10000.0 ** (-np.arange(count) / count)
    freq = jnp.asarray(np.tile(np.tile(freqs, 4)[:, None], (1, LANES)), f32)
    boxes_t = boxes.transpose(0, 2, 1)
    chip, keys = 2 * block, 4 * block
    rows = pages * block
    half = width // 2
    pairs = half // LANES
    shard = width // 8
    hidden_width = weights[1].shape[1]
    down_rows = hidden_width // 8
    packed_rows = down_rows + shard
    tiny_rows = 88
    small = (16, width)
    struct = jax.ShapeDtypeStruct
    vmem, dma = pltpu.VMEM, pltpu.SemaphoreType.DMA
    outs = [
        struct((pages, width, keys), low),
        struct((pages, pairs, chip, LANES), low),
        struct((pages, pairs, keys, LANES), low),
        struct((pages, pairs, keys, LANES), low),
        struct((pages, keys, LANES), f32),
        struct((pages, pairs, 2, keys, chip), low),
        struct((rows, width), low),
        struct((pages, block, width), low),
    ]
    scratch = [
        vmem((pages, 4, block, width), low),
        vmem((pages, 4, 4, LANES), jnp.int32),
        vmem((pages, block, width), low),
        vmem((pages, block, width), f32),
        vmem((pages, block, width), low),
        vmem((pages, 2, block, half), low),
        vmem((pages, 2, block, width), low),
        vmem((pages, block, width), low),
        *[dma((pages, 2))] * 6, dma((pages,)), dma((pages,)),
        dma((pages,)), dma((pages,)), dma((pages,)), dma((pages, 2)), dma((pages, 2)), dma((pages,)), dma((pages,)),
    ]
    if summed:
        outs += [
            struct((2, 3, 2, packed_rows // 2, LANES), low),
            struct((2, 3, 2, down_rows // 2, LANES), low),
            struct((2, pairs, 2, 3, shard // 2, LANES), low),
            struct(small, f32),
            struct((tiny_rows, LANES), f32),
        ]
        scratch += [
            vmem((6, 8, down_rows, LANES), low),
            vmem((6, 8, packed_rows, LANES), low),
            vmem((3, 16, down_rows // 2, LANES), low),
            vmem((3, 16, packed_rows // 2, LANES), low),
            vmem((3, 15, down_rows // 2, LANES), low),
            vmem((3, 15, packed_rows // 2, LANES), low),
            vmem((pairs, 3, 15, shard // 2, LANES), low),
            vmem((6,) + small, f32),
            vmem((5,) + small, f32),
            vmem((6, tiny_rows, LANES), f32),
            vmem((5, tiny_rows, LANES), f32),
        ]
        groups = len(GROUPS)
        scratch += ([dma((3, 4))] * 2 + [dma((3, groups))] * 2 + [dma((3,))] * 4) * 2
        scratch += [dma((pairs, 3))] * 2 + [dma((pairs, 3, 3))] * 2 + [dma((pairs, 3))] * 2
        scratch += [dma((5,))] * 4
    else:
        outs += [
            struct((6, 8, down_rows, LANES), low),
            struct((6, 8, packed_rows, LANES), low),
            struct((pairs, 3, 8, shard, LANES), low),
            struct(small, f32),
            struct((tiny_rows, LANES), f32),
        ]
    return pl.pallas_call(
        functools.partial(layer_kernel, summed),
        out_shape=tuple(outs),
        in_specs=[any_spec()] * 7 + [pl.BlockSpec(memory_space=pltpu.SMEM)] + [vmem_spec()] * 10,
        out_specs=(any_spec(),) * 7 + (vmem_spec(),) * 6,
        scratch_shapes=scratch,
        compiler_params=pltpu.CompilerParams(
            collective_id=2, has_side_effects=True, vmem_limit_bytes=63 * 2**20
        ),
        name="layer",
    )(
        tokens, boxes_t, cotangent.reshape(rows, width), *weights, qkv_w, lengths, freq, *vectors, qkv_b, box_w
    )[6:]


def finish_kernel(
    early_in, rest_in, late_in, small_in, tiny_in, dx_in, layer_in,
    up_out, down_out, out_out, qkv_out, qkv_b, box, out_b, gain1, shift1, up_b, down_b, gain2, shift2, input_grad,
    layer_out, early, rest, late, small, tiny, up, down, out, qkv, sems, out_sems,
):
    page = lax.axis_index("page")
    shard = out.shape[0]
    pieces = up.shape[1] // (6 * LANES)
    pairs = (
        (early_in, early), (rest_in, rest), (late_in, late), (small_in, small), (tiny_in, tiny), (dx_in, input_grad),
        (layer_in, layer_out),
    )
    copies = [pltpu.make_async_copy(src, dst, sems.at[at]) for at, (src, dst) in enumerate(pairs)]
    for copy in copies:
        copy.start()
    results = ((up, up_out), (down, down_out), (out, out_out), (qkv, qkv_out))
    done = [pltpu.make_async_copy(src, dst, out_sems.at[at]) for at, (src, dst) in enumerate(results)]
    columns = [(which, order) for which in range(2) for order in range(3)]
    per = pieces // 2
    copies[0].wait()
    for column, (which, order) in enumerate(columns):
        rows = early[which, order].astype(f32)
        at = column * LANES
        for half in range(2):
            for piece in range(per):
                up_at = (column * pieces + half * per + piece) * LANES
                up[:, up_at : up_at + LANES] = rows[half, piece * shard : (piece + 1) * shard]
            out[half * shard // 2 : (half + 1) * shard // 2, at : at + LANES] = rows[half, per * shard :]
    done[0].start()
    done[2].start()
    copies[1].wait()
    for column, (which, order) in enumerate(columns):
        at = column * LANES
        down[:, at : at + LANES] = rest[which, order].astype(f32).reshape(-1, LANES)
    done[1].start()
    copies[2].wait()
    for column, (which, order) in enumerate(columns):
        for part in range(3):
            at = (part * 6 + column) * LANES
            qkv[:, at : at + LANES] = late[which, order, :, part].astype(f32).reshape(shard, LANES)
    done[3].start()
    copies[3].wait()
    copies[4].wait()
    rows = pltpu.roll(small[:8], lax.rem(8 * shard - page * shard, 8 * shard), 1)
    for at, ref in enumerate((gain2, shift2, down_b, gain1, shift1, out_b)):
        ref[...] = rows[at, :shard]
    flat = jnp.concatenate([small[8 + at : 9 + at, : pieces * LANES] for at in range(6)], 1)
    every = flat.shape[1]
    flat = pltpu.roll(flat, lax.rem(every - page * up_b.shape[0], every), 1)
    up_b[...] = flat[0, : up_b.shape[0]]
    box[...] = tiny[pl.ds(pl.multiple_of(page * 8, 8), 8)]
    count = qkv_b.shape[0]
    first = page * count
    parts = [tiny[pl.ds(64 + first // LANES + piece, 1)] for piece in range(4)]
    rest = lax.rem(first, LANES)
    row = pltpu.roll(jnp.concatenate(parts, 1), lax.rem(4 * LANES - rest, 4 * LANES), 1)
    qkv_b[...] = row[0, :count]
    for copy in copies[5:] + done:
        copy.wait()


def finish(early, rest, late, small, tiny, dx, layer):
    struct = jax.ShapeDtypeStruct
    shapes = (
        (96, 3072), (384, 768), (96, 768), (96, 2304), (288,), (8, LANES), (96,), (96,), (96,), (384,), (96,), (96,), (96,),
    )
    operands = (early, rest, late, small, tiny, dx, layer)
    return pl.pallas_call(
        finish_kernel,
        out_shape=tuple(struct(shape, f32) for shape in shapes) + (struct(dx.shape, low), struct(layer.shape, low)),
        in_specs=[any_spec()] * 7,
        out_specs=(any_spec(),) * 4 + (vmem_spec(),) * 11,
        scratch_shapes=[pltpu.VMEM(operand.shape, operand.dtype) for operand in operands[:5]]
        + [pltpu.VMEM(shape, f32) for shape in shapes[:4]]
        + [pltpu.SemaphoreType.DMA((7,)), pltpu.SemaphoreType.DMA((4,))],
        compiler_params=pltpu.CompilerParams(vmem_limit_bytes=63 * 2**20),
        name="finish",
    )(*operands)


def reduce_by_collectives(packed, packed_down, packed_qkv, vectors):
    core = lax.axis_index("blk") % 2
    packed = packed.reshape(6, 8, 2, 240, LANES)
    up = packed[:, :, :, :192].reshape(6, 8, 4, 96, LANES).transpose(1, 3, 0, 2, 4).reshape(768, 3072)
    down = packed_down.transpose(1, 2, 0, 3).reshape(3072, 768)
    out = packed[:, :, :, 192:].transpose(1, 2, 3, 0, 4).reshape(768, 768)
    own = packed_qkv.transpose(2, 3, 1, 0, 4).reshape(768, 3, 384)
    qkv = jnp.zeros((768, 3, 2, 384), low)
    qkv = lax.dynamic_update_slice(qkv, own[:, :, None], (0, 0, core, 0)).reshape(768, 2304)
    grads = jax.tree.map(lambda g: g.astype(f32), (qkv, out, up, down, *vectors))
    page_sums = tuple(
        lax.psum_scatter(grad, "page", scatter_dimension=0, tiled=True) for grad in grads
    )
    return jax.tree.map(
        lambda part: part.astype(f32), lax.psum(jax.tree.map(lambda g: g.astype(low), page_sums), "blk")
    )


def local(
    tokens, lengths, boxes, qkv_weight, qkv_bias, box_weight, out_weight, out_bias, norm1_gain,
    norm1_bias, up_weight, up_bias, down_weight, down_bias, norm2_gain, norm2_bias, cotangent,
):
    pages, block, width = tokens.shape
    rows = pages * block
    summed = lax.axis_size("page") == 8
    output, input_grad, *parts = layer(
        tokens, boxes, lengths, cotangent, (out_weight, up_weight, down_weight),
        (out_bias, norm1_gain, norm1_bias, up_bias, down_bias, norm2_gain, norm2_bias),
        qkv_weight, qkv_bias, box_weight, summed,
    )
    if summed:
        early, rest, late, small, tiny = parts
        (
            up_w, down_w, out_w, qkv_w, qkv_b, box, out_b, gain1, shift1, up_b, down_b, gain2, shift2, input_grad,
            output,
        ) = finish(early, rest, late, small, tiny, input_grad, output)
        box = box.reshape(-1)
    else:
        down, packed, packed_qkv, small, tiny = parts
        vectors = (
            tiny[64:82].reshape(-1), tiny[:64].reshape(-1), small[5], small[3], small[4],
            small[8:14, :512].reshape(-1), small[2], small[0], small[1],
        )
        (
            qkv_w, out_w, up_w, down_w, qkv_b, box, out_b, gain1, shift1, up_b, down_b, gain2, shift2,
        ) = reduce_by_collectives(packed, down, packed_qkv, vectors)
    return (
        output.reshape(pages, block, width), input_grad, qkv_w, qkv_b, box, out_w, out_b, gain1, shift1, up_w, up_b, down_w, down_b, gain2, shift2,
    )


def solution(mesh):
    return jax.shard_map(
        local,
        mesh=mesh,
        in_specs=(
            P("page", "blk", None),
            P("page"),
            P("page", "blk", None),
            P(),
            P(),
            P(),
            P(),
            P(),
            P(),
            P(),
            P(),
            P(),
            P(),
            P(),
            P(),
            P(),
            P("page", "blk", None),
        ),
        out_specs=(
            P("page", "blk", None),
            P("page", "blk", None),
            P("page", None),
            P("page"),
            P("page"),
            P("page", None),
            P("page"),
            P("page"),
            P("page"),
            P("page", None),
            P("page"),
            P("page", None),
            P("page"),
            P("page"),
            P("page"),
        ),
        check_vma=False,
    )
```

```python
import functools

import jax
import jax.numpy as jnp
import numpy as np
from jax import lax
from jax.experimental import pallas as pl
from jax.experimental.pallas import tpu as pltpu
from jax.sharding import PartitionSpec as P

norm_eps = 1e-12
MESH = pl.DeviceIdType.MESH
LANES = 128
low = jnp.bfloat16
f32 = jnp.float32


def core_of(blk):
    return blk + 1 - 2 * (blk % 2)


def side_of(blk):
    return (blk + 2) % 4


def greet(others):
    barrier = pltpu.get_barrier_semaphore()
    for other in others:
        pl.semaphore_signal(barrier, inc=1, device_id=other, device_id_type=MESH)
    pl.semaphore_wait(barrier, len(others))


def remote(src, dst, send_sem, recv_sem, to):
    return pltpu.make_async_remote_copy(
        src_ref=src, dst_ref=dst, send_sem=send_sem, recv_sem=recv_sem, device_id=to,
        device_id_type=MESH,
    )


def dot(a, b):
    return jnp.dot(a, b, preferred_element_type=f32)


def dot_nt(a, b):
    return lax.dot_general(a, b, (((1,), (1,)), ((), ())), preferred_element_type=f32)


def dot_tn(a, b):
    return lax.dot_general(a, b, (((0,), (0,)), ((), ())), preferred_element_type=f32)


def sin_cos(theta):
    turns = jnp.floor(theta * 0.6366197723675814 + 0.5)
    rest = theta - turns * 1.5703125
    rest = rest - turns * 4.837512969970703125e-4
    rest = rest - turns * 7.54978995489188216e-8
    square = rest * rest
    sine = ((-1.9515295891e-4 * square + 8.3321608736e-3) * square - 1.6666654611e-1) * square
    sine = sine * rest + rest
    cosine = (2.443315711809948e-5 * square - 1.388731625493765e-3) * square + 4.166664568298827e-2
    cosine = cosine * square * square - 0.5 * square + 1.0
    quarter = turns.astype(jnp.int32)
    odd = (quarter & 1) == 1
    sine_at = jnp.where(odd, cosine, sine)
    cosine_at = jnp.where(odd, sine, cosine)
    sine_at = jnp.where((quarter & 2) == 2, -sine_at, sine_at)
    cosine_at = jnp.where(((quarter + 1) & 2) == 2, -cosine_at, cosine_at)
    return sine_at, cosine_at


def lane_halves(shape):
    return lax.broadcasted_iota(jnp.int32, shape, 1) < LANES // 2


def turned(both):
    swapped = pltpu.roll(both, LANES // 2, 1)
    left = lane_halves(both.shape)
    return jnp.where(left, -swapped, both), jnp.where(left, both, swapped)


def rotate_key(proj, cosine2, sine2):
    return proj * cosine2 + pltpu.roll(proj, LANES // 2, 1) * sine2


def any_spec():
    return pl.BlockSpec(memory_space=pl.ANY)


def vmem_spec():
    return pl.BlockSpec(memory_space=pltpu.VMEM)


GROUPS = ((12, 16), (8, 12), (6, 8), (4, 6), (2, 4), (1, 2))


def flip(page, way):
    x, z = page % 2, page // 2
    if way == "x":
        return z * 2 + (1 - x)
    if way == "a":
        return (z + 1 - 2 * (z % 2)) * 2 + x
    return ((z + 2) % 4) * 2 + x


DOWN_ORDERS = ("xaym", "ayxm", "yxam")
EARLY_ORDERS = ("xaym", "axym", "yxam")
LATE_ORDERS = ("xyam", "axym", "xyam")
PLAN = {
    "f0": ("Dc0", "Ds0"),
    "f1": ("Dc1", "Ds1", "Dc2"),
    "f2": ("Dc3",),
    "fe": ("Dr0", "Ds2", "Ds3"),
    "fw": ("Ss",),
    "b0": ("Dr1", "Dr2"),
    "b2": ("Sa0", "Dr3"),
    "b4": ("Er0", "Es2", "Ds4", "Es3", "X0p"),
    "q1": ("Sa1", "Er1"),
    "g0": ("X1p",),
    "g1": ("L1s", "X0fin", "Er2", "Es4"),
    "p2": ("Dr4", "Ts", "Ds5", "L2s", "X1fin", "Sa2"),
    "tail": ("Er3", "X2p", "Er4", "L0s", "Es5", "Sa3", "L1a0", "Sa4", "Ta0", "Dsh", "X2fin", "L2a0", "Dho", "L0a0", "L1a1", "Dfin", "L2a1", "Ta1", "L0a1", "Esh", "L1a2", "L2a2", "L0a2", "Ta2", "L1a3", "Eho", "L2a3", "Ta3", "Efin", "L0a3", "Ta4", "L1fin", "L2fin", "L0fin"),
    "bs": ("Ec2", "Ec0", "Es0", "Ec3", "Ec1", "Es1"),
}


class Ways:
    def __init__(self):
        self.page, self.blk = lax.axis_index("page"), lax.axis_index("blk")
        self.core, self.half = self.blk % 2, self.blk // 2
        self.mate, self.side = (self.page, core_of(self.blk)), (self.page, side_of(self.blk))

    def partner(self, ways):
        page, blk = self.page, self.blk
        for way in ways:
            if way == "y":
                blk = side_of(blk)
            elif way == "c":
                blk = core_of(blk)
            else:
                page = flip(page, way)
        return page, blk

    def piece(self, order, code):
        page, half = self.page, self.half
        for place, way in enumerate(order):
            if code >> (3 - place) & 1:
                if way == "y":
                    half = 1 - half
                else:
                    page = flip(page, way)
        return page, half

    def everyone(self):
        return [self.partner(ways) for ways in ("x", "a", "m", "y", "c", "yc")]


def step_of(code):
    return 4 - code.bit_length()


class EarlySum:
    def __init__(self, ways, orders, packed, mates, got, final, sems):
        self.ways, self.orders = ways, orders
        self.packed, self.mates, self.got, self.final = packed, mates, got, final
        (self.core_send, self.core_recv, self.send_sem, self.recv_sem, self.last_send, self.last_recv,
         self.end_send, self.end_recv) = sems
        self.rows = packed.shape[2] // 2

    slices = ((12, 16), (8, 12), (4, 8), (0, 4))

    def place(self, order, code, core, begin=0, end=None):
        page, half = self.ways.piece(self.orders[order], code)
        count = (self.rows if end is None else end) - begin
        return 3 * core + order, page, pl.ds(pl.multiple_of(half * self.rows + begin, 16), count)

    def swap(self, orders, begin=0, end=None):
        ways = self.ways
        for at, (first, last) in enumerate(self.slices):
            for code in range(first, last):
                for order in orders:
                    remote(
                        self.packed.at[self.place(order, code, 1 - ways.core, begin, end)],
                        self.mates.at[order, code, begin:end], self.core_send.at[order, at],
                        self.core_recv.at[order, at], ways.mate,
                    ).start()

    def core_group(self, order, at):
        begin, end = self.slices[at]
        part = self.mates.at[order, begin:end]
        return remote(part, part, self.core_send.at[order, at], self.core_recv.at[order, at], self.ways.mate)

    def add_core(self, at):
        for order in range(3):
            self.core_group(order, at).wait_recv()
            for code in range(*self.slices[at]):
                place = self.place(order, code, self.ways.core)
                self.packed[place] = self.packed[place] + self.mates[order, code]

    def group(self, order, group):
        begin, end = GROUPS[group]
        part = self.got.at[order, begin - 1 : end - 1]
        way = self.orders[order][step_of(begin)]
        return remote(
            part, part, self.send_sem.at[order, group], self.recv_sem.at[order, group], self.ways.partner(way)
        )

    def send(self, group):
        begin, end = GROUPS[group]
        for code in range(begin, end):
            for order in range(3):
                remote(
                    self.packed.at[self.place(order, code, self.ways.core)], self.got.at[order, code - 1],
                    self.send_sem.at[order, group], self.recv_sem.at[order, group],
                    self.ways.partner(self.orders[order][step_of(begin)]),
                ).start()

    def receive(self, group):
        begin, end = GROUPS[group]
        base = 1 << (begin.bit_length() - 1)
        for order in range(3):
            self.group(order, group).wait_recv()
            for code in range(begin, end):
                place = self.place(order, code - base, self.ways.core)
                self.packed[place] = self.packed[place] + self.got[order, code - 1]

    def share(self):
        for order in range(3):
            self.group(order, 5).wait_recv()
            place = self.place(order, 0, self.ways.core)
            self.final[self.ways.core, order, self.ways.half] = self.packed[place] + self.got[order, 0]
            self.last_copy(order).start()

    def last_copy(self, order):
        part = self.final.at[self.ways.core, order, self.ways.half]
        return remote(part, part, self.last_send.at[order], self.last_recv.at[order], self.ways.side)

    def end_copy(self, order):
        part = self.final.at[self.ways.core, order]
        return remote(part, part, self.end_send.at[order], self.end_recv.at[order], self.ways.mate)

    def hand_over(self):
        for order in range(3):
            self.last_copy(order).wait_recv()
            self.end_copy(order).start()

    def end(self):
        for order in range(3):
            self.end_copy(order).wait()
            self.last_copy(order).wait_send()
            for at in range(4):
                self.core_group(order, at).wait_send()
            for group in range(len(GROUPS)):
                self.group(order, group).wait_send()


class LateSum:
    def __init__(self, ways, orders, hp, packed, held, got, final, sems):
        self.ways, self.orders, self.hp = ways, orders, hp
        self.packed, self.held, self.got, self.final = packed, held, got, final
        self.first_send, self.first_recv, self.send_sem, self.recv_sem, self.last_send, self.last_recv = sems
        self.rows = held.shape[3]

    def part(self, order, code):
        page, half = self.ways.piece(self.orders[order], code)
        return self.hp, order, page, pl.ds(pl.multiple_of(half * self.rows, 16), self.rows)

    def start(self):
        hp = self.hp
        for code in (12, 13, 14, 15, 8, 9, 10, 11):
            for order in range(3):
                remote(
                    self.packed.at[self.part(order, code)], self.got.at[hp, order, code - 1],
                    self.first_send.at[hp, order], self.first_recv.at[hp, order],
                    self.ways.partner(self.orders[order][0]),
                ).start()

    def first(self, order):
        part = self.got.at[self.hp, order, 7:15]
        return remote(
            part, part, self.first_send.at[self.hp, order], self.first_recv.at[self.hp, order],
            self.ways.partner(self.orders[order][0]),
        )

    def copy(self, order, step):
        begin, end = 8 >> step, 16 >> step
        return remote(
            self.held.at[self.hp, order, begin:end], self.got.at[self.hp, order, begin - 1 : end - 1],
            self.send_sem.at[self.hp, order, step - 1], self.recv_sem.at[self.hp, order, step - 1],
            self.ways.partner(self.orders[order][step]),
        )

    def shares(self):
        ways, hp = self.ways, self.hp
        part = self.final.at[ways.core, hp, ways.half]
        for which, to in enumerate((ways.side, ways.mate, ways.partner("yc"))):
            yield remote(part, part, self.last_send.at[hp, which], self.last_recv.at[hp, which], to)

    def advance(self, step):
        ways, hp = self.ways, self.hp
        for order in range(3):
            if step == 0:
                self.first(order).wait_recv()
                for code in (4, 5, 6, 7, 0, 1, 2, 3):
                    self.held[hp, order, code] = self.packed[self.part(order, code)] + self.got[hp, order, code + 7]
                    if code == 7:
                        self.copy(order, 1).start()
            elif step < 3:
                self.copy(order, step).wait_recv()
                count = 8 >> step
                self.held[hp, order, :count] = (
                    self.held[hp, order, :count] + self.got[hp, order, count - 1 : 2 * count - 1]
                )
                self.copy(order, step + 1).start()
            else:
                self.copy(order, 3).wait_recv()
                self.final[ways.core, hp, ways.half, order] = self.held[hp, order, 0] + self.got[hp, order, 0]
        if step == 3:
            for copy in self.shares():
                copy.start()

    def finish(self):
        for copy in self.shares():
            copy.wait()
        for order in range(3):
            self.first(order).wait_send()
            for step in (1, 2, 3):
                self.copy(order, step).wait_send()


class SmallSum:
    rounds = "xamyc"

    def __init__(self, ways, value, got, sems):
        self.ways, self.value, self.got = ways, value, got
        self.send_sem, self.recv_sem = sems

    def copy(self, step):
        return remote(
            self.value.at[step], self.got.at[step], self.send_sem.at[step], self.recv_sem.at[step],
            self.ways.partner(self.rounds[step]),
        )

    def start(self):
        self.copy(0).start()

    def advance(self, step):
        self.copy(step).wait_recv()
        self.value[step + 1] = self.value[step] + self.got[step]
        if step < 4:
            self.copy(step + 1).start()

    def finish(self):
        for step in range(5):
            self.copy(step).wait_send()


def norm_of(resid):
    center = resid - jnp.mean(resid, axis=-1, keepdims=True)
    spread = jnp.mean(center * center, axis=-1, keepdims=True)
    inverse = lax.rsqrt(spread + norm_eps)
    return center * inverse, inverse


def norm_back(grad, normed, inverse):
    mean = jnp.mean(grad, axis=-1, keepdims=True)
    along = jnp.mean(grad * normed, axis=-1, keepdims=True)
    return inverse * (grad - mean - normed * along)


def column_sum(values):
    return jnp.sum(values, axis=0, keepdims=True)


def layer_kernel(
    summed, tokens_in, boxes, cotangent_in, out_w, up_w, down_w, qkv_w, lengths, freq, out_b, gain1, shift1, up_b,
    down_b, gain2, shift2, qkv_b, box_w,
    x_t_hbm, q_hbm, k_hbm, v_hbm, sc_hbm, p_hbm, layer_out, dx_out, *refs
):
    if summed:
        (
            early_out, down_out, late_out, small_out, tiny_out,
            x, box, ctx_own, dresid1, dctx_own, dctx, dx_mate, dx_side,
            x_mate_send, x_mate_recv, x_side_send, x_side_recv, x_pass_send, x_pass_recv, ctx_send, ctx_recv,
            own_sem, mate_send, mate_recv, core_send, core_recv, side_send, side_recv,
            packed_down, packed, down_mates, early_mates, down_got, early_got, late_got,
            small_value, small_got, tiny_value, tiny_got, *sems,
        ) = refs
        down_sems, early_sems, late_sems, small_sems, tiny_sems = sems[:8], sems[8:16], sems[16:22], sems[22:24], sems[24:]
        g_rows = small_value.at[0]
    else:
        (
            packed_down, packed, late_out, g_rows, tiny_out,
            x, box, ctx_own, dresid1, dctx_own, dctx, dx_mate, dx_side,
            x_mate_send, x_mate_recv, x_side_send, x_side_recv, x_pass_send, x_pass_recv, ctx_send, ctx_recv,
            own_sem, mate_send, mate_recv, core_send, core_recv, side_send, side_recv,
        ) = refs
    ways = Ways()
    core, mate, side = ways.core, ways.mate, ways.side
    greet(ways.everyone() if summed else [mate, side])
    pages, block, width = dctx_own.shape
    half = width // 2
    pairs = half // LANES
    chip, keys = 2 * block, 4 * block
    shard = width // 8
    head = LANES // 2
    scale = 0.125
    chunks = 6
    chunk = up_w.shape[1] // chunks
    up_pieces = chunk // LANES
    if summed:
        down = EarlySum(ways, DOWN_ORDERS, packed_down, down_mates, down_got, down_out, down_sems)
        early = EarlySum(ways, EARLY_ORDERS, packed, early_mates, early_got, early_out, early_sems)
        small = SmallSum(ways, small_value, small_got, small_sems)
        tiny = SmallSum(ways, tiny_value, tiny_got, tiny_sems)
        first_chunk = chunks // 2 * (1 - core)
    else:
        first_chunk = 0

    def row(ref):
        return ref[...].reshape(1, -1)

    def of_half(part, which):
        return pl.ds(pl.multiple_of(part * 2 * half + which * half, LANES), half)

    def own_copy(pg):
        return pltpu.make_async_copy(
            dctx_own.at[pg, :, of_half(0, core)], dctx.at[pg, core], own_sem.at[pg]
        )

    def mate_copy(pg):
        return remote(
            dctx_own.at[pg, :, of_half(0, 1 - core)], dctx.at[pg, core], mate_send.at[pg],
            mate_recv.at[pg], mate,
        )

    def send_dctx():
        for pg in range(pages):
            mate_copy(pg).start()
            own_copy(pg).start()

    moves = {}
    if summed:
        for name, chain in (("D", down), ("E", early)):
            for at in range(6):
                moves["%ss%d" % (name, at)] = functools.partial(chain.send, at)
                moves["%sr%d" % (name, at)] = functools.partial(chain.receive, at)
            for at in range(4):
                moves["%sc%d" % (name, at)] = functools.partial(chain.add_core, at)
            moves[name + "sh"], moves[name + "ho"], moves[name + "fin"] = chain.share, chain.hand_over, chain.end
        for name, chain in (("S", small), ("T", tiny)):
            moves[name + "s"] = chain.start
            for at in range(5):
                moves["%sa%d" % (name, at)] = functools.partial(chain.advance, at)

    def at_place(place):
        if summed:
            for name in PLAN.get(place, ()):
                moves[name]()

    def at_step(step, places):
        for at, place in enumerate(places):
            if place in PLAN and summed:
                pl.when(step == at)(functools.partial(at_place, place))

    def feed_loads(cotangent, w_out, w_up, w_down, w_sem, up_sem, down_sem):
        rows_in = pltpu.make_async_copy(cotangent_in, cotangent, w_sem.at[0])
        out_load = pltpu.make_async_copy(out_w, w_out, w_sem.at[1])

        def up_load(j):
            return pltpu.make_async_copy(
                up_w.at[:, pl.ds(pl.multiple_of(j * chunk, LANES), chunk)], w_up.at[j], up_sem.at[j]
            )

        def down_load(j):
            return pltpu.make_async_copy(
                down_w.at[pl.ds(pl.multiple_of(j * chunk, LANES), chunk)], w_down.at[j], down_sem.at[j]
            )

        return rows_in, out_load, up_load, down_load

    def attend_phase(
        start_loads, x_t, w_q, w_kv, q, k, v, sc, probs, ctx, box2, raw, own_load, w_sem, out_sem, p_sem, ctx_sem
    ):
        loads = [
            pltpu.make_async_copy(qkv_w.at[:, of_half(0, core)], w_q, w_sem.at[0]),
            pltpu.make_async_copy(qkv_w.at[:, of_half(1, core)], w_kv.at[:, :half], w_sem.at[1]),
            pltpu.make_async_copy(qkv_w.at[:, of_half(2, core)], w_kv.at[:, half:], w_sem.at[2]),
        ]
        own = []
        for pg in range(pages):
            own.append(pltpu.make_async_copy(tokens_in.at[pg], x.at[pg, core], own_load.at[pg, 0]))
            own.append(pltpu.make_async_copy(boxes.at[pg], box.at[pg, core], own_load.at[pg, 1]))
        for copy in own:
            copy.start()
        for copy in loads:
            copy.start()
        to_mate, to_side = [], []
        for pg in range(pages):
            for which, (src, dst) in enumerate(((tokens_in, x), (boxes, box))):
                to_side.append(
                    remote(src.at[pg], dst.at[pg, 2 + core], x_side_send.at[pg, which], x_side_recv.at[pg, which], side)
                )
                to_side[-1].start()
                to_mate.append(
                    remote(src.at[pg], dst.at[pg, core], x_mate_send.at[pg, which], x_mate_recv.at[pg, which], mate)
                )
                to_mate[-1].start()
        start_loads()
        saved = ((x_t, x_t_hbm), (sc, sc_hbm), (q, q_hbm), (k, k_hbm), (v, v_hbm))
        zero = jnp.zeros_like(box_w)
        box2[...] = jnp.concatenate(
            [jnp.concatenate([box_w[...], zero], 1), jnp.concatenate([zero, box_w[...]], 1)], 0
        )

        def bias_of(part):
            both = [
                qkv_b[(2 * part + which) * half : (2 * part + which + 1) * half].reshape(1, half)
                for which in range(2)
            ]
            return jnp.where(core == 0, both[0], both[1])

        for copy in loads:
            copy.wait()

        both_in = ((tokens_in, x), (boxes, box))

        def sines(pg, side_place):
            for at in (2 * side_place, 2 * side_place + 1):
                rows = box[pg, at].astype(f32)
                spread = [
                    jnp.broadcast_to(rows[c : c + 1], (freq.shape[0] // 4, LANES)) for c in range(4)
                ]
                sine, cosine = sin_cos(jnp.concatenate(spread, 0) * freq[...])
                sc[pg, at * LANES : (at + 1) * LANES] = jnp.concatenate([sine, cosine], 0).T

        def project(pg, side_place):
            rows = slice(side_place * chip, (side_place + 1) * chip)
            part = x[pg, 2 * side_place : 2 * side_place + 2].reshape(chip, width)
            x_t[pg, :, rows] = part.T
            bias = jnp.concatenate([bias_of(1), bias_of(2)], 1)
            kv_part = (dot(part, w_kv[...]) + bias).astype(low)
            for hp in range(pairs):
                k[pg, hp, rows] = kv_part[:, hp * LANES : (hp + 1) * LANES]
                v[pg, hp, rows] = kv_part[:, half + hp * LANES : half + (hp + 1) * LANES]
            if side_place == 0:
                q_part = (dot(part, w_q[...]) + bias_of(0)).astype(low)
                for hp in range(pairs):
                    q[pg, hp] = q_part[:, hp * LANES : (hp + 1) * LANES]
            sines(pg, side_place)

        @pl.loop(0, pages)
        def _(pg):
            for which, (src, dst) in enumerate(both_in):
                pltpu.make_async_copy(src.at[pg], dst.at[pg, core], own_load.at[pg, which]).wait()
                remote(
                    src.at[pg], dst.at[pg, core], x_mate_send.at[pg, which], x_mate_recv.at[pg, which], mate
                ).wait_recv()
            project(pg, 0)

        @pl.loop(0, pages)
        def _(pg):
            passed = []
            for which, (src, dst) in enumerate(both_in):
                remote(
                    src.at[pg], dst.at[pg, 2 + core], x_side_send.at[pg, which], x_side_recv.at[pg, which], side
                ).wait_recv()
                copy = remote(
                    dst.at[pg, 2 + core], dst.at[pg, 2 + core], x_pass_send.at[pg, which],
                    x_pass_recv.at[pg, which], mate,
                )
                copy.start()
                passed.append(copy)
            for copy in passed:
                copy.wait_recv()
            project(pg, 1)
            for which, (src, dst) in enumerate(saved):
                pltpu.make_async_copy(src.at[pg], dst.at[pg], out_sem.at[pg, which]).start()
            place = lax.broadcasted_iota(jnp.int32, (keys, chip), 0) + ways.half * chip
            place = jnp.where(place >= keys, place - keys, place)
            valid = place < lengths[pg]

            both = sc[pg]
            cosine2, sine2 = turned(both)
            basis = both.astype(low)
            basis_q = (both[:chip] * scale).astype(low)
            left = lane_halves((chip, LANES))
            cosine_q = jnp.where(left, -cosine2[:chip], cosine2[:chip]) * scale
            sine_q = jnp.where(left, sine2[:chip], -sine2[:chip]) * scale
            for hp in range(pairs):
                q_pair, k_pair = q[pg, hp], k[pg, hp]
                q_proj = dot(q_pair, box2[...])
                k_proj = dot(k_pair, box2[...])
                for e in range(2):
                    at = slice(e * LANES, (e + 1) * LANES)
                    q_pos = rotate_key(q_proj[:, at], cosine_q, sine_q).astype(low)
                    k_pos = rotate_key(k_proj[:, at], cosine2, sine2).astype(low)
                    mine = left if e == 0 else jnp.logical_not(left)
                    q_own = jnp.where(mine, q_pair.astype(f32) * scale, 0.0).astype(low)
                    scores = dot_nt(
                        jnp.concatenate([basis, k_pos], 1), jnp.concatenate([q_pos, basis_q], 1)
                    )
                    scores = scores + dot_nt(k_pair, q_own)
                    raw[2 * hp + e] = jnp.where(valid, scores, -1e30)
            for hp in range(pairs):
                for e in range(2):
                    scores = raw[2 * hp + e]
                    top = jnp.max(scores, axis=0, keepdims=True)
                    grown = jnp.exp(scores - top)
                    total = jnp.sum(grown, axis=0, keepdims=True)
                    probs[pg, hp, e] = (grown * (1.0 / total)).astype(low)
                pltpu.make_async_copy(probs.at[pg, hp], p_hbm.at[pg, hp], p_sem.at[pg, hp]).start()
            for hp in range(pairs):
                v_t = v[pg, hp].T
                outs = [dot(v_t[e * head : (e + 1) * head], probs[pg, hp, e]) for e in range(2)]
                context = jnp.concatenate(outs, 0).T.astype(low)
                lanes = slice(hp * LANES, (hp + 1) * LANES)
                ctx[pg, 0, :, lanes] = context[: chip // 2]
                ctx[pg, 1, :, lanes] = context[chip // 2 :]

            mine = pl.ds(pl.multiple_of(core * half, LANES), half)
            pltpu.make_async_copy(ctx.at[pg, core], ctx_own.at[pg, :, mine], ctx_sem.at[pg]).start()
            remote(
                ctx.at[pg, 1 - core], ctx_own.at[pg, :, mine], ctx_send.at[pg], ctx_recv.at[pg], mate
            ).start()
            for copy in passed:
                copy.wait_send()

        mine = pl.ds(pl.multiple_of(core * half, LANES), half)
        for pg in range(pages):
            for which, (src, dst) in enumerate(saved):
                pltpu.make_async_copy(src.at[pg], dst.at[pg], out_sem.at[pg, which]).wait()
            for hp in range(pairs):
                pltpu.make_async_copy(probs.at[pg, hp], p_hbm.at[pg, hp], p_sem.at[pg, hp]).wait()
            pltpu.make_async_copy(ctx.at[pg, core], ctx_own.at[pg, :, mine], ctx_sem.at[pg]).wait()
            remote(
                ctx.at[pg, 1 - core], ctx_own.at[pg, :, mine], ctx_send.at[pg], ctx_recv.at[pg], mate
            ).wait_send()
        for copy in to_side + to_mate:
            copy.wait_send()

    def feed_phase(
        cotangent, w_out, w_up, w_down, w_sem, up_sem, down_sem, output, act, slope, norm1, inverse1, hidden, hidden_t,
        grow, staged, up_rows, out_sem,
    ):
        rows_in, out_load, up_load, down_load = feed_loads(cotangent, w_out, w_up, w_down, w_sem, up_sem, down_sem)
        g_rows[...] = jnp.zeros_like(g_rows)
        for j in range(chunks):
            up_rows[j : j + 1] = up_b[j * chunk : (j + 1) * chunk].reshape(1, chunk)
        out_load.wait()
        rows_in.wait()
        for pg in range(pages):
            other = pl.ds(pl.multiple_of((1 - core) * (width // 2), LANES), width // 2)
            part = ctx_own.at[pg, :, other]
            remote(part, part, ctx_send.at[pg], ctx_recv.at[pg], mate).wait_recv()
        ctx = ctx_own[...].reshape(pages * block, width)
        tokens = jnp.concatenate([x[pg, core] for pg in range(pages)], 0)
        resid = tokens.astype(f32) + dot(ctx, w_out[...]) + row(out_b)
        normed, inverse = norm_of(resid)
        norm1[...] = normed
        inverse1[...] = jnp.broadcast_to(inverse, inverse1.shape)
        first = normed * row(gain1) + row(shift1)
        hidden[...] = first.astype(low)
        hidden_t[...] = first.astype(low).T
        grow[...] = first + row(down_b)

        for j in range(chunks):
            up_load(j).wait()
            down_load(j).wait()

        @pl.loop(0, chunks // 3)
        def _(step):
            for j in (3 * step, 3 * step + 1, 3 * step + 2):
                upper = dot(hidden[...], w_up[j]) + up_rows[pl.ds(j, 1)]
                cdf = 0.5 + 0.5 * lax.erf(upper * 0.7071067811865476)
                act[j] = (upper * cdf).astype(low)
                slope[j] = (cdf + upper * (jnp.exp(upper * upper * -0.5) * 0.3989422804014327)).astype(low)

        @pl.loop(0, chunks // 3)
        def _(step):
            grow[...] += sum(dot(act[3 * step + at], w_down[3 * step + at]) for at in range(3))

        normed2, inverse2 = norm_of(grow[...])
        output[...] = (normed2 * row(gain2) + row(shift2)).astype(low)
        output_copy = pltpu.make_async_copy(output, layer_out, out_sem)
        output_copy.start()
        cot = cotangent[...].astype(f32)
        g_rows[0:1] = column_sum(cot * normed2)
        g_rows[1:2] = column_sum(cot)
        dresid2 = norm_back(cot * row(gain2), normed2, inverse2)
        dffn = dresid2.astype(low)
        g_rows[2:3] = column_sum(dffn.astype(f32))
        grow[...] = dresid2
        staged[...] = dffn

        @pl.loop(0, chunks // 2)
        def _(step):
            dffn = staged[...]
            for j in (2 * step, 2 * step + 1):
                grad_down = dot_tn(act[j], dffn).astype(low)
                for piece in range(up_pieces):
                    at = j * up_pieces + piece
                    per = up_pieces * chunks // 8
                    rows = pl.ds(pl.multiple_of((at % per) * LANES, LANES), LANES)
                    for column in range(6):
                        packed_down[column, at // per, rows] = grad_down[
                            piece * LANES : (piece + 1) * LANES, column * LANES : (column + 1) * LANES
                        ]

        if summed:
            down.swap(range(3))
        up_end = up_pieces * shard // 2
        per_half = up_end + shard // 2

        @pl.loop(0, chunks // 2)
        def _(step):
            dffn = staged[...]
            for j in (2 * step, 2 * step + 1):
                act[j] = (dot_nt(dffn, w_down[j]) * slope[j].astype(f32)).astype(low)

        @pl.loop(0, chunks)
        def _(step):
            at_step(step, ["f%d" % at for at in range(chunks)])
            j = lax.rem(step + first_chunk, chunks)
            dupper = act[j]
            g_rows[pl.ds(8 + j, 1), :chunk] = column_sum(dupper.astype(f32))
            grow[...] += dot_nt(dupper, w_up[j])
            grad_up = dot(hidden_t[...], dupper).astype(low)
            for piece in range(up_pieces):
                part = grad_up[:, piece * LANES : (piece + 1) * LANES].reshape(8, shard, LANES)
                at = piece // (up_pieces // 2) * per_half + piece % (up_pieces // 2) * shard
                packed[j, :, at : at + shard] = part
            if summed:

                for order in range(3):

                    @pl.when(step == order)
                    def _(order=order):
                        early.swap([order], 0, up_end)

        dhidden = grow[...]
        normed = norm1[...]
        g_rows[3:4] = column_sum(dhidden * normed)
        g_rows[4:5] = column_sum(dhidden)
        back = norm_back(dhidden * row(gain1), normed, inverse1[:, :1])
        dresid1[...] = back.reshape(dresid1.shape)
        dattn = back.astype(low)
        g_rows[5:6] = column_sum(dattn.astype(f32))
        dctx_own[...] = dot_nt(dattn, w_out[...]).astype(low).reshape(dctx_own.shape)
        send_dctx()
        at_place("fe")
        grad_out = dot_tn(ctx_own[...].reshape(pages * block, width), dattn).astype(low)
        for column in range(6):
            part = grad_out[:, column * LANES : (column + 1) * LANES].reshape(8, shard, LANES)
            for half in range(2):
                at = half * per_half + up_end
                packed[column, :, at : at + shard // 2] = part[:, half * shard // 2 : (half + 1) * shard // 2]
        if summed:
            early.swap(range(3), up_end, per_half)
        at_place("fw")
        output_copy.wait()

    def back_phase(
        x_t, q, k, v, sc, probs, dq, dkv, w_c, dx, box_t, g_box, g_bias, late_packed, late_held, in_sem, p_sem, w_sem
    ):
        def loads(pg):
            names = ((q_hbm, q), (k_hbm, k), (v_hbm, v), (sc_hbm, sc))
            copies = [
                pltpu.make_async_copy(src.at[pg], dst.at[pg], in_sem.at[pg, at])
                for at, (src, dst) in enumerate(names)
            ]
            at = pl.ds(pl.multiple_of(pg * keys, LANES), keys)
            copies.append(pltpu.make_async_copy(x_t_hbm.at[pg], x_t.at[:, at], in_sem.at[pg, 4]))
            return copies

        def p_load(hp, pg):
            return pltpu.make_async_copy(p_hbm.at[pg, hp], probs.at[pg, hp], p_sem.at[pg, hp])

        w_loads = [
            pltpu.make_async_copy(qkv_w.at[:, of_half(part, core)], w_c.at[part], w_sem.at[part])
            for part in range(3)
        ]
        for pg in range(pages):
            for copy in loads(pg):
                copy.start()
            for hp in range(pairs):
                p_load(hp, pg).start()
        for copy in w_loads:
            copy.start()
        at_place("bs")

        def late(hp):
            return LateSum(ways, LATE_ORDERS, hp, late_packed, late_held, late_got, late_out, late_sems)

        for e in range(2):
            box_t[e] = jnp.zeros_like(box_t[e])
            box_t[e, :, e * head : (e + 1) * head] = box_w[...].astype(f32).T.astype(low)
        g_box[...] = jnp.zeros_like(g_box)

        def take(pg):
            for copy in loads(pg):
                copy.wait()
            own_copy(pg).wait()
            mate_copy(pg).wait_recv()

        def one_pair(pg, hp):
            lanes = pl.ds(pl.multiple_of(hp * LANES, LANES), LANES)
            p_load(hp, pg).wait()
            both = sc[pg]
            cosine2, sine2 = turned(both)
            flat = both.T
            sine_t, cosine_t = flat[:head, :chip], flat[head:, :chip]
            basis = both.astype(low)
            basis_t = flat.astype(low)
            q_pair, k_pair, v_pair = q[pg, hp], k[pg, hp], v[pg, hp]
            q_t, k_t = q_pair.T, k_pair.T
            dc = dctx[pg, :, :, lanes].reshape(chip, LANES)
            left = lane_halves((chip, LANES))
            zero = jnp.zeros_like(dc)
            dk, dv, dqs = 0.0, 0.0, []
            for e in range(2):
                mine = left if e == 0 else jnp.logical_not(left)
                own_rows = slice(e * head, (e + 1) * head)
                p = probs[pg, hp, e]
                dc_own = jnp.where(mine, dc, zero)
                q_own = jnp.where(mine, q_pair, zero)
                dp = dot_nt(v_pair, dc_own)
                p_wide = p.astype(f32)
                delta = jnp.sum(p_wide * dp, axis=0, keepdims=True)
                ds = (p_wide * (dp - delta)).astype(low)
                dv = dv + dot(p, dc_own)
                dk_feat = dot(ds, jnp.concatenate([q_own, basis[:chip]], 1)) * scale
                dq_feat = dot(jnp.concatenate([k_t[own_rows], basis_t], 0), ds) * scale
                dk_proj = rotate_key(dk_feat[:, LANES:], cosine2, sine2).astype(low)
                a, b = dq_feat[head : 2 * head], dq_feat[2 * head :]
                dq_proj = jnp.concatenate(
                    [a * cosine_t - b * sine_t, a * sine_t + b * cosine_t], 0
                ).astype(low)
                dk = dk + dk_feat[:, :LANES] + dot(dk_proj, box_t[e])
                dqs.append(dq_feat[:head] + dot(box_w[...], dq_proj))
                g_box[...] += dot(k_t[own_rows], dk_proj) + dot_nt(q_t[own_rows], dq_proj)
            at = pl.ds(pl.multiple_of(pg * keys, LANES), keys)
            at_q = pl.ds(pl.multiple_of(pg * chip, LANES), chip)
            dq[hp, at_q] = jnp.concatenate(dqs, 0).T.astype(low)
            dkv[hp, at, :LANES] = dk.astype(low)
            dkv[hp, at, LANES:] = dv.astype(low)

        def pair_grads(hp):
            dkv_all = dkv[hp]
            dq_all = dq[hp]
            g_kv = column_sum(dkv_all.astype(f32))
            g_bias[pl.ds(hp, 1)] = column_sum(dq_all.astype(f32))
            g_bias[pl.ds(hp + pairs, 1)] = g_kv[:, :LANES]
            g_bias[pl.ds(hp + 2 * pairs, 1)] = g_kv[:, LANES:]
            grad = dot(x_t[...], dkv_all).astype(low)
            x_q = jnp.concatenate([x_t[:, pg * keys : pg * keys + chip] for pg in range(pages)], 1)
            grad_q = dot(x_q, dq_all).astype(low)
            late_packed[hp, 0] = grad_q.reshape(8, shard, LANES)
            late_packed[hp, 1] = grad[:, :LANES].reshape(8, shard, LANES)
            late_packed[hp, 2] = grad[:, LANES:].reshape(8, shard, LANES)

        def core_copy(pg, at):
            return remote(
                dx.at[pg, at, 1 - core], dx_mate.at[pg, at], core_send.at[pg, at], core_recv.at[pg, at],
                mate,
            )

        def side_copy(pg):
            return remote(dx.at[pg, 1, core], dx_side.at[pg], side_send.at[pg], side_recv.at[pg], side)

        def input_part(pg):
            for at in (1, 0):
                rows = pl.ds(pl.multiple_of(pg * keys + at * chip, LANES), chip)
                dks = jnp.concatenate([dkv[hp, rows, :LANES] for hp in range(pairs)], 1)
                dvs = jnp.concatenate([dkv[hp, rows, LANES:] for hp in range(pairs)], 1)
                total = dot_nt(dks, w_c[1]) + dot_nt(dvs, w_c[2])
                if at == 0:
                    rows_q = pl.ds(pl.multiple_of(pg * chip, LANES), chip)
                    dqs = jnp.concatenate([dq[hp, rows_q] for hp in range(pairs)], 1)
                    total = total + dot_nt(dqs, w_c[0])
                dx[pg, at] = total.astype(low).reshape(2, block, width)
                core_copy(pg, at).start()

        def pass_input(pg):
            core_copy(pg, 1).wait_recv()
            dx[pg, 1, core] = dx[pg, 1, core] + dx_mate[pg, 1]
            side_copy(pg).start()

        def bias_rows():
            for part in range(3):
                for which in range(2):
                    own = jnp.where(core == which, 1.0, 0.0)
                    for hp in range(pairs):
                        at = part * pairs + hp
                        yield 64 + (2 * part + which) * pairs + hp, g_bias[at : at + 1] * own

        def finish_input(pg):
            core_copy(pg, 0).wait_recv()
            side_copy(pg).wait_recv()
            total = dx[pg, 0, core].astype(f32) + dx_mate[pg, 0].astype(f32) + dx_side[pg].astype(f32)
            dx_out[pg] = (total + dresid1[pg]).astype(low)

        for pg in range(pages):
            moves["X%dp" % pg] = functools.partial(pass_input, pg)
            moves["X%dfin" % pg] = functools.partial(finish_input, pg)
        if summed:
            for hp in range(pairs):
                chain = late(hp)
                moves["L%ds" % hp], moves["L%dfin" % hp] = chain.start, chain.finish
                for at in range(4):
                    moves["L%da%d" % (hp, at)] = functools.partial(chain.advance, at)

        @pl.loop(0, pages - 1)
        def _(pg):
            take(pg)

            @pl.loop(0, pairs)
            def _(hp):
                at_step(pg * pairs + hp, ["b%d" % at for at in range(6)])
                one_pair(pg, hp)

            at_step(pg, ["p0", "p1"])

            @pl.when(pg == 0)
            def _():
                for copy in w_loads:
                    copy.wait()

            input_part(pg)
            at_step(pg, ["q0", "q1"])

        last = pages - 1
        take(last)

        @pl.loop(0, pairs)
        def _(hp):
            at_step(hp, ["b6", "b7", "b8"])
            one_pair(last, hp)
            pair_grads(hp)
            at_step(hp, ["g0", "g1"])

        if summed:
            tiny_value[0, : 8 * 8] = g_box[...]
            tiny_value[0, 64:] = jnp.zeros((24, LANES), f32)
            for at, row in bias_rows():
                tiny_value[0, at : at + 1] = row
        at_place("p2")
        input_part(last)
        at_place("tail")
        if not summed:
            for pg in range(pages):
                pass_input(pg)
            for pg in range(pages):
                finish_input(pg)
        for pg in range(pages):
            for at in range(2):
                core_copy(pg, at).wait_send()
            side_copy(pg).wait_send()
            mate_copy(pg).wait_send()
        if summed:
            small_out[...] = small_value[5]
            tiny_out[...] = tiny_value[5]
            small.finish()
            tiny.finish()
        else:
            late_out[...] = late_packed[...]
            tiny_out[:64] = g_box[...]
            tiny_out[64:] = jnp.zeros((24, LANES), f32)
            for at, row in bias_rows():
                tiny_out[at : at + 1] = row

    vmem, dma = pltpu.VMEM, pltpu.SemaphoreType.DMA
    rows = pages * block
    def forward(*weights):
        rows_in, out_load, up_load, down_load = feed_loads(*weights)

        def start_loads():
            out_load.start()
            rows_in.start()
            for j in range(chunks):
                up_load(j).start()
                down_load(j).start()

        pl.run_scoped(
            functools.partial(attend_phase, start_loads),
            vmem((pages, width, keys), low),
            vmem((width, half), low),
            vmem((width, 2 * half), low),
            vmem((pages, pairs, chip, LANES), low),
            vmem((pages, pairs, keys, LANES), low),
            vmem((pages, pairs, keys, LANES), low),
            vmem((pages, keys, LANES), f32),
            vmem((pages, pairs, 2, keys, chip), low),
            vmem((pages, 2, block, half), low),
            vmem((2 * box_w.shape[0], 2 * box_w.shape[1]), low),
            vmem((2 * pairs, keys, chip), f32),
            dma((pages, 2)), dma((3,)), dma((pages, 5)), dma((pages, pairs)), dma((pages,)),
        )
        pl.run_scoped(
            functools.partial(feed_phase, *weights),
            vmem((rows, width), low),
            vmem((chunks, rows, chunk), low),
            vmem((chunks, rows, chunk), low),
            vmem((rows, width), f32),
            vmem((rows, LANES), f32),
            vmem((rows, width), low),
            vmem((width, rows), low),
            vmem((rows, width), f32),
            vmem((rows, width), low),
            vmem((chunks, chunk), f32),
            dma,
        )

    pl.run_scoped(
        forward,
        vmem((rows, width), low),
        vmem((width, width), low),
        vmem((chunks, width, chunk), low),
        vmem((chunks, chunk, width), low),
        dma((2,)), dma((chunks,)), dma((chunks,)),
    )
    late_shape = (pairs, 3, 8, shard, LANES)
    pl.run_scoped(
        back_phase,
        vmem((width, pages * keys), low),
        vmem((pages, pairs, chip, LANES), low),
        vmem((pages, pairs, keys, LANES), low),
        vmem((pages, pairs, keys, LANES), low),
        vmem((pages, keys, LANES), f32),
        vmem((pages, pairs, 2, keys, chip), low),
        vmem((pairs, pages * chip, LANES), low),
        vmem((pairs, pages * keys, 2 * LANES), low),
        vmem((3, width, half), low),
        vmem((pages, 2, 2, block, width), low),
        vmem((2, LANES, LANES), low),
        vmem(box_w.shape, f32),
        vmem((3 * pairs, LANES), f32),
        vmem(late_shape, low),
        vmem((pairs, 3, 8, shard // 2, LANES), low),
        dma((pages, 5)), dma((pages, pairs)), dma((3,)),
    )


def layer(tokens, boxes, lengths, cotangent, weights, vectors, qkv_w, qkv_b, box_w, summed):
    pages, block, width = tokens.shape
    head_dim, pos = box_w.shape
    count = pos // 8
    freqs = 10000.0 ** (-np.arange(count) / count)
    freq = jnp.asarray(np.tile(np.tile(freqs, 4)[:, None], (1, LANES)), f32)
    boxes_t = boxes.transpose(0, 2, 1)
    chip, keys = 2 * block, 4 * block
    rows = pages * block
    half = width // 2
    pairs = half // LANES
    shard = width // 8
    hidden_width = weights[1].shape[1]
    down_rows = hidden_width // 8
    packed_rows = down_rows + shard
    tiny_rows = 88
    small = (16, width)
    struct = jax.ShapeDtypeStruct
    vmem, dma = pltpu.VMEM, pltpu.SemaphoreType.DMA
    outs = [
        struct((pages, width, keys), low),
        struct((pages, pairs, chip, LANES), low),
        struct((pages, pairs, keys, LANES), low),
        struct((pages, pairs, keys, LANES), low),
        struct((pages, keys, LANES), f32),
        struct((pages, pairs, 2, keys, chip), low),
        struct((rows, width), low),
        struct((pages, block, width), low),
    ]
    scratch = [
        vmem((pages, 4, block, width), low),
        vmem((pages, 4, 4, LANES), jnp.int32),
        vmem((pages, block, width), low),
        vmem((pages, block, width), f32),
        vmem((pages, block, width), low),
        vmem((pages, 2, block, half), low),
        vmem((pages, 2, block, width), low),
        vmem((pages, block, width), low),
        *[dma((pages, 2))] * 6, dma((pages,)), dma((pages,)),
        dma((pages,)), dma((pages,)), dma((pages,)), dma((pages, 2)), dma((pages, 2)), dma((pages,)), dma((pages,)),
    ]
    if summed:
        outs += [
            struct((2, 3, 2, packed_rows // 2, LANES), low),
            struct((2, 3, 2, down_rows // 2, LANES), low),
            struct((2, pairs, 2, 3, shard // 2, LANES), low),
            struct(small, f32),
            struct((tiny_rows, LANES), f32),
        ]
        scratch += [
            vmem((6, 8, down_rows, LANES), low),
            vmem((6, 8, packed_rows, LANES), low),
            vmem((3, 16, down_rows // 2, LANES), low),
            vmem((3, 16, packed_rows // 2, LANES), low),
            vmem((3, 15, down_rows // 2, LANES), low),
            vmem((3, 15, packed_rows // 2, LANES), low),
            vmem((pairs, 3, 15, shard // 2, LANES), low),
            vmem((6,) + small, f32),
            vmem((5,) + small, f32),
            vmem((6, tiny_rows, LANES), f32),
            vmem((5, tiny_rows, LANES), f32),
        ]
        groups = len(GROUPS)
        scratch += ([dma((3, 4))] * 2 + [dma((3, groups))] * 2 + [dma((3,))] * 4) * 2
        scratch += [dma((pairs, 3))] * 2 + [dma((pairs, 3, 3))] * 2 + [dma((pairs, 3))] * 2
        scratch += [dma((5,))] * 4
    else:
        outs += [
            struct((6, 8, down_rows, LANES), low),
            struct((6, 8, packed_rows, LANES), low),
            struct((pairs, 3, 8, shard, LANES), low),
            struct(small, f32),
            struct((tiny_rows, LANES), f32),
        ]
    return pl.pallas_call(
        functools.partial(layer_kernel, summed),
        out_shape=tuple(outs),
        in_specs=[any_spec()] * 7 + [pl.BlockSpec(memory_space=pltpu.SMEM)] + [vmem_spec()] * 10,
        out_specs=(any_spec(),) * 7 + (vmem_spec(),) * 6,
        scratch_shapes=scratch,
        compiler_params=pltpu.CompilerParams(
            collective_id=2, has_side_effects=True, vmem_limit_bytes=63 * 2**20
        ),
        name="layer",
    )(
        tokens, boxes_t, cotangent.reshape(rows, width), *weights, qkv_w, lengths, freq, *vectors, qkv_b, box_w
    )[6:]


def finish_kernel(
    early_in, rest_in, late_in, small_in, tiny_in, dx_in, layer_in,
    up_out, down_out, out_out, qkv_out, qkv_b, box, out_b, gain1, shift1, up_b, down_b, gain2, shift2, input_grad,
    layer_out, early, rest, late, small, tiny, up, down, out, qkv, sems, out_sems,
):
    page = lax.axis_index("page")
    shard = out.shape[0]
    pieces = up.shape[1] // (6 * LANES)
    pairs = (
        (early_in, early), (rest_in, rest), (late_in, late), (small_in, small), (tiny_in, tiny), (dx_in, input_grad),
        (layer_in, layer_out),
    )
    copies = [pltpu.make_async_copy(src, dst, sems.at[at]) for at, (src, dst) in enumerate(pairs)]
    for copy in copies:
        copy.start()
    results = ((up, up_out), (down, down_out), (out, out_out), (qkv, qkv_out))
    done = [pltpu.make_async_copy(src, dst, out_sems.at[at]) for at, (src, dst) in enumerate(results)]
    columns = [(which, order) for which in range(2) for order in range(3)]
    per = pieces // 2
    copies[0].wait()
    for column, (which, order) in enumerate(columns):
        rows = early[which, order].astype(f32)
        at = column * LANES
        for half in range(2):
            for piece in range(per):
                up_at = (column * pieces + half * per + piece) * LANES
                up[:, up_at : up_at + LANES] = rows[half, piece * shard : (piece + 1) * shard]
            out[half * shard // 2 : (half + 1) * shard // 2, at : at + LANES] = rows[half, per * shard :]
    done[0].start()
    done[2].start()
    copies[1].wait()
    for column, (which, order) in enumerate(columns):
        at = column * LANES
        down[:, at : at + LANES] = rest[which, order].astype(f32).reshape(-1, LANES)
    done[1].start()
    copies[2].wait()
    for column, (which, order) in enumerate(columns):
        for part in range(3):
            at = (part * 6 + column) * LANES
            qkv[:, at : at + LANES] = late[which, order, :, part].astype(f32).reshape(shard, LANES)
    done[3].start()
    copies[3].wait()
    copies[4].wait()
    rows = pltpu.roll(small[:8], lax.rem(8 * shard - page * shard, 8 * shard), 1)
    for at, ref in enumerate((gain2, shift2, down_b, gain1, shift1, out_b)):
        ref[...] = rows[at, :shard]
    flat = jnp.concatenate([small[8 + at : 9 + at, : pieces * LANES] for at in range(6)], 1)
    every = flat.shape[1]
    flat = pltpu.roll(flat, lax.rem(every - page * up_b.shape[0], every), 1)
    up_b[...] = flat[0, : up_b.shape[0]]
    box[...] = tiny[pl.ds(pl.multiple_of(page * 8, 8), 8)]
    count = qkv_b.shape[0]
    first = page * count
    parts = [tiny[pl.ds(64 + first // LANES + piece, 1)] for piece in range(4)]
    rest = lax.rem(first, LANES)
    row = pltpu.roll(jnp.concatenate(parts, 1), lax.rem(4 * LANES - rest, 4 * LANES), 1)
    qkv_b[...] = row[0, :count]
    for copy in copies[5:] + done:
        copy.wait()


def finish(early, rest, late, small, tiny, dx, layer):
    struct = jax.ShapeDtypeStruct
    shapes = (
        (96, 3072), (384, 768), (96, 768), (96, 2304), (288,), (8, LANES), (96,), (96,), (96,), (384,), (96,), (96,), (96,),
    )
    operands = (early, rest, late, small, tiny, dx, layer)
    return pl.pallas_call(
        finish_kernel,
        out_shape=tuple(struct(shape, f32) for shape in shapes) + (struct(dx.shape, low), struct(layer.shape, low)),
        in_specs=[any_spec()] * 7,
        out_specs=(any_spec(),) * 4 + (vmem_spec(),) * 11,
        scratch_shapes=[pltpu.VMEM(operand.shape, operand.dtype) for operand in operands[:5]]
        + [pltpu.VMEM(shape, f32) for shape in shapes[:4]]
        + [pltpu.SemaphoreType.DMA((7,)), pltpu.SemaphoreType.DMA((4,))],
        compiler_params=pltpu.CompilerParams(vmem_limit_bytes=63 * 2**20),
        name="finish",
    )(*operands)


def reduce_by_collectives(packed, packed_down, packed_qkv, vectors):
    core = lax.axis_index("blk") % 2
    packed = packed.reshape(6, 8, 2, 240, LANES)
    up = packed[:, :, :, :192].reshape(6, 8, 4, 96, LANES).transpose(1, 3, 0, 2, 4).reshape(768, 3072)
    down = packed_down.transpose(1, 2, 0, 3).reshape(3072, 768)
    out = packed[:, :, :, 192:].transpose(1, 2, 3, 0, 4).reshape(768, 768)
    own = packed_qkv.transpose(2, 3, 1, 0, 4).reshape(768, 3, 384)
    qkv = jnp.zeros((768, 3, 2, 384), low)
    qkv = lax.dynamic_update_slice(qkv, own[:, :, None], (0, 0, core, 0)).reshape(768, 2304)
    grads = jax.tree.map(lambda g: g.astype(f32), (qkv, out, up, down, *vectors))
    page_sums = tuple(
        lax.psum_scatter(grad, "page", scatter_dimension=0, tiled=True) for grad in grads
    )
    return jax.tree.map(
        lambda part: part.astype(f32), lax.psum(jax.tree.map(lambda g: g.astype(low), page_sums), "blk")
    )


def local(
    tokens, lengths, boxes, qkv_weight, qkv_bias, box_weight, out_weight, out_bias, norm1_gain,
    norm1_bias, up_weight, up_bias, down_weight, down_bias, norm2_gain, norm2_bias, cotangent,
):
    pages, block, width = tokens.shape
    rows = pages * block
    summed = lax.axis_size("page") == 8
    output, input_grad, *parts = layer(
        tokens, boxes, lengths, cotangent, (out_weight, up_weight, down_weight),
        (out_bias, norm1_gain, norm1_bias, up_bias, down_bias, norm2_gain, norm2_bias),
        qkv_weight, qkv_bias, box_weight, summed,
    )
    if summed:
        early, rest, late, small, tiny = parts
        (
            up_w, down_w, out_w, qkv_w, qkv_b, box, out_b, gain1, shift1, up_b, down_b, gain2, shift2, input_grad,
            output,
        ) = finish(early, rest, late, small, tiny, input_grad, output)
        box = box.reshape(-1)
    else:
        down, packed, packed_qkv, small, tiny = parts
        vectors = (
            tiny[64:82].reshape(-1), tiny[:64].reshape(-1), small[5], small[3], small[4],
            small[8:14, :512].reshape(-1), small[2], small[0], small[1],
        )
        (
            qkv_w, out_w, up_w, down_w, qkv_b, box, out_b, gain1, shift1, up_b, down_b, gain2, shift2,
        ) = reduce_by_collectives(packed, down, packed_qkv, vectors)
    return (
        output.reshape(pages, block, width), input_grad, qkv_w, qkv_b, box, out_w, out_b, gain1, shift1, up_w, up_b, down_w, down_b, gain2, shift2,
    )


def solution(mesh):
    return jax.shard_map(
        local,
        mesh=mesh,
        in_specs=(
            P("page", "blk", None),
            P("page"),
            P("page", "blk", None),
            P(),
            P(),
            P(),
            P(),
            P(),
            P(),
            P(),
            P(),
            P(),
            P(),
            P(),
            P(),
            P(),
            P("page", "blk", None),
        ),
        out_specs=(
            P("page", "blk", None),
            P("page", "blk", None),
            P("page", None),
            P("page"),
            P("page"),
            P("page", None),
            P("page"),
            P("page"),
            P("page"),
            P("page", None),
            P("page"),
            P("page", None),
            P("page"),
            P("page"),
            P("page"),
        ),
        check_vma=False,
    )
```
